128 devices in a mesh: pipe: 2 (over y_lo), shard: 32 (over z, x, core), tensor: 2 (over y_hi).
Axes of the slice: x: 4, y: 4 (y_hi: 2, y_lo: 2; y = y_hi * 2 + y_lo), z: 4, core: 2. Of those that a mesh axis runs over, the one named last changes fastest.
Arguments:
- clip_frames: bfloat16 [4, 6144, 768], P(None, 'shard'), may hold values from -6 to 6
- out_cotangent: bfloat16 [4, 6144, 768], P(None, 'shard'), may hold values from -6 to 6
- clip_lengths: int32 [4, 32], P(None, 'shard'), may hold values from 48 to 192, as said below
- query_weight: bfloat16 [2, 768, 768], P('pipe', 'shard', 'tensor'), may hold values from -0.21875 to 0.21875
- key_weight: bfloat16 [2, 768, 768], P('pipe', 'shard', 'tensor'), may hold values from -0.21875 to 0.21875
- value_weight: bfloat16 [2, 768, 768], P('pipe', 'shard', 'tensor'), may hold values from -0.21875 to 0.21875
- output_weight: bfloat16 [2, 768, 768], P('pipe', 'shard', 'tensor'), may hold values from -0.875 to 0.875
- up_weight: bfloat16 [2, 768, 3072], P('pipe', 'shard', 'tensor'), may hold values from -0.21875 to 0.21875
- down_weight: bfloat16 [2, 768, 3072], P('pipe', 'shard', 'tensor'), may hold values from -0.15625 to 0.15625
- query_bias: bfloat16 [2, 64, 12], P('pipe', 'shard', 'tensor'), may hold values from -3 to 3
- value_bias: bfloat16 [2, 64, 12], P('pipe', 'shard', 'tensor'), may hold values from -3 to 3
- output_bias: bfloat16 [2, 768], P('pipe', 'shard'), may hold values from -3 to 3
- up_bias: bfloat16 [2, 64, 48], P('pipe', 'shard', 'tensor'), may hold values from -3 to 3
- down_bias: bfloat16 [2, 768], P('pipe', 'shard'), may hold values from -3 to 3
- first_gain: bfloat16 [2, 768], P('pipe', 'shard'), may hold values from 0.5 to 1.5
- first_shift: bfloat16 [2, 768], P('pipe', 'shard'), may hold values from -2 to 2
- second_gain: bfloat16 [2, 768], P('pipe', 'shard'), may hold values from 0.5 to 1.5
- second_shift: bfloat16 [2, 768], P('pipe', 'shard'), may hold values from -2 to 2
Outputs:
- section_output: bfloat16 [2, 4, 6144, 768], P('pipe', None, 'shard')
- input_grad: bfloat16 [2, 4, 6144, 768], P('pipe', None, 'shard')
- query_weight_grad: float32 [2, 768, 768], P('pipe', 'shard', 'tensor')
- key_weight_grad: float32 [2, 768, 768], P('pipe', 'shard', 'tensor')
- value_weight_grad: float32 [2, 768, 768], P('pipe', 'shard', 'tensor')
- output_weight_grad: float32 [2, 768, 768], P('pipe', 'shard', 'tensor')
- up_weight_grad: float32 [2, 768, 3072], P('pipe', 'shard', 'tensor')
- down_weight_grad: float32 [2, 768, 3072], P('pipe', 'shard', 'tensor')
- query_bias_grad: float32 [2, 64, 12], P('pipe', 'shard', 'tensor')
- value_bias_grad: float32 [2, 64, 12], P('pipe', 'shard', 'tensor')
- output_bias_grad: float32 [2, 768], P('pipe', 'shard')
- up_bias_grad: float32 [2, 64, 48], P('pipe', 'shard', 'tensor')
- down_bias_grad: float32 [2, 768], P('pipe', 'shard')
- first_gain_grad: float32 [2, 768], P('pipe', 'shard')
- first_shift_grad: float32 [2, 768], P('pipe', 'shard')
- second_gain_grad: float32 [2, 768], P('pipe', 'shard')
- second_shift_grad: float32 [2, 768], P('pipe', 'shard')
The draws below stay inside these ranges and needn't reach their ends.
Inputs may be any that keep to these rules, and one draw needn't show every extreme that they name: `clip_lengths`: frames of a clip at or past its length are padding and are not attended to as keys; some clip of the batch has all 192 frames.
All inputs are finite; a program needn't handle non-finite values.
Results may differ from the reference program's by a relative error of at most 0.033.
Values may be sent and summed in bfloat16 or wider, within the bound.
No kernel may reach another device: no remote copies, remote signals or barrier semaphores. Data moves between devices by JAX's collectives and lax.ppermute only.
A program may use at most 192 MiB of HBM per device.

```python
import jax
import jax.numpy as jnp
from jax import lax

D = 768
HEADS = 12
HEAD = 64
FF = 3072
LEN = 192
MB = 4
GROUP = 64
CLIPS = 32
TOKENS = 6144


def draw_clip_lengths(key, part):
    key = jax.random.fold_in(key, 11)
    draw_key, spot_key = jax.random.split(key)
    drawn_lengths = jax.random.randint(draw_key, (MB * CLIPS,), LEN // 4, LEN + 1)
    full_spot = jax.random.randint(spot_key, (), 0, MB * CLIPS)
    flat_lengths = jnp.where(jnp.arange(MB * CLIPS) == full_spot, LEN, drawn_lengths)
    return flat_lengths.reshape(MB, CLIPS).astype(jnp.int32)


def block_levels(stream_key, dims, cuts, smallest, top_value):
    factor_of, own = 1.0, jax.random.fold_in(stream_key, 6)
    for position, parts in cuts:
        steps = jnp.exp(jax.random.uniform(jax.random.fold_in(own, position), (parts,), jnp.float32, smallest / len(cuts), top_value / len(cuts)))
        factor_of = factor_of * jnp.repeat(steps, dims[position] // parts).reshape([-1 if axis == position else 1 for axis in range(len(dims))])
    return factor_of


def bell_draw(key, shape, width, limit, cuts=(), held_as=jnp.bfloat16):
    array = width * jax.random.normal(key, shape, jnp.float32)
    if cuts:
        array = array * block_levels(key, shape, cuts, -0.22, 0.18)
    return jnp.clip(array, -limit, limit).astype(held_as)


def setup_inputs(seed: int = 0) -> dict:
    splits = jax.random.split(jax.random.key(seed), 19)
    return {
        "clip_frames": bell_draw(splits[0], (MB, TOKENS, D), 1.0, 6.0, ((1, 32),)),
        "out_cotangent": bell_draw(splits[1], (MB, TOKENS, D), 1.0, 6.0, ((1, 32),)),
        "clip_lengths": draw_clip_lengths(jax.random.fold_in(splits[18], 71), 0),
        "query_weight": bell_draw(splits[3], (2, D, D), D ** -0.5, 0.21875, ((0, 2), (1, 32), (2, 2))),
        "key_weight": bell_draw(splits[4], (2, D, D), D ** -0.5, 0.21875, ((0, 2), (1, 32), (2, 2))),
        "value_weight": bell_draw(splits[5], (2, D, D), D ** -0.5, 0.21875, ((0, 2), (1, 32), (2, 2))),
        "output_weight": bell_draw(splits[6], (2, D, D), (D // 16) ** -0.5, 0.875, ((0, 2), (1, 32), (2, 2))),
        "up_weight": bell_draw(splits[7], (2, D, FF), D ** -0.5, 0.21875, ((0, 2), (1, 32), (2, 2))),
        "down_weight": bell_draw(splits[8], (2, D, FF), (FF // 2) ** -0.5, 0.15625, ((0, 2), (1, 32), (2, 2))),
        "query_bias": bell_draw(splits[9], (2, HEAD, HEADS), 0.5, 3.0, ((0, 2), (1, 32), (2, 2))),
        "value_bias": bell_draw(splits[10], (2, HEAD, HEADS), 0.5, 3.0, ((0, 2), (1, 32), (2, 2))),
        "output_bias": bell_draw(splits[11], (2, D), 0.5, 3.0, ((0, 2), (1, 32))),
        "up_bias": bell_draw(splits[12], (2, GROUP, FF // GROUP), 0.5, 3.0, ((0, 2), (1, 32), (2, 2))),
        "down_bias": bell_draw(splits[13], (2, D), 0.5, 3.0, ((0, 2), (1, 32))),
        "first_gain": jnp.clip(1.0 + 0.1 * jax.random.normal(splits[14], (2, D), jnp.float32), 0.5, 1.5).astype(jnp.bfloat16),
        "first_shift": bell_draw(splits[15], (2, D), 0.3, 2.0, ((0, 2), (1, 32))),
        "second_gain": jnp.clip(1.0 + 0.1 * jax.random.normal(splits[16], (2, D), jnp.float32), 0.5, 1.5).astype(jnp.bfloat16),
        "second_shift": bell_draw(splits[17], (2, D), 0.3, 2.0, ((0, 2), (1, 32))),
    }


highest = lax.Precision.HIGHEST

@jax.custom_vjp
def low(v):
    return lax.optimization_barrier(v.astype(jnp.bfloat16)).astype(jnp.float32)

@jax.custom_vjp
def low_back(v):
    return v

def low_keep(v):
    return (low(v), None)

def low_pass(kept, grad):
    return (grad,)

def back_keep(v):
    return (v, None)

def back_low(kept, grad):
    return (low(grad),)
low.defvjp(low_keep, low_pass)
low_back.defvjp(back_keep, back_low)

def product(left_side, right_side):
    return jnp.dot(left_side, right_side, precision=highest, preferred_element_type=jnp.float32)

def normalize(values, norm_gain, norm_shift):
    center = values - lax.optimization_barrier(jnp.mean(values, -1, keepdims=True))
    rescale = lax.rsqrt(lax.optimization_barrier(jnp.mean(center * center, -1, keepdims=True)) + 1e-05)
    return center * rescale * norm_gain + norm_shift

def attend_clip(packed):
    queries, key_rows, value_rows, length = packed
    row_count = queries.shape[0]
    query_heads = queries.reshape(row_count, HEADS, HEAD)
    key_heads = key_rows.reshape(row_count, HEADS, HEAD)
    value_heads = value_rows.reshape(row_count, HEADS, HEAD)
    scores = jnp.einsum('qhd,khd->hqk', query_heads, key_heads, precision=highest)
    scores = low_back(scores * HEAD ** (-0.5))
    live_keys = (jnp.arange(row_count) < length)[None, None, :]
    scores = jnp.where(live_keys, scores, -1e+30)
    weights_soft = low(jax.nn.softmax(scores, axis=-1))
    mixed_rows = jnp.einsum('hqk,khd->qhd', weights_soft, value_heads, precision=highest)
    return mixed_rows.reshape(row_count, HEADS * HEAD)

def layer_apply(row_block, lengths_row, params):
    w_query, w_key, w_value, w_out, w_up, w_down, b_query, b_value, b_out, b_up, b_down, gain_one, shift_one, gain_two, shift_two = params
    normed = low(normalize(row_block, gain_one, shift_one))
    queries = low(low_back(product(normed, w_query) + b_query.T.reshape(-1)))
    key_rows = low(low_back(product(normed, w_key)))
    value_rows = low(low_back(product(normed, w_value) + b_value.T.reshape(-1)))
    clip_count = lengths_row.shape[0]
    mixed_rows = lax.map(jax.checkpoint(attend_clip), (queries.reshape(clip_count, -1, D), key_rows.reshape(clip_count, -1, D), value_rows.reshape(clip_count, -1, D), lengths_row))
    mixed_rows = low(low_back(mixed_rows.reshape(-1, D)))
    middle = row_block + low_back(product(mixed_rows, w_out.T)) + b_out
    normed_two = low(normalize(middle, gain_two, shift_two))
    pre_active = low_back(product(normed_two, w_up) + b_up.T.reshape(-1))
    active_rows = low(jax.nn.gelu(pre_active, approximate=False))
    return middle + low_back(product(active_rows, w_down.T)) + b_down

def reference(clip_frames, out_cotangent, clip_lengths, query_weight, key_weight, value_weight, output_weight, up_weight, down_weight, query_bias, value_bias, output_bias, up_bias, down_bias, first_gain, first_shift, second_gain, second_shift):
    params = tuple((array_item.astype(jnp.float32) for array_item in (query_weight, key_weight, value_weight, output_weight, up_weight, down_weight, query_bias, value_bias, output_bias, up_bias, down_bias, first_gain, first_shift, second_gain, second_shift)))
    first_outs = []
    final_outs = []
    first_grads = []
    second_grads = []
    totals = None
    for micro_index in range(MB):
        lengths_row = clip_lengths[micro_index]

        def network(params_all, first_rows, probe_rows):
            layer_zero = tuple((array_item[0] for array_item in params_all))
            layer_one = tuple((array_item[1] for array_item in params_all))
            first_out = layer_apply(first_rows, lengths_row, layer_zero)
            passed = low(low_back(first_out)) + probe_rows
            return (layer_apply(passed, lengths_row, layer_one), first_out)
        frames = clip_frames[micro_index].astype(jnp.float32)
        (final_rows, first_out), pullback = jax.vjp(network, params, frames, jnp.zeros_like(frames))
        param_grads, frame_grad, probe_grad = pullback((out_cotangent[micro_index].astype(jnp.float32), jnp.zeros_like(first_out)))
        first_outs.append(first_out)
        final_outs.append(final_rows)
        first_grads.append(frame_grad)
        second_grads.append(probe_grad)
        if totals is None:
            totals = param_grads
        else:
            totals = tuple((left_side + right_side for left_side, right_side in zip(totals, param_grads)))
    section_output = jnp.stack([jnp.stack(first_outs), jnp.stack(final_outs)]).astype(jnp.bfloat16)
    input_grad = jnp.stack([jnp.stack(first_grads), jnp.stack(second_grads)]).astype(jnp.bfloat16)
    return (section_output, input_grad, totals[0], totals[1], totals[2], totals[3], totals[4], totals[5], totals[6], totals[7], totals[8], totals[9], totals[10], totals[11], totals[12], totals[13], totals[14])
```

```python
import jax
import jax.numpy as jnp
import numpy as np
from jax import lax
from jax.sharding import Mesh
from jax.sharding import PartitionSpec as P

HEAD = 64
bf16 = jnp.bfloat16
f32 = jnp.float32

half_root = 0.7071067811865476
gauss_factor = 0.3989422804014327


EXCHANGES = {"xu": ("x", 1), "xv": ("x", 3), "zu": ("z", 1), "zv": ("z", 3), "c": ("core", 1)}
SIZES = {"x": 4, "z": 4, "core": 2}
WEIGHT_BITS = ("c", "zv", "zu", "xv", "xu")
SHARD_MASK = {"c": 1, "xu": 2, "xv": 6, "zu": 8, "zv": 24}
ORDERS = (
    ("xu", "xv", "zu", "zv"),
    ("xv", "xu", "zv", "zu"),
    ("zu", "zv", "xu", "xv"),
    ("zv", "zu", "xv", "xu"),
)
MASKS = np.zeros(32, np.int32)
for _index in range(32):
    for _place, _bit in enumerate(WEIGHT_BITS):
        if (_index >> (4 - _place)) & 1:
            MASKS[_index] ^= SHARD_MASK[_bit]


def exchange(value, bit):
    axis, flip = EXCHANGES[bit]
    return lax.ppermute(value, axis, [(i, i ^ flip) for i in range(SIZES[axis])])


def exchange_pipe(value):
    return lax.ppermute(value, "pipe", [(0, 1), (1, 0)])


def exchange_both(value):
    return lax.ppermute(value, ("pipe", "tensor"), [(i, i ^ 3) for i in range(4)])


def exchange_tensor(value):
    return lax.ppermute(value, "tensor", [(0, 1), (1, 0)])


def dot(left_side, right_side):
    return jnp.dot(left_side, right_side, preferred_element_type=f32)


def contract_rows(left_side, right_side):
    return lax.dot_general(left_side, right_side, (((0,), (0,)), ((), ())), preferred_element_type=f32)


def contract_cols(left_side, right_side):
    return lax.dot_general(left_side, right_side, (((1,), (1,)), ((), ())), preferred_element_type=f32)


def norm_forward(values, norm_gain, norm_shift):
    center = values - jnp.mean(values, -1, keepdims=True)
    rescale = lax.rsqrt(jnp.mean(center * center, -1, keepdims=True) + 1e-05)
    normed = center * rescale
    return (normed * norm_gain + norm_shift, normed, rescale)


def norm_backward(grad_rows, normed, rescale, norm_gain):
    scaled = grad_rows * norm_gain
    inner = (
        scaled
        - jnp.mean(scaled, -1, keepdims=True)
        - normed * jnp.mean(scaled * normed, -1, keepdims=True)
    )
    return (rescale * inner, jnp.sum(grad_rows * normed, 0), jnp.sum(grad_rows, 0))


def gelu_slope(pre_active):
    return (
        0.5 * (1.0 + lax.erf(pre_active * half_root))
        + pre_active * jnp.exp(-0.5 * pre_active * pre_active) * gauss_factor
    )


def pack_parts(w_query, w_key, w_value, w_out, w_up, w_down, small):
    return (
        jnp.concatenate([w_query, w_key, w_value], 1),
        jnp.concatenate([w_out, small, w_up[:, :768]], 1),
        jnp.concatenate([w_up[:, 768:], w_down[:, :384]], 1),
        w_down[:, 384:],
    )


def unpack_parts(parts):
    first, second, third, fourth = parts
    return (
        first[:, :384],
        first[:, 384:768],
        first[:, 768:],
        second[:, :384],
        jnp.concatenate([second[:, 512:], third[:, :768]], 1),
        jnp.concatenate([third[:, 768:], fourth], 1),
        second[:, 384:512],
    )


PART_COLS = (1152, 1280, 1152, 1152)
PART_ENDS = (0, 1152, 2432, 3584, 4736)


def split_parts(packed):
    return [packed[..., PART_ENDS[i] : PART_ENDS[i + 1]] for i in range(4)]


def gather_layers(own):
    pipe = lax.axis_index("pipe")
    other = exchange_pipe(own)
    mine = jnp.stack([jnp.where(pipe == 0, own, other), jnp.where(pipe == 0, other, own)])
    theirs = exchange_both(mine)
    parts = [
        jnp.concatenate([a, b], -1)[:, None] for a, b in zip(split_parts(mine), split_parts(theirs))
    ]
    for step in range(2):
        got = [exchange(part, ORDERS[i][step]) for i, part in enumerate(parts)]
        parts = [jnp.concatenate([a, b], 1) for a, b in zip(parts, got)]
    layers = []
    for layer in range(2):
        held = [part[layer] for part in parts]
        for step in range(2, 4):
            got = [exchange(part, ORDERS[i][step]) for i, part in enumerate(held)]
            held = [jnp.concatenate([a, b], 0) for a, b in zip(held, got)]
        got = [exchange(part, "c") for part in held]
        whole = []
        for i in range(4):
            both = jnp.stack([held[i], got[i]])
            axes = list(reversed(ORDERS[i]))
            cols = both.shape[-1]
            both = both.reshape((2, 2, 2, 2, 2, 24, cols))
            both = both.transpose([0] + [1 + axes.index(bit) for bit in WEIGHT_BITS[1:]] + [5, 6])
            whole.append(both.reshape(768, cols))
        layers.append(whole)
    return layers


def scatter_plane_large(parts):
    out = []
    for i, part in enumerate(parts):
        cols = part.shape[-1]
        out.append(part.reshape(2, 2, 2, 2, 2, 24, cols))
    got = [exchange(part[1], "c") for part in out]
    out = [add(part[0], other) for part, other in zip(out, got)]
    names = [list(WEIGHT_BITS[1:]) for _ in range(4)]
    return halve(out, names, (3, 2)), names


def add(left_side, right_side):
    return (left_side.astype(f32) + right_side.astype(f32)).astype(bf16)


def halve(parts, names, steps):
    for step in steps:
        keep, send = [], []
        for i, part in enumerate(parts):
            axis = names[i].index(ORDERS[i][step]) + part.ndim - 2 - len(names[i])
            keep.append(lax.index_in_dim(part, 0, axis, False))
            send.append(lax.index_in_dim(part, 1, axis, False))
        got = [exchange(part, ORDERS[i][step]) for i, part in enumerate(send)]
        for i in range(4):
            names[i].remove(ORDERS[i][step])
        parts = [add(a, b) for a, b in zip(keep, got)]
    return parts


def scatter_end(first_layer, second_layer, names):
    pipe = lax.axis_index("pipe")
    parts = [jnp.stack([a, b]) for a, b in zip(first_layer, second_layer)]
    parts = halve(parts, names, (1, 0))
    mine = jnp.concatenate([part[..., : PART_COLS[i]] for i, part in enumerate(parts)], -1)
    theirs = jnp.concatenate([part[..., PART_COLS[i] :] for i, part in enumerate(parts)], -1)
    total = mine.astype(f32) + exchange_both(theirs).astype(f32)
    keep = jnp.where(pipe == 0, total[0], total[1])
    send = jnp.where(pipe == 0, total[1], total[0]).astype(bf16)
    return keep + exchange_pipe(send).astype(f32)


def pack_small(b_query, b_value, b_up, vectors):
    rows = jnp.concatenate([b_query, b_value, b_up], 1)
    rows = jnp.pad(rows, ((0, 22), (0, 128 - 32 - 36)))
    cols = jnp.pad(jnp.stack(vectors, 1), ((0, 0), (0, 26)))
    return jnp.concatenate([cols, rows], 1)


def unpack_small(small):
    rows = small[:2, 32:68]
    return (rows[:, :6], rows[:, 6:12], rows[:, 12:36], [small[:, i] for i in range(6)])


def spread_small(small, place_units):
    vectors = [small[:, i].astype(f32) for i in range(6)]
    rows = jnp.concatenate([small[:, 32:68], small[:, 160:196]], 1)
    rows = rows.reshape(32, 24, 72)[:, :2].reshape(64, 72)
    rows = dot(place_units, rows)
    rows = rows.reshape(64, 2, 36)
    b_query = rows[:, :, :6].transpose(1, 2, 0).reshape(-1)
    b_value = rows[:, :, 6:12].transpose(1, 2, 0).reshape(-1)
    b_up = rows[:, :, 12:].transpose(1, 2, 0).reshape(-1)
    return b_query, b_value, b_up, vectors


def gather_small(b_query, b_value, b_up, vectors, place_units):
    rows = jnp.concatenate(
        [b_query.reshape(2, 6, HEAD), b_value.reshape(2, 6, HEAD), b_up.reshape(2, 24, HEAD)], 1
    )
    rows = rows.transpose(2, 0, 1).reshape(HEAD, 72).astype(bf16)
    rows = contract_rows(place_units, rows).astype(bf16)
    rows = jnp.pad(rows.reshape(32, 2, 72), ((0, 0), (0, 22), (0, 0))).reshape(768, 72)
    cols = jnp.pad(jnp.stack(vectors, 1).astype(bf16), ((0, 0), (0, 26)))
    gap = jnp.zeros((768, 60), bf16)
    return [jnp.concatenate([cols, rows[:, 36 * i : 36 * i + 36], gap], 1) for i in range(2)]


def layer_weights(whole, place_units):
    first, second, third, fourth = whole
    w_out = jnp.concatenate([second[:, :384], second[:, 1280:1664]], 1)
    small = jnp.concatenate([second[:, 384:512], second[:, 1664:1792]], 1)
    w_up = jnp.concatenate(
        [second[:, 512:1280], third[:, :768], second[:, 1792:], third[:, 1152:1920]], 1
    )
    w_down = jnp.concatenate(
        [third[:, 768:1152], fourth[:, :1152], third[:, 1920:], fourth[:, 1152:]], 1
    )
    b_query, b_value, b_up, vectors = spread_small(small, place_units)
    zeros = jnp.zeros((2, 384), f32)
    b_first = jnp.concatenate(
        [b_query.reshape(2, 384), zeros, b_value.reshape(2, 384)], 1
    ).reshape(-1)
    return (first, w_out, w_up, w_down, b_first, b_up, vectors)


def to_heads(rows):
    return rows.reshape(rows.shape[0], 2, 3, 6, HEAD).transpose(2, 1, 3, 0, 4).reshape(3, 12, -1, HEAD)


def layer_forward(section_in, length, weights):
    w_first, w_out, w_up, w_down, b_first, b_up, vectors = weights
    b_out, b_down, gain_one, shift_one, gain_two, shift_two = vectors
    normed, unit_one, scale_one = norm_forward(section_in, gain_one, shift_one)
    normed_b = normed.astype(bf16)
    heads = to_heads((dot(normed_b, w_first) + b_first).astype(bf16))
    query_b, key_b, value_b = heads[0], heads[1], heads[2]
    row_count = section_in.shape[0]
    scores = jnp.einsum("hqd,hkd->hqk", query_b, key_b, preferred_element_type=f32) * HEAD ** (-0.5)
    live_keys = (jnp.arange(row_count) < length)[None, None, :]
    scores = jnp.where(live_keys, scores, -1e30)
    powers = jnp.exp(scores - jnp.max(scores, -1, keepdims=True))
    soft = powers / jnp.sum(powers, -1, keepdims=True)
    soft_b = soft.astype(bf16)
    mixed = jnp.einsum("hqk,hkd->hqd", soft_b, value_b, preferred_element_type=f32)
    mixed_b = mixed.astype(bf16).transpose(1, 0, 2).reshape(row_count, -1)
    middle = section_in + contract_cols(mixed_b, w_out) + b_out
    normed_two, unit_two, scale_two = norm_forward(middle, gain_two, shift_two)
    normed_two_b = normed_two.astype(bf16)
    pre_active = dot(normed_two_b, w_up) + b_up
    active_b = jax.nn.gelu(pre_active, approximate=False).astype(bf16)
    result = middle + contract_cols(active_b, w_down) + b_down
    kept = (
        normed_b, unit_one, scale_one, query_b, key_b, value_b, soft, mixed_b,
        unit_two, scale_two, normed_two_b, pre_active, active_b,
    )
    return result, kept


def layer_backward(grad_rows, kept, weights, place_units):
    w_first, w_out, w_up, w_down, b_first, b_up, vectors = weights
    b_out, b_down, gain_one, shift_one, gain_two, shift_two = vectors
    (
        normed_b, unit_one, scale_one, query_b, key_b, value_b, soft, mixed_b,
        unit_two, scale_two, normed_two_b, pre_active, active_b,
    ) = kept
    row_count = grad_rows.shape[0]
    grad_b = grad_rows.astype(bf16)
    down_bias_term = jnp.sum(grad_rows, 0)
    down_term = contract_rows(grad_b, active_b).astype(bf16)
    grad_upper_b = (dot(grad_b, w_down) * gelu_slope(pre_active)).astype(bf16)
    up_bias_term = jnp.sum(grad_upper_b, 0, dtype=f32)
    up_term = contract_rows(normed_two_b, grad_upper_b).astype(bf16)
    grad_normed_two = contract_cols(grad_upper_b, w_up)
    grad_norm_two, gain_two_term, shift_two_term = norm_backward(
        grad_normed_two, unit_two, scale_two, gain_two
    )
    grad_middle = grad_rows + grad_norm_two
    out_bias_term = jnp.sum(grad_middle, 0)
    grad_middle_b = grad_middle.astype(bf16)
    out_term = contract_rows(grad_middle_b, mixed_b).astype(bf16)
    grad_mixed_b = dot(grad_middle_b, w_out).astype(bf16)
    grad_heads = grad_mixed_b.reshape(row_count, 12, HEAD).transpose(1, 0, 2)
    soft_b = soft.astype(bf16)
    grad_soft = jnp.einsum("hqd,hkd->hqk", grad_heads, value_b, preferred_element_type=f32)
    grad_scores_b = (soft * (grad_soft - jnp.sum(grad_soft * soft, -1, keepdims=True))).astype(bf16)
    factor = HEAD ** (-0.5)
    grad_query = jnp.einsum("hqk,hkd->hqd", grad_scores_b, key_b, preferred_element_type=f32) * factor
    grad_key = jnp.einsum("hqk,hqd->hkd", grad_scores_b, query_b, preferred_element_type=f32) * factor
    grad_value = jnp.einsum("hqk,hqd->hkd", soft_b, grad_heads, preferred_element_type=f32)
    grad_first_b = jnp.stack([grad_query.astype(bf16), grad_key.astype(bf16), grad_value.astype(bf16)])
    query_bias_term = jnp.sum(grad_first_b[0], 1, dtype=f32).reshape(-1)
    value_bias_term = jnp.sum(grad_first_b[2], 1, dtype=f32).reshape(-1)
    grad_first_b = (
        grad_first_b.reshape(3, 2, 6, row_count, HEAD).transpose(3, 1, 0, 2, 4).reshape(row_count, -1)
    )
    first_term = contract_rows(normed_b, grad_first_b).astype(bf16)
    grad_normed = contract_cols(grad_first_b, w_first)
    grad_norm_one, gain_one_term, shift_one_term = norm_backward(
        grad_normed, unit_one, scale_one, gain_one
    )
    grad_input = grad_middle + grad_norm_one
    small = gather_small(
        query_bias_term, value_bias_term, up_bias_term,
        [out_bias_term, down_bias_term, gain_one_term, shift_one_term, gain_two_term, shift_two_term],
        place_units,
    )
    parts = [
        first_term,
        jnp.concatenate(
            [out_term[:, :384], small[0], up_term[:, :768], out_term[:, 384:], small[1], up_term[:, 1536:2304]], 1
        ),
        jnp.concatenate(
            [up_term[:, 768:1536], down_term[:, :384], up_term[:, 2304:], down_term[:, 1536:1920]], 1
        ),
        jnp.concatenate([down_term[:, 384:1536], down_term[:, 1920:]], 1),
    ]
    return grad_input, parts


def share_outputs(first_rows, second_rows):
    pipe, tensor = lax.axis_index("pipe"), lax.axis_index("tensor")
    keep = jnp.where(pipe == 0, first_rows, second_rows)
    send = jnp.where(pipe == 0, second_rows, first_rows)
    same_pipe = exchange_tensor(keep)
    other_pipe = exchange_pipe(send)
    other_both = exchange_both(send)
    rows = jnp.stack([keep, same_pipe, other_pipe, other_both])
    rows = jnp.where(tensor == 0, rows, rows[jnp.array([1, 0, 3, 2])])
    return jnp.where(pipe == 0, rows, rows[jnp.array([2, 3, 0, 1])])[None]


def local(clip_frames, out_cotangent, clip_lengths, *params):
    params = [param[0] for param in params]
    w_query, w_key, w_value, w_out, w_up, w_down, b_query, b_value, b_out, b_up, b_down = params[:11]
    pipe, tensor = lax.axis_index("pipe"), lax.axis_index("tensor")
    shard = lax.axis_index("z") * 8 + lax.axis_index("x") * 2 + lax.axis_index("core")
    micro = pipe * 2 + tensor

    blocks = shard ^ jnp.asarray(MASKS)
    rows_at = (blocks[:, None] * 24 + jnp.arange(24)[None]).reshape(-1)
    place_rows = (jnp.arange(768)[:, None] == rows_at[None]).astype(bf16)
    units_at = (blocks[:, None] * 2 + jnp.arange(2)[None]).reshape(-1)
    place_units = (jnp.arange(64)[:, None] == units_at[None]).astype(bf16)

    small = pack_small(b_query, b_value, b_up, [b_out, b_down] + params[11:])
    own = jnp.concatenate(pack_parts(w_query, w_key, w_value, w_out, w_up, w_down, small), 1)
    layers = gather_layers(own)
    weights = [layer_weights(whole, place_units) for whole in layers]

    frames = lax.dynamic_index_in_dim(clip_frames, micro, 0, keepdims=False)
    cotangent = lax.dynamic_index_in_dim(out_cotangent, micro, 0, keepdims=False)
    length = lax.dynamic_index_in_dim(clip_lengths, micro, 0, keepdims=False)[0]
    section_in = dot(frames, place_rows)
    grad_out = dot(cotangent, place_rows)

    def placed_back(rows):
        return contract_cols(rows, place_rows).astype(bf16)

    first_out, kept_first = layer_forward(section_in, length, weights[0])
    first_out = first_out.astype(bf16)
    second_out, kept_second = layer_forward(first_out.astype(f32), length, weights[1])
    second_out = second_out.astype(bf16)
    section_output = share_outputs(placed_back(first_out), placed_back(second_out))

    second_grad, second_parts = layer_backward(grad_out, kept_second, weights[1], place_units)
    second_grad = second_grad.astype(bf16)
    second_parts, names = scatter_plane_large(second_parts)
    first_grad, first_parts = layer_backward(second_grad.astype(f32), kept_first, weights[0], place_units)
    first_grad = first_grad.astype(bf16)
    first_parts, _ = scatter_plane_large(first_parts)
    input_grad = share_outputs(placed_back(first_grad), placed_back(second_grad))

    total = scatter_end(first_parts, second_parts, names)
    (g_query, g_key, g_value, g_out, g_up, g_down, g_small) = unpack_parts(split_parts(total))
    gb_query, gb_value, gb_up, vectors = unpack_small(g_small)
    grads = [g_query, g_key, g_value, g_out, g_up, g_down, gb_query, gb_value, vectors[0], gb_up] + vectors[1:]
    return (section_output, input_grad) + tuple(grad[None] for grad in grads)


def solution(mesh):
    fine = Mesh(
        mesh.devices.reshape(2, 4, 4, 2, 2), ("pipe", "z", "x", "core", "tensor")
    )
    shard = ("z", "x", "core")
    rows = P(None, shard, None)
    matrix = P("pipe", shard, "tensor")
    vector = P("pipe", shard)
    params = (matrix,) * 8 + (vector, matrix) + (vector,) * 5
    return jax.shard_map(
        local,
        mesh=fine,
        in_specs=(rows, rows, P(None, shard)) + params,
        out_specs=(P("pipe", None, shard, None),) * 2 + params,
        check_vma=False,
    )
```

```python
import functools

import jax
import jax.numpy as jnp
import numpy as np
from jax import lax
from jax.experimental import pallas as pl
from jax.experimental.pallas import tpu as pltpu
from jax.sharding import Mesh
from jax.sharding import PartitionSpec as P

HEAD = 64
bf16 = jnp.bfloat16
f32 = jnp.float32

half_root = 0.7071067811865476
gauss_factor = 0.3989422804014327


def dot(left_side, right_side):
    return lax.dot_general(left_side, right_side, (((1,), (0,)), ((), ())), preferred_element_type=f32)


def dot_rows(left_side, right_side):
    return lax.dot_general(left_side, right_side, (((0,), (0,)), ((), ())), preferred_element_type=f32)


def dot_cols(left_side, right_side):
    return lax.dot_general(left_side, right_side, (((1,), (1,)), ((), ())), preferred_element_type=f32)


def norm_parts(values):
    center = values - jnp.mean(values, -1, keepdims=True)
    rescale = lax.rsqrt(jnp.mean(center * center, -1, keepdims=True) + 1e-05)
    return center * rescale, rescale


def norm_backward(grad_rows, normed, rescale, norm_gain):
    scaled = grad_rows * norm_gain
    inner = (
        scaled
        - jnp.mean(scaled, -1, keepdims=True)
        - normed * jnp.mean(scaled * normed, -1, keepdims=True)
    )
    return rescale * inner


def attention_forward_kernel(
    length_ref, x_ref, own_ref, peer_ref, own_out_ref, peer_out_ref, vec_ref,
    middle_ref, heads_ref, soft_ref, mixed_ref,
):
    length = length_ref[0]
    normed, _ = norm_parts(x_ref[...].astype(f32))
    normed_b = (normed * vec_ref[2:3] + vec_ref[3:4]).astype(bf16)
    for j in range(3):
        for half, weight_ref in enumerate((own_ref, peer_ref)):
            cols = slice(384 * half, 384 * half + 384)
            rows = dot(normed_b, weight_ref[j])
            if j != 1:
                rows = rows + vec_ref[6 + j // 2 : 7 + j // 2, cols]
            heads_ref[j, :, cols] = rows.astype(bf16)
    count = x_ref.shape[0]
    live_keys = lax.broadcasted_iota(jnp.int32, (count, count), 1) < length
    for pair in range(6):
        both = []
        for head in (2 * pair, 2 * pair + 1):
            cols = slice(HEAD * head, HEAD * head + HEAD)
            scores = dot_cols(heads_ref[0, :, cols], heads_ref[1, :, cols]) * HEAD ** (-0.5)
            scores = jnp.where(live_keys, scores, -1e30)
            powers = jnp.exp(scores - jnp.max(scores, -1, keepdims=True))
            soft = powers / jnp.sum(powers, -1, keepdims=True)
            soft_ref[head] = soft
            both.append(dot(soft.astype(bf16), heads_ref[2, :, cols]))
        mixed_ref[:, 128 * pair : 128 * pair + 128] = jnp.concatenate(both, 1).astype(bf16)
    total = dot_cols(mixed_ref[:, :384], own_out_ref[:, :384])
    total = total + dot_cols(mixed_ref[:, 384:], peer_out_ref[:, :384])
    middle_ref[...] = x_ref[...].astype(f32) + total + vec_ref[0:1]


def units_forward_kernel(middle_ref, own_ref, peer_ref, vec_ref, up_bias_ref, result_ref, active_ref, slope_ref):
    middle = middle_ref[...]
    normed, _ = norm_parts(middle)
    normed_b = (normed * vec_ref[4:5] + vec_ref[5:6]).astype(bf16)
    total = middle + vec_ref[1:2]
    for half, weight_ref in enumerate((own_ref, peer_ref)):
        for j in range(2):
            cols = slice(768 * (2 * half + j), 768 * (2 * half + j) + 768)
            pre_active = dot(normed_b, weight_ref[j]) + up_bias_ref[0:1, cols]
            below = 0.5 * (1.0 + lax.erf(pre_active * half_root))
            active_b = (pre_active * below).astype(bf16)
            active_ref[:, cols] = active_b
            slope_ref[:, cols] = below + pre_active * jnp.exp(-0.5 * pre_active * pre_active) * gauss_factor
            total = total + dot_cols(active_b, weight_ref[2 + j])
    result_ref[...] = total.astype(bf16)


def units_backward_kernel(
    grad_ref, middle_ref, active_ref, slope_ref, own_ref, peer_ref, vec_ref,
    grad_middle_ref, grad_own_ref, grad_peer_ref, vec_grad_ref, up_bias_grad_ref,
):
    grad_b = grad_ref[...]
    grad_rows = grad_b.astype(f32)
    normed, rescale = norm_parts(middle_ref[...])
    normed_b = (normed * vec_ref[4:5] + vec_ref[5:6]).astype(bf16)
    normed_t = normed_b.T
    grad_t = grad_b.T
    grad_normed = None
    for half, weight_ref, out_ref in ((1, peer_ref, grad_peer_ref), (0, own_ref, grad_own_ref)):
        for j in range(2):
            cols = slice(768 * (2 * half + j), 768 * (2 * half + j) + 768)
            out_ref[2 + j] = dot(grad_t, active_ref[:, cols]).astype(bf16)
            grad_upper = (dot(grad_b, weight_ref[2 + j]) * slope_ref[:, cols]).astype(bf16)
            up_bias_grad_ref[0:1, cols] = jnp.sum(grad_upper.astype(f32), 0, keepdims=True)
            out_ref[j] = dot(normed_t, grad_upper).astype(bf16)
            term = dot_cols(grad_upper, weight_ref[j])
            grad_normed = term if grad_normed is None else grad_normed + term
    grad_middle = grad_rows + norm_backward(grad_normed, normed, rescale, vec_ref[4:5])
    grad_middle_ref[...] = grad_middle
    vec_grad_ref[...] = jnp.zeros_like(vec_grad_ref)
    vec_grad_ref[0:1] = jnp.sum(grad_middle, 0, keepdims=True)
    vec_grad_ref[1:2] = jnp.sum(grad_rows, 0, keepdims=True)
    vec_grad_ref[4:5] = jnp.sum(grad_normed * normed, 0, keepdims=True)
    vec_grad_ref[5:6] = jnp.sum(grad_normed, 0, keepdims=True)


def attention_backward_kernel(
    grad_ref, x_ref, heads_ref, soft_ref, mixed_ref, own_ref, peer_ref, own_out_ref, peer_out_ref, vec_ref,
    grad_in_ref, grad_own_ref, grad_peer_ref, grad_own_out_ref, grad_peer_out_ref, vec_grad_ref,
    grad_mixed_ref, grad_heads_ref,
):
    grad_b = grad_ref[...].astype(bf16)
    grad_t = grad_b.T
    grad_peer_out_ref[...] = dot(grad_t, mixed_ref[:, 384:]).astype(bf16)
    grad_own_out_ref[...] = dot(grad_t, mixed_ref[:, :384]).astype(bf16)
    grad_mixed_ref[:, :384] = dot(grad_b, own_out_ref[:, :384]).astype(bf16)
    grad_mixed_ref[:, 384:] = dot(grad_b, peer_out_ref[:, :384]).astype(bf16)
    factor = HEAD ** (-0.5)
    for pair in range(6):
        found = ([], [], [])
        for head in (2 * pair, 2 * pair + 1):
            cols = slice(HEAD * head, HEAD * head + HEAD)
            soft = soft_ref[head]
            grad_head = grad_mixed_ref[:, cols]
            grad_soft = dot_cols(grad_head, heads_ref[2, :, cols])
            inner = jnp.sum(grad_soft * soft, -1, keepdims=True)
            grad_scores = (soft * (grad_soft - inner)).astype(bf16)
            found[0].append(dot(grad_scores, heads_ref[1, :, cols]) * factor)
            found[1].append(dot_rows(grad_scores, heads_ref[0, :, cols]) * factor)
            found[2].append(dot_rows(soft.astype(bf16), grad_head))
        for j in range(3):
            grad_heads_ref[j, :, 128 * pair : 128 * pair + 128] = jnp.concatenate(found[j], 1).astype(bf16)
    normed, rescale = norm_parts(x_ref[...].astype(f32))
    normed_b = (normed * vec_ref[2:3] + vec_ref[3:4]).astype(bf16)
    normed_t = normed_b.T
    grad_normed = None
    for half, weight_ref, out_ref in ((1, peer_ref, grad_peer_ref), (0, own_ref, grad_own_ref)):
        for j in range(3):
            rows = grad_heads_ref[j, :, 384 * half : 384 * half + 384]
            out_ref[j] = dot(normed_t, rows).astype(bf16)
            term = dot_cols(rows, weight_ref[j])
            grad_normed = term if grad_normed is None else grad_normed + term
    grad_in = grad_ref[...] + norm_backward(grad_normed, normed, rescale, vec_ref[2:3])
    grad_in_ref[...] = grad_in.astype(bf16)
    vec_grad_ref[...] = jnp.zeros_like(vec_grad_ref)
    vec_grad_ref[2:3] = jnp.sum(grad_normed * normed, 0, keepdims=True)
    vec_grad_ref[3:4] = jnp.sum(grad_normed, 0, keepdims=True)
    vec_grad_ref[6:7] = jnp.sum(grad_heads_ref[0].astype(f32), 0, keepdims=True)
    vec_grad_ref[7:8] = jnp.sum(grad_heads_ref[2].astype(f32), 0, keepdims=True)


def kernel_call(kernel, name, inputs, outputs, flops, scratch=(), scalar=False):
    whole = pl.BlockSpec(memory_space=pltpu.VMEM)
    specs = [whole] * len(inputs)
    if scalar:
        specs[0] = pl.BlockSpec(memory_space=pltpu.SMEM)
    shapes = [jax.ShapeDtypeStruct(shape, dtype) for shape, dtype in outputs]
    moved = sum(int(np.prod(a.shape)) * a.dtype.itemsize for a in list(inputs) + shapes)
    return pl.pallas_call(
        kernel,
        name=name,
        out_shape=shapes,
        in_specs=specs,
        out_specs=[whole] * len(shapes),
        scratch_shapes=list(scratch),
        cost_estimate=pl.CostEstimate(flops=flops, bytes_accessed=moved, transcendentals=0),
        compiler_params=pltpu.CompilerParams(vmem_limit_bytes=52 * 2**20),
    )(*inputs)


ROWS = (192, 768)
HEADS_SHAPE = (3, 192, 768)


def attention_forward(length, x, attn, vec):
    own, peer, own_out, peer_out = attn
    return kernel_call(
        attention_forward_kernel, "attention_forward",
        [length, x, own, peer, own_out, peer_out, vec],
        [(ROWS, f32), (HEADS_SHAPE, bf16), ((12, 192, 192), f32), (ROWS, bf16)],
        1_100_000_000, scalar=True,
    )


def units_forward(middle, units, vec, up_bias):
    own, peer = units
    return kernel_call(
        units_forward_kernel, "units_forward", [middle, own, peer, vec, up_bias],
        [(ROWS, bf16), ((192, 3072), bf16), ((192, 3072), f32)], 1_800_000_000,
    )


def units_backward(grad_b, middle, active, slope, units, vec):
    own, peer = units
    return kernel_call(
        units_backward_kernel, "units_backward", [grad_b, middle, active, slope, own, peer, vec],
        [(ROWS, f32), (own.shape, bf16), (peer.shape, bf16), ((8, 768), f32), ((1, 3072), f32)], 3_600_000_000,
    )


def attention_backward(grad_middle, x, heads, soft, mixed, attn, vec):
    own, peer, own_out, peer_out = attn
    return kernel_call(
        attention_backward_kernel, "attention_backward",
        [grad_middle, x, heads, soft, mixed, own, peer, own_out, peer_out, vec],
        [(ROWS, bf16), (own.shape, bf16), (peer.shape, bf16), ((768, 384), bf16), ((768, 384), bf16), ((8, 768), f32)],
        2_300_000_000,
        scratch=[pltpu.VMEM(ROWS, bf16), pltpu.VMEM(HEADS_SHAPE, bf16)],
    )


EXCHANGES = {"xu": ("x", 4, 1), "xv": ("x", 4, 3), "zu": ("z", 4, 1), "zv": ("z", 4, 3), "c": ("core", 2, 1)}
BLOCK_BITS = ("zv", "zu", "xv", "xu")
BIT_MASK = {"xu": 1, "xv": 3, "zu": 4, "zv": 12}
ORDERS = (
    ("xu", "xv", "zu", "zv"),
    ("xv", "xu", "zv", "zu"),
    ("zu", "zv", "xu", "xv"),
    ("zv", "zu", "xv", "xu"),
)
MASKS = np.zeros(16, np.int32)
for _index in range(16):
    for _place, _bit in enumerate(BLOCK_BITS):
        if (_index >> (3 - _place)) & 1:
            MASKS[_index] ^= BIT_MASK[_bit]
ATTN_COLS = (384, 384, 384, 512)


def exchange(value, bit):
    axis, size, flip = EXCHANGES[bit]
    return lax.ppermute(value, axis, [(i, i ^ flip) for i in range(size)])


def exchange_pipe(value):
    return lax.ppermute(value, "pipe", [(0, 1), (1, 0)])


def exchange_both(value):
    return lax.ppermute(value, ("pipe", "tensor"), [(i, i ^ 3) for i in range(4)])


def exchange_tensor(value):
    return lax.ppermute(value, "tensor", [(0, 1), (1, 0)])


def pin(*values):
    return lax.optimization_barrier(values)


def block_place(part, index):
    place = 0
    for step in range(4):
        if (index >> step) & 1:
            place += 8 >> BLOCK_BITS.index(ORDERS[part][step])
    return place


def assemble_kernel(counts, *refs):
    total = sum(counts)
    held, got, outs, sems = refs[:total], refs[total : 2 * total], refs[2 * total : -1], refs[-1]
    copies = []
    for part in range(total):
        if len(counts) == 1 or part < counts[0]:
            target = outs[0].at[part]
        else:
            target = outs[1]
        for index in range(16):
            source = (held if index < 8 else got)[part].at[index % 8]
            rows = target.at[pl.ds(48 * block_place(part, index), 48)]
            copies.append(pltpu.make_async_copy(source, rows, sems.at[len(copies)]))
            copies[-1].start()
    for copy in copies:
        copy.wait()


def assemble(held, got):
    cols = [part.shape[-1] for part in held]
    if cols[0] == cols[3]:
        counts, shapes = (4,), [(4, 768, cols[0])]
    else:
        counts, shapes = (3, 1), [(3, 768, cols[0]), (768, cols[3])]
    anywhere = pl.BlockSpec(memory_space=pl.ANY)
    return pl.pallas_call(
        functools.partial(assemble_kernel, counts),
        name="assemble",
        out_shape=[jax.ShapeDtypeStruct(shape, bf16) for shape in shapes],
        in_specs=[anywhere] * 8,
        out_specs=[anywhere] * len(shapes),
        scratch_shapes=[pltpu.SemaphoreType.DMA((64,))],
        cost_estimate=pl.CostEstimate(flops=0, bytes_accessed=2 * 768 * 2 * sum(cols), transcendentals=0),
    )(*held, *got)


def gather_start(own):
    pipe, core = lax.axis_index("pipe"), lax.axis_index("core")
    mine = jnp.where(core == 0, own[0], own[1])
    other = exchange(jnp.where(core == 0, own[1], own[0]), "c")
    rows = jnp.where(core == 0, jnp.concatenate([mine, other]), jnp.concatenate([other, mine]))
    other = exchange_pipe(rows)
    mine = jnp.stack([jnp.where(pipe == 0, rows, other), jnp.where(pipe == 0, other, rows)])
    theirs = exchange_both(mine)
    a, b = mine, theirs
    parts = [
        [a[..., :192], b[..., :192], a[..., 832:1600]],
        [a[..., 192:384], b[..., 192:384], b[..., 832:1600]],
        [a[..., 384:576], b[..., 384:576], a[..., 1600:]],
        [a[..., 576:768], b[..., 576:768], a[..., 768:832], b[..., 768:832], b[..., 1600:]],
    ]
    parts = [jnp.concatenate(part, -1)[:, None] for part in parts]
    for step in range(2):
        got = [exchange(part, ORDERS[i][step]) for i, part in enumerate(parts)]
        parts = [jnp.concatenate([x, y], 1) for x, y in zip(parts, got)]
    groups = []
    for layer in range(2):
        groups.append([part[layer, :, :, : ATTN_COLS[i]] for i, part in enumerate(parts)])
        groups.append([part[layer, :, :, ATTN_COLS[i] :] for i, part in enumerate(parts)])
    return groups


def gather_third(held):
    got = [exchange(part, ORDERS[i][2]) for i, part in enumerate(held)]
    return [jnp.concatenate([x, y], 0) for x, y in zip(held, got)]


def gather_fourth(held):
    return [exchange(part, ORDERS[i][3]) for i, part in enumerate(held)]


def gather_core(held, got):
    own = assemble(held, got)
    return own, [exchange(array, "c") for array in own]


def add(left_side, right_side):
    return (left_side.astype(f32) + right_side.astype(f32)).astype(bf16)


def halve(state, step):
    out = []
    for i, (names, x, y) in enumerate(state):
        bit = ORDERS[i][step]
        axis = names.index(bit) + x.ndim - 2 - len(names)
        keep, send = [add(lax.index_in_dim(x, side, axis, False), lax.index_in_dim(y, side, axis, False)) for side in (0, 1)]
        out.append((tuple(name for name in names if name != bit), keep, exchange(send, bit)))
    return out


def scatter_core(own, other):
    got = [exchange(array, "c") for array in other]
    state = []
    for x, y in zip(own, got):
        shape = (2, 2, 2, 2, 48, x.shape[-1])
        for_part = (lambda v: [v]) if x.ndim == 2 else list
        for u, v in zip(for_part(x), for_part(y)):
            state.append((BLOCK_BITS, u.reshape(shape), v.reshape(shape)))
    return state


def scatter_end(groups):
    pipe, core = lax.axis_index("pipe"), lax.axis_index("core")
    state = []
    for i in range(4):
        sides = []
        for side in (1, 2):
            layers = [jnp.concatenate([groups[2 * k][i][side], groups[2 * k + 1][i][side]], -1) for k in range(2)]
            sides.append(jnp.stack(layers))
        state.append((groups[0][i][0], *sides))
    state = halve(halve(state, 1), 0)
    p = [x.astype(f32) + y.astype(f32) for _, x, y in state]
    mine = [p[0][..., :192], p[1][..., :192], p[2][..., :192], p[3][..., :192], p[3][..., 384:448]]
    mine = jnp.concatenate(mine + [p[0][..., 384:], p[2][..., 384:]], -1)
    theirs = [p[0][..., 192:384], p[1][..., 192:384], p[2][..., 192:384], p[3][..., 192:384], p[3][..., 448:512]]
    theirs = jnp.concatenate(theirs + [p[1][..., 384:], p[3][..., 512:]], -1)
    total = mine + exchange_both(theirs.astype(bf16)).astype(f32)
    keep = jnp.where(pipe == 0, total[0], total[1])
    send = jnp.where(pipe == 0, total[1], total[0]).astype(bf16)
    rows = keep + exchange_pipe(send).astype(f32)
    keep = jnp.where(core == 0, rows[:24], rows[24:])
    send = jnp.where(core == 0, rows[24:], rows[:24]).astype(bf16)
    other = exchange(send, "c").astype(f32)
    return jnp.where(core == 0, keep, other), jnp.where(core == 0, other, keep)


def share_outputs(first_rows, second_rows):
    pipe, tensor = lax.axis_index("pipe"), lax.axis_index("tensor")
    keep = jnp.where(pipe == 0, first_rows, second_rows)
    send = jnp.where(pipe == 0, second_rows, first_rows)
    return keep, exchange_tensor(keep), exchange_pipe(send), exchange_both(send)


def order_outputs(rows):
    pipe, tensor = lax.axis_index("pipe"), lax.axis_index("tensor")
    a, b, c, d = rows
    a, b = jnp.where(tensor == 0, a, b), jnp.where(tensor == 0, b, a)
    c, d = jnp.where(tensor == 0, c, d), jnp.where(tensor == 0, d, c)
    a, c = jnp.where(pipe == 0, a, c), jnp.where(pipe == 0, c, a)
    b, d = jnp.where(pipe == 0, b, d), jnp.where(pipe == 0, d, b)
    return jnp.stack([a, b, c, d])[None]


def pack_share(w_query, w_key, w_value, w_out, w_up, w_down, b_query, b_value, b_up, vectors):
    cols = jnp.pad(jnp.stack(vectors, 1), ((0, 0), (0, 2)))
    out = []
    for half in range(2):
        third, sixth, whole = (slice(n * half, n * half + n) for n in (3, 12, 192))
        rows = jnp.concatenate([b_query[:, third], b_value[:, third], b_up[:, sixth]], 1)
        small = jnp.concatenate([cols, jnp.pad(rows, ((0, 22), (0, 38)))], 1)
        wide = slice(768 * half, 768 * half + 768)
        out.append(
            jnp.concatenate(
                [w_query[:, whole], w_key[:, whole], w_value[:, whole], w_out[:, whole], small, w_up[:, wide], w_down[:, wide]],
                1,
            )
        )
    return out


def unpack_share(halves):
    def cols(start, stop):
        return jnp.concatenate([half[:, start:stop] for half in halves], 1)

    grads = [cols(192 * i, 192 * i + 192) for i in range(4)] + [cols(832, 1600), cols(1600, 2368)]
    rows = [half[:2, 776:794] for half in halves]
    bias = [jnp.concatenate([row[:, lo:hi] for row in rows], 1) for lo, hi in ((0, 3), (3, 6), (6, 18))]
    return grads, bias, [halves[0][:, 768 + i] for i in range(6)]


def spread_small(own_out, peer_out, place_units):
    vectors = own_out[:, 384:390].astype(f32).T
    rows = jnp.concatenate([own_out[:, 384:], peer_out[:, 384:]], 1).reshape(32, 24, 4, 64)[:, :2, :, 8:26]
    rows = dot(place_units, rows.reshape(64, 72)).reshape(64, 4, 18).transpose(1, 2, 0)
    b_query, b_value = rows[:, :3].reshape(1, 768), rows[:, 3:6].reshape(1, 768)
    return jnp.concatenate([vectors, b_query, b_value]), rows[:, 6:].reshape(1, 3072)


def gather_small(vec_grad, up_bias_grad, place_units):
    rows = jnp.concatenate(
        [vec_grad[6].reshape(4, 3, HEAD), vec_grad[7].reshape(4, 3, HEAD), up_bias_grad.reshape(4, 12, HEAD)], 1
    )
    rows = rows.transpose(2, 0, 1).reshape(HEAD, 72).astype(bf16)
    rows = dot_rows(place_units, rows).astype(bf16).reshape(32, 2, 4, 18)
    rows = jnp.pad(rows, ((0, 0), (0, 22), (0, 0), (8, 38))).reshape(768, 256)
    cols = jnp.pad(vec_grad[:6].T.astype(bf16), ((0, 0), (0, 58)))
    small = rows + jnp.concatenate([cols] * 4, 1)
    return small[:, :128], small[:, 128:]


def local(clip_frames, out_cotangent, clip_lengths, *params):
    params = [param[0] for param in params]
    w_query, w_key, w_value, w_out, w_up, w_down, b_query, b_value, b_out, b_up, b_down = params[:11]
    micro = lax.axis_index("pipe") * 2 + lax.axis_index("tensor")
    chip = lax.axis_index("z") * 4 + lax.axis_index("x")

    blocks = (chip ^ jnp.asarray(MASKS))[:, None]
    rows_at = (blocks * 48 + jnp.arange(48)[None]).reshape(-1)
    place_rows = (jnp.arange(768)[:, None] == rows_at[None]).astype(bf16)
    units_at = (blocks * 4 + jnp.arange(4)[None]).reshape(-1)
    place_units = (jnp.arange(64)[:, None] == units_at[None]).astype(bf16)

    own = pack_share(
        w_query, w_key, w_value, w_out, w_up, w_down, b_query, b_value, b_up, [b_out, b_down] + params[11:]
    )
    groups = gather_start(own)

    frames = lax.dynamic_index_in_dim(clip_frames, micro, 0, keepdims=False)
    cotangent = lax.dynamic_index_in_dim(out_cotangent, micro, 0, keepdims=False)
    length = lax.dynamic_index_in_dim(clip_lengths, micro, 0, keepdims=False)
    x_first = dot(frames, place_rows).astype(bf16)
    grad_out = dot(cotangent, place_rows).astype(bf16)

    def placed_back(rows):
        return dot_cols(rows, place_rows).astype(bf16)

    def attn_of(own, peer):
        return own[0], peer[0], own[1], peer[1]

    held = [gather_third(group) for group in groups]
    got = [gather_fourth(held[0]), gather_fourth(held[1])]
    attn_first = attn_of(*gather_core(held[0], got[0]))
    vec_first, up_bias_first = spread_small(attn_first[2], attn_first[3], place_units)
    middle_first, heads_first, soft_first, mixed_first = attention_forward(length, x_first, attn_first, vec_first)
    units_first = [array[0] for array in gather_core(held[1], got[1])]
    got.append(gather_fourth(held[2]))
    middle_first, got[2] = pin(middle_first, got[2])
    x_second, active_first, slope_first = units_forward(middle_first, units_first, vec_first, up_bias_first)
    attn_second = attn_of(*gather_core(held[2], got[2]))
    got.append(gather_fourth(held[3]))
    x_second, got[3] = pin(x_second, got[3])
    vec_second, up_bias_second = spread_small(attn_second[2], attn_second[3], place_units)
    middle_second, heads_second, soft_second, mixed_second = attention_forward(length, x_second, attn_second, vec_second)
    units_second = [array[0] for array in gather_core(held[3], got[3])]
    out_second, active_second, slope_second = units_forward(middle_second, units_second, vec_second, up_bias_second)
    shared = share_outputs(placed_back(x_second), placed_back(out_second))

    grad_middle, grad_own, grad_peer, vec_grad_second, up_bias_grad = units_backward(
        grad_out, middle_second, active_second, slope_second, units_second, vec_second
    )
    units_state = [None, scatter_core([grad_own], [grad_peer])]
    second_grad, grad_own, grad_peer, grad_own_out, grad_peer_out, vec_grad = attention_backward(
        grad_middle, x_second, heads_second, soft_second, mixed_second, attn_second, vec_second
    )
    small_own, small_peer = gather_small(vec_grad_second + vec_grad, up_bias_grad, place_units)
    grad_own_out = jnp.concatenate([grad_own_out, small_own], 1)
    grad_peer_out = jnp.concatenate([grad_peer_out, small_peer], 1)
    second_grad, units_state[1], shared = pin(second_grad, [s[1:] for s in units_state[1]], shared)
    units_state[1] = [(BLOCK_BITS, *s) for s in units_state[1]]
    section_output = order_outputs(shared)
    attn_state = [None, scatter_core([grad_own, grad_own_out], [grad_peer, grad_peer_out])]

    units_state[1] = halve(units_state[1], 3)
    grad_middle, grad_own, grad_peer, vec_grad_first, up_bias_grad = units_backward(
        second_grad, middle_first, active_first, slope_first, units_first, vec_first
    )
    names = [[s[0] for s in units_state[1]], [s[0] for s in attn_state[1]]]
    grad_middle, values = pin(grad_middle, ([s[1:] for s in units_state[1]], [s[1:] for s in attn_state[1]]))
    units_state[1] = [(name, *s) for name, s in zip(names[0], values[0])]
    attn_state[1] = [(name, *s) for name, s in zip(names[1], values[1])]
    units_state[1] = halve(units_state[1], 2)
    attn_state[1] = halve(attn_state[1], 3)
    units_state[0] = scatter_core([grad_own], [grad_peer])
    first_grad, grad_own, grad_peer, grad_own_out, grad_peer_out, vec_grad = attention_backward(
        grad_middle, x_first, heads_first, soft_first, mixed_first, attn_first, vec_first
    )
    states = (units_state[1], attn_state[1], units_state[0])
    names = [[s[0] for s in state] for state in states]
    grad_own, grad_peer, values = pin(grad_own, grad_peer, [[s[1:] for s in state] for state in states])
    units_state[1], attn_state[1], units_state[0] = [
        [(name, *s) for name, s in zip(some, state)] for some, state in zip(names, values)
    ]
    small_own, small_peer = gather_small(vec_grad_first + vec_grad, up_bias_grad, place_units)
    grad_own_out = jnp.concatenate([grad_own_out, small_own], 1)
    grad_peer_out = jnp.concatenate([grad_peer_out, small_peer], 1)
    attn_state[0] = scatter_core([grad_own, grad_own_out], [grad_peer, grad_peer_out])
    units_state[0] = halve(halve(units_state[0], 3), 2)
    attn_state[1] = halve(attn_state[1], 2)
    attn_state[0] = halve(halve(attn_state[0], 3), 2)
    input_grad = order_outputs(share_outputs(placed_back(first_grad), placed_back(second_grad)))

    halves = scatter_end([attn_state[0], units_state[0], attn_state[1], units_state[1]])
    grads, bias, vectors = unpack_share(halves)
    grads = grads + [bias[0], bias[1], vectors[0], bias[2]] + vectors[1:]
    return (section_output, input_grad) + tuple(grad[None] for grad in grads)


def solution(mesh):
    fine = Mesh(mesh.devices.reshape(2, 4, 4, 2, 2), ("pipe", "z", "x", "core", "tensor"))
    shard = ("z", "x", "core")
    rows = P(None, shard, None)
    matrix = P("pipe", shard, "tensor")
    vector = P("pipe", shard)
    params = (matrix,) * 8 + (vector, matrix) + (vector,) * 5
    return jax.shard_map(
        local,
        mesh=fine,
        in_specs=(rows, rows, P(None, shard)) + params,
        out_specs=(P("pipe", None, shard, None),) * 2 + params,
        check_vma=False,
    )
```

```python
import functools

import jax
import jax.numpy as jnp
import numpy as np
from jax import lax
from jax.experimental import pallas as pl
from jax.experimental.pallas import tpu as pltpu
from jax.sharding import Mesh
from jax.sharding import PartitionSpec as P

HEAD = 64
bf16 = jnp.bfloat16
f32 = jnp.float32

half_root = 0.7071067811865476
gauss_factor = 0.3989422804014327


EXCHANGES = {"xu": ("x", 4, 1), "xv": ("x", 4, 3), "zu": ("z", 4, 1), "zv": ("z", 4, 3), "c": ("core", 2, 1)}
BLOCK_BITS = ("zv", "zu", "xv", "xu")
BIT_MASK = {"xu": 1, "xv": 3, "zu": 4, "zv": 12}
ORDERS = (
    ("xu", "xv", "zu", "zv"),
    ("xv", "xu", "zv", "zu"),
    ("zu", "zv", "xu", "xv"),
    ("zv", "zu", "xv", "xu"),
)
MASKS = np.zeros(16, np.int32)
for _index in range(16):
    for _place, _bit in enumerate(BLOCK_BITS):
        if (_index >> (3 - _place)) & 1:
            MASKS[_index] ^= BIT_MASK[_bit]
ATTN_COLS = (384, 384, 384, 512)


def block_place(part, index):
    place = 0
    for step in range(4):
        if (index >> step) & 1:
            place += 8 >> BLOCK_BITS.index(ORDERS[part][step])
    return place


def dot(left_side, right_side):
    return lax.dot_general(left_side, right_side, (((1,), (0,)), ((), ())), preferred_element_type=f32)


def dot_rows(left_side, right_side):
    return lax.dot_general(left_side, right_side, (((0,), (0,)), ((), ())), preferred_element_type=f32)


def dot_cols(left_side, right_side):
    return lax.dot_general(left_side, right_side, (((1,), (1,)), ((), ())), preferred_element_type=f32)


def norm_parts(values):
    center = values - jnp.mean(values, -1, keepdims=True)
    rescale = lax.rsqrt(jnp.mean(center * center, -1, keepdims=True) + 1e-05)
    return center * rescale, rescale


def norm_backward(grad_rows, normed, rescale, norm_gain):
    scaled = grad_rows * norm_gain
    inner = (
        scaled
        - jnp.mean(scaled, -1, keepdims=True)
        - normed * jnp.mean(scaled * normed, -1, keepdims=True)
    )
    return rescale * inner


def put_blocks(out_ref, part, slot, value):
    value = value.astype(bf16)
    for index in range(16):
        place = 48 * block_place(part, index)
        rows = value[place : place + 48]
        if slot is None:
            out_ref[index] = rows
        else:
            out_ref[slot, index] = rows


def attention_forward_kernel(
    length_ref, x_ref, own_ref, peer_ref, own_out_ref, peer_out_ref, vec_ref,
    middle_ref, heads_ref, soft_ref, mixed_ref,
):
    length = length_ref[0]
    normed, _ = norm_parts(x_ref[...].astype(f32))
    normed_b = (normed * vec_ref[2:3] + vec_ref[3:4]).astype(bf16)
    for j in range(3):
        for half, weight_ref in enumerate((own_ref, peer_ref)):
            cols = slice(384 * half, 384 * half + 384)
            rows = dot(normed_b, weight_ref[j])
            if j != 1:
                rows = rows + vec_ref[6 + j // 2 : 7 + j // 2, cols]
            heads_ref[j, :, cols] = rows.astype(bf16)
    count = x_ref.shape[0]
    live_keys = lax.broadcasted_iota(jnp.int32, (count, count), 1) < length
    for pair in range(6):
        both = []
        for head in (2 * pair, 2 * pair + 1):
            cols = slice(HEAD * head, HEAD * head + HEAD)
            scores = dot_cols(heads_ref[0, :, cols], heads_ref[1, :, cols]) * HEAD ** (-0.5)
            scores = jnp.where(live_keys, scores, -1e30)
            powers = jnp.exp(scores - jnp.max(scores, -1, keepdims=True))
            soft = powers / jnp.sum(powers, -1, keepdims=True)
            soft_ref[head] = soft
            both.append(dot(soft.astype(bf16), heads_ref[2, :, cols]))
        mixed_ref[:, 128 * pair : 128 * pair + 128] = jnp.concatenate(both, 1).astype(bf16)
    total = dot_cols(mixed_ref[:, :384], own_out_ref[:, :384])
    total = total + dot_cols(mixed_ref[:, 384:], peer_out_ref[:, :384])
    middle_ref[...] = x_ref[...].astype(f32) + total + vec_ref[0:1]


def units_forward_kernel(middle_ref, own_ref, peer_ref, vec_ref, up_bias_ref, result_ref, active_ref, slope_ref):
    middle = middle_ref[...]
    normed, _ = norm_parts(middle)
    normed_b = (normed * vec_ref[4:5] + vec_ref[5:6]).astype(bf16)
    total = middle + vec_ref[1:2]
    for half, weight_ref in enumerate((own_ref, peer_ref)):
        for j in range(2):
            cols = slice(768 * (2 * half + j), 768 * (2 * half + j) + 768)
            pre_active = dot(normed_b, weight_ref[j]) + up_bias_ref[0:1, cols]
            below = 0.5 * (1.0 + lax.erf(pre_active * half_root))
            active_b = (pre_active * below).astype(bf16)
            active_ref[:, cols] = active_b
            slope_ref[:, cols] = below + pre_active * jnp.exp(-0.5 * pre_active * pre_active) * gauss_factor
            total = total + dot_cols(active_b, weight_ref[2 + j])
    result_ref[...] = total.astype(bf16)


def units_backward_kernel(
    grad_ref, middle_ref, active_ref, slope_ref, own_ref, peer_ref, vec_ref,
    grad_middle_ref, grad_own_ref, grad_peer_ref, vec_grad_ref, up_bias_grad_ref,
):
    grad_b = grad_ref[...]
    grad_rows = grad_b.astype(f32)
    normed, rescale = norm_parts(middle_ref[...])
    normed_b = (normed * vec_ref[4:5] + vec_ref[5:6]).astype(bf16)
    normed_t = normed_b.T
    grad_t = grad_b.T
    grad_normed = None
    for half, weight_ref, out_ref in ((1, peer_ref, grad_peer_ref), (0, own_ref, grad_own_ref)):
        for j in range(2):
            cols = slice(768 * (2 * half + j), 768 * (2 * half + j) + 768)
            put_blocks(out_ref, 2 + j, 2 + j, dot(grad_t, active_ref[:, cols]))
            grad_upper = (dot(grad_b, weight_ref[2 + j]) * slope_ref[:, cols]).astype(bf16)
            up_bias_grad_ref[0:1, cols] = jnp.sum(grad_upper.astype(f32), 0, keepdims=True)
            put_blocks(out_ref, j, j, dot(normed_t, grad_upper))
            term = dot_cols(grad_upper, weight_ref[j])
            grad_normed = term if grad_normed is None else grad_normed + term
    grad_middle = grad_rows + norm_backward(grad_normed, normed, rescale, vec_ref[4:5])
    grad_middle_ref[...] = grad_middle
    vec_grad_ref[...] = jnp.zeros_like(vec_grad_ref)
    vec_grad_ref[0:1] = jnp.sum(grad_middle, 0, keepdims=True)
    vec_grad_ref[1:2] = jnp.sum(grad_rows, 0, keepdims=True)
    vec_grad_ref[4:5] = jnp.sum(grad_normed * normed, 0, keepdims=True)
    vec_grad_ref[5:6] = jnp.sum(grad_normed, 0, keepdims=True)


def attention_backward_kernel(
    grad_ref, x_ref, heads_ref, soft_ref, mixed_ref, own_ref, peer_ref, own_out_ref, peer_out_ref, vec_ref,
    grad_in_ref, grad_own_ref, grad_peer_ref, grad_own_out_ref, grad_peer_out_ref, vec_grad_ref,
    grad_mixed_ref, grad_heads_ref,
):
    grad_b = grad_ref[...].astype(bf16)
    grad_t = grad_b.T
    put_blocks(grad_peer_out_ref, 3, None, dot(grad_t, mixed_ref[:, 384:]))
    put_blocks(grad_own_out_ref, 3, None, dot(grad_t, mixed_ref[:, :384]))
    grad_mixed_ref[:, :384] = dot(grad_b, own_out_ref[:, :384]).astype(bf16)
    grad_mixed_ref[:, 384:] = dot(grad_b, peer_out_ref[:, :384]).astype(bf16)
    factor = HEAD ** (-0.5)
    for pair in range(6):
        found = ([], [], [])
        for head in (2 * pair, 2 * pair + 1):
            cols = slice(HEAD * head, HEAD * head + HEAD)
            soft = soft_ref[head]
            grad_head = grad_mixed_ref[:, cols]
            grad_soft = dot_cols(grad_head, heads_ref[2, :, cols])
            inner = jnp.sum(grad_soft * soft, -1, keepdims=True)
            grad_scores = (soft * (grad_soft - inner)).astype(bf16)
            found[0].append(dot(grad_scores, heads_ref[1, :, cols]) * factor)
            found[1].append(dot_rows(grad_scores, heads_ref[0, :, cols]) * factor)
            found[2].append(dot_rows(soft.astype(bf16), grad_head))
        for j in range(3):
            grad_heads_ref[j, :, 128 * pair : 128 * pair + 128] = jnp.concatenate(found[j], 1).astype(bf16)
    normed, rescale = norm_parts(x_ref[...].astype(f32))
    normed_b = (normed * vec_ref[2:3] + vec_ref[3:4]).astype(bf16)
    normed_t = normed_b.T
    grad_normed = None
    for half, weight_ref, out_ref in ((1, peer_ref, grad_peer_ref), (0, own_ref, grad_own_ref)):
        for j in range(3):
            rows = grad_heads_ref[j, :, 384 * half : 384 * half + 384]
            put_blocks(out_ref, j, j, dot(normed_t, rows))
            term = dot_cols(rows, weight_ref[j])
            grad_normed = term if grad_normed is None else grad_normed + term
    grad_in = grad_ref[...] + norm_backward(grad_normed, normed, rescale, vec_ref[2:3])
    grad_in_ref[...] = grad_in.astype(bf16)
    vec_grad_ref[...] = jnp.zeros_like(vec_grad_ref)
    vec_grad_ref[2:3] = jnp.sum(grad_normed * normed, 0, keepdims=True)
    vec_grad_ref[3:4] = jnp.sum(grad_normed, 0, keepdims=True)
    vec_grad_ref[6:7] = jnp.sum(grad_heads_ref[0].astype(f32), 0, keepdims=True)
    vec_grad_ref[7:8] = jnp.sum(grad_heads_ref[2].astype(f32), 0, keepdims=True)


def kernel_call(kernel, name, inputs, outputs, flops, scratch=(), scalar=False):
    whole = pl.BlockSpec(memory_space=pltpu.VMEM)
    specs = [whole] * len(inputs)
    if scalar:
        specs[0] = pl.BlockSpec(memory_space=pltpu.SMEM)
    shapes = [jax.ShapeDtypeStruct(shape, dtype) for shape, dtype in outputs]
    moved = sum(int(np.prod(a.shape)) * a.dtype.itemsize for a in list(inputs) + shapes)
    return pl.pallas_call(
        kernel,
        name=name,
        out_shape=shapes,
        in_specs=specs,
        out_specs=[whole] * len(shapes),
        scratch_shapes=list(scratch),
        cost_estimate=pl.CostEstimate(flops=flops, bytes_accessed=moved, transcendentals=0),
        compiler_params=pltpu.CompilerParams(vmem_limit_bytes=52 * 2**20),
    )(*inputs)


ROWS = (192, 768)
HEADS_SHAPE = (3, 192, 768)
UNITS_SHAPE = (4, 16, 48, 768)
ATTN_SHAPE = (3, 16, 48, 384)


def attention_forward(length, x, attn, vec):
    own, peer, own_out, peer_out = attn
    return kernel_call(
        attention_forward_kernel, "attention_forward",
        [length, x, own, peer, own_out, peer_out, vec],
        [(ROWS, f32), (HEADS_SHAPE, bf16), ((12, 192, 192), f32), (ROWS, bf16)],
        1_100_000_000, scalar=True,
    )


def units_forward(middle, units, vec, up_bias):
    own, peer = units
    return kernel_call(
        units_forward_kernel, "units_forward", [middle, own, peer, vec, up_bias],
        [(ROWS, bf16), ((192, 3072), bf16), ((192, 3072), f32)], 1_800_000_000,
    )


def units_backward(grad_b, middle, active, slope, units, vec):
    own, peer = units
    return kernel_call(
        units_backward_kernel, "units_backward", [grad_b, middle, active, slope, own, peer, vec],
        [(ROWS, f32), (UNITS_SHAPE, bf16), (UNITS_SHAPE, bf16), ((8, 768), f32), ((1, 3072), f32)], 3_600_000_000,
    )


def attention_backward(grad_middle, x, heads, soft, mixed, attn, vec):
    own, peer, own_out, peer_out = attn
    return kernel_call(
        attention_backward_kernel, "attention_backward",
        [grad_middle, x, heads, soft, mixed, own, peer, own_out, peer_out, vec],
        [(ROWS, bf16), (ATTN_SHAPE, bf16), (ATTN_SHAPE, bf16), (ATTN_SHAPE[1:], bf16), (ATTN_SHAPE[1:], bf16), ((8, 768), f32)],
        2_300_000_000,
        scratch=[pltpu.VMEM(ROWS, bf16), pltpu.VMEM(HEADS_SHAPE, bf16)],
    )


def exchange(value, bit):
    axis, size, flip = EXCHANGES[bit]
    return lax.ppermute(value, axis, [(i, i ^ flip) for i in range(size)])


def exchange_pipe(value):
    return lax.ppermute(value, "pipe", [(0, 1), (1, 0)])


def exchange_both(value):
    return lax.ppermute(value, ("pipe", "tensor"), [(i, i ^ 3) for i in range(4)])


def exchange_tensor(value):
    return lax.ppermute(value, "tensor", [(0, 1), (1, 0)])


def pin(*values):
    return lax.optimization_barrier(values)


def assemble_kernel(count, *refs):
    held, got, outs = refs[:4], refs[4:8], refs[8:]
    for part in range(4):
        for index in range(16):
            rows = (held if index < 8 else got)[part][index % 8]
            place = slice(48 * block_place(part, index), 48 * block_place(part, index) + 48)
            if part < count:
                outs[0][part, place] = rows
            else:
                outs[1][place] = rows


def assemble(held, got):
    cols = [part.shape[-1] for part in held]
    if cols[0] == cols[3]:
        shapes = [(4, 768, cols[0])]
    else:
        shapes = [(3, 768, cols[0]), (768, cols[3])]
    kernel = functools.partial(assemble_kernel, shapes[0][0])
    return kernel_call(kernel, "assemble", [*held, *got], [(shape, bf16) for shape in shapes], 0)


def gather_start(own):
    tensor = lax.axis_index("tensor")
    rows = lax.all_to_all(jnp.stack(own * 4), ("pipe", "tensor", "core"), 0, 0, tiled=True)
    rows = rows.reshape(2, 2, 48, 2368)
    a = jnp.where(tensor == 0, rows[:, 0], rows[:, 1])
    b = jnp.where(tensor == 0, rows[:, 1], rows[:, 0])
    parts = [
        [a[..., :192], b[..., :192], a[..., 832:1600]],
        [a[..., 192:384], b[..., 192:384], b[..., 832:1600]],
        [a[..., 384:576], b[..., 384:576], a[..., 1600:]],
        [a[..., 576:768], b[..., 576:768], a[..., 768:832], b[..., 768:832], b[..., 1600:]],
    ]
    parts = [jnp.concatenate(part, -1)[:, None] for part in parts]
    for step in range(2):
        got = [exchange(part, ORDERS[i][step]) for i, part in enumerate(parts)]
        parts = [jnp.concatenate([x, y], 1) for x, y in zip(parts, got)]
    return parts, [exchange(part, ORDERS[i][2]) for i, part in enumerate(parts)]


def gather_group(parts, got, layer, units):
    out = []
    for i in range(4):
        cols = slice(ATTN_COLS[i], None) if units else slice(ATTN_COLS[i])
        out.append(jnp.concatenate([parts[i][layer, :, :, cols], got[i][layer, :, :, cols]], 0))
    return out


def gather_fourth(held):
    return [exchange(part, ORDERS[i][3]) for i, part in enumerate(held)]


def gather_core(held, got):
    own = assemble(held, got)
    return own, [exchange(array, "c") for array in own]


def fold_kernel(outputs, *refs):
    count = len(outputs)
    pairs, outs = refs[: -2 * count], refs[-2 * count :]
    for number, places in enumerate(outputs):
        for pair, index, layer, start in places:
            x, y = pairs[2 * pair], pairs[2 * pair + 1]
            for side in range(2):
                total = (x[(*index, side, 0)].astype(f32) + y[(*index, side, 0)].astype(f32)).astype(bf16)
                out = outs[number + count * side]
                cols = slice(start, start + total.shape[-1])
                if layer is None:
                    out[0, :, cols] = total
                else:
                    out[layer, 0, :, cols] = total


def fold(pairs, outputs, layers, name):
    arrays, specs = [], []
    for pair in pairs:
        for array in pair:
            lead, (n, rows, cols) = array.shape[:-3], array.shape[-3:]
            n //= 2
            arrays.append(array.reshape(*lead, 2, n, rows, cols))
            zeros = (0,) * (len(lead) + 1)
            specs.append(pl.BlockSpec((*lead, 2, 1, rows, cols), lambda b, zeros=zeros: (*zeros, b, 0, 0)))
    shapes, out_specs = [], []
    for places in outputs:
        width = max(start + pairs[pair][0].shape[-1] for pair, _, _, start in places)
        lead = () if layers is None else (layers,)
        zeros = (0,) * len(lead)
        shapes.append(jax.ShapeDtypeStruct((*lead, n, 48, width), bf16))
        out_specs.append(pl.BlockSpec((*lead, 1, 48, width), lambda b, zeros=zeros: (*zeros, b, 0, 0)))
    moved = sum(2 * int(np.prod(a.shape)) for a in arrays + shapes * 2)
    out = pl.pallas_call(
        functools.partial(fold_kernel, outputs),
        name=name,
        grid=(n,),
        out_shape=shapes * 2,
        in_specs=specs,
        out_specs=out_specs * 2,
        cost_estimate=pl.CostEstimate(flops=moved // 4, bytes_accessed=moved, transcendentals=0),
        compiler_params=pltpu.CompilerParams(vmem_limit_bytes=52 * 2**20),
    )(*arrays)
    return out[: len(outputs)], out[len(outputs) :]


def send_parts(parts, step):
    return [exchange(part, ORDERS[i][step]) for i, part in enumerate(parts)]


def send_core(arrays):
    return [exchange(array, "c") for array in arrays]


def fold_attention(own, got, name):
    pairs = list(zip(own, got))
    return fold(pairs, [[(0, (i,), None, 0)] for i in range(3)] + [[(1, (), None, 0)]], None, name)


def fold_units(own, got, name):
    return fold([(own, got)], [[(0, (i,), None, 0)] for i in range(4)], None, name)


def fold_layer(attn_own, attn_got, units_own, units_got, name):
    pairs = list(zip(attn_own, attn_got)) + [(units_own, units_got)]
    outputs = [[(min(i // 3, 1), (i,) if i < 3 else (), None, 0), (2, (i,), None, ATTN_COLS[i])] for i in range(4)]
    return fold(pairs, outputs, None, name)


def fold_both(attn, units, second):
    pairs = []
    outputs = []
    for i in range(4):
        pairs += [(attn[0][i], attn[1][i]), (units[0][i], units[1][i]), (second[0][i], second[1][i])]
        outputs.append([(3 * i, (), 0, 0), (3 * i + 1, (), 0, ATTN_COLS[i]), (3 * i + 2, (), 1, 0)])
    return fold(pairs, outputs, 2, "fold_both")


def fold_on(kept, got, name):
    pairs = list(zip(kept, got))
    return fold(pairs, [[(i, (layer,), layer, 0) for layer in range(2)] for i in range(4)], 2, name)


def scatter_end(kept, got):
    tensor = lax.axis_index("tensor")
    p = [x[:, 0].astype(f32) + y[:, 0].astype(f32) for x, y in zip(kept, got)]
    mine = [p[0][..., :192], p[1][..., :192], p[2][..., :192], p[3][..., :192], p[3][..., 384:448]]
    mine = jnp.concatenate(mine + [p[0][..., 384:], p[2][..., 384:]], -1).astype(bf16)
    theirs = [p[0][..., 192:384], p[1][..., 192:384], p[2][..., 192:384], p[3][..., 192:384], p[3][..., 448:512]]
    theirs = jnp.concatenate(theirs + [p[1][..., 384:], p[3][..., 512:]], -1).astype(bf16)
    a = jnp.where(tensor == 0, mine, theirs)
    b = jnp.where(tensor == 0, theirs, mine)
    rows = jnp.stack([a, b], 1).reshape(8, 24, 2368)
    rows = lax.all_to_all(rows, ("pipe", "tensor", "core"), 0, 0, tiled=True)
    rows = jnp.sum(rows.reshape(4, 2, 24, 2368).astype(f32), 0)
    return rows[0], rows[1]


def share_outputs(first_rows, second_rows):
    pipe, tensor = lax.axis_index("pipe"), lax.axis_index("tensor")
    keep = jnp.where(pipe == 0, first_rows, second_rows)
    send = jnp.where(pipe == 0, second_rows, first_rows)
    return keep, exchange_tensor(keep), exchange_pipe(send), exchange_both(send)


def order_outputs(rows):
    pipe, tensor = lax.axis_index("pipe"), lax.axis_index("tensor")
    a, b, c, d = rows
    a, b = jnp.where(tensor == 0, a, b), jnp.where(tensor == 0, b, a)
    c, d = jnp.where(tensor == 0, c, d), jnp.where(tensor == 0, d, c)
    a, c = jnp.where(pipe == 0, a, c), jnp.where(pipe == 0, c, a)
    b, d = jnp.where(pipe == 0, b, d), jnp.where(pipe == 0, d, b)
    return jnp.stack([a, b, c, d])[None]


def pack_share(w_query, w_key, w_value, w_out, w_up, w_down, b_query, b_value, b_up, vectors):
    cols = jnp.pad(jnp.stack(vectors, 1), ((0, 0), (0, 2)))
    out = []
    for half in range(2):
        third, sixth, whole = (slice(n * half, n * half + n) for n in (3, 12, 192))
        rows = jnp.concatenate([b_query[:, third], b_value[:, third], b_up[:, sixth]], 1)
        small = jnp.concatenate([cols, jnp.pad(rows, ((0, 22), (0, 38)))], 1)
        wide = slice(768 * half, 768 * half + 768)
        out.append(
            jnp.concatenate(
                [w_query[:, whole], w_key[:, whole], w_value[:, whole], w_out[:, whole], small, w_up[:, wide], w_down[:, wide]],
                1,
            )
        )
    return out


def unpack_share(halves):
    def cols(start, stop):
        return jnp.concatenate([half[:, start:stop] for half in halves], 1)

    grads = [cols(192 * i, 192 * i + 192) for i in range(4)] + [cols(832, 1600), cols(1600, 2368)]
    rows = [half[:2, 776:794] for half in halves]
    bias = [jnp.concatenate([row[:, lo:hi] for row in rows], 1) for lo, hi in ((0, 3), (3, 6), (6, 18))]
    return grads, bias, [halves[0][:, 768 + i] for i in range(6)]


def spread_small(own_out, peer_out, place_units):
    vectors = own_out[:, 384:390].astype(f32).T
    rows = jnp.concatenate([own_out[:, 384:], peer_out[:, 384:]], 1).reshape(32, 24, 4, 64)[:, :2, :, 8:26]
    rows = dot(place_units, rows.reshape(64, 72)).reshape(64, 4, 18).transpose(1, 2, 0)
    b_query, b_value = rows[:, :3].reshape(1, 768), rows[:, 3:6].reshape(1, 768)
    return jnp.concatenate([vectors, b_query, b_value]), rows[:, 6:].reshape(1, 3072)


def gather_small(vec_grad, up_bias_grad, place_units):
    rows = jnp.concatenate(
        [vec_grad[6].reshape(4, 3, HEAD), vec_grad[7].reshape(4, 3, HEAD), up_bias_grad.reshape(4, 12, HEAD)], 1
    )
    rows = rows.transpose(2, 0, 1).reshape(HEAD, 72).astype(bf16)
    rows = dot_rows(place_units, rows).astype(bf16).reshape(32, 2, 4, 18)
    rows = jnp.pad(rows, ((0, 0), (0, 22), (0, 0), (8, 38))).reshape(768, 256)
    cols = jnp.pad(vec_grad[:6].T.astype(bf16), ((0, 0), (0, 58)))
    small = rows + jnp.concatenate([cols] * 4, 1)
    small = small.reshape(2, 2, 2, 2, 48, 256)
    axes = [BLOCK_BITS.index(bit) for bit in reversed(ORDERS[3])]
    small = small.transpose(*axes, 4, 5).reshape(16, 48, 256)
    return small[..., :128], small[..., 128:]


def local(clip_frames, out_cotangent, clip_lengths, *params):
    params = [param[0] for param in params]
    w_query, w_key, w_value, w_out, w_up, w_down, b_query, b_value, b_out, b_up, b_down = params[:11]
    micro = lax.axis_index("pipe") * 2 + lax.axis_index("tensor")
    chip = lax.axis_index("z") * 4 + lax.axis_index("x")

    blocks = (chip ^ jnp.asarray(MASKS))[:, None]
    rows_at = (blocks * 48 + jnp.arange(48)[None]).reshape(-1)
    place_rows = (jnp.arange(768)[:, None] == rows_at[None]).astype(bf16)
    units_at = (blocks * 4 + jnp.arange(4)[None]).reshape(-1)
    place_units = (jnp.arange(64)[:, None] == units_at[None]).astype(bf16)

    own = pack_share(
        w_query, w_key, w_value, w_out, w_up, w_down, b_query, b_value, b_up, [b_out, b_down] + params[11:]
    )
    parts, third = gather_start(own)
    held = [gather_group(parts, third, i // 2, i % 2) for i in range(4)]

    frames = lax.dynamic_index_in_dim(clip_frames, micro, 0, keepdims=False)
    cotangent = lax.dynamic_index_in_dim(out_cotangent, micro, 0, keepdims=False)
    length = lax.dynamic_index_in_dim(clip_lengths, micro, 0, keepdims=False)
    x_first = dot(frames, place_rows).astype(bf16)
    grad_out = dot(cotangent, place_rows).astype(bf16)

    def placed_back(rows):
        return dot_cols(rows, place_rows).astype(bf16)

    def attn_of(own, peer):
        return own[0], peer[0], own[1], peer[1]

    got = [gather_fourth(held[0]), gather_fourth(held[1])]
    attn_first = attn_of(*gather_core(held[0], got[0]))
    vec_first, up_bias_first = spread_small(attn_first[2], attn_first[3], place_units)
    middle_first, heads_first, soft_first, mixed_first = attention_forward(length, x_first, attn_first, vec_first)
    units_first = [array[0] for array in gather_core(held[1], got[1])]
    got.append(gather_fourth(held[2]))
    middle_first, got[2] = pin(middle_first, got[2])
    x_second, active_first, slope_first = units_forward(middle_first, units_first, vec_first, up_bias_first)
    attn_second = attn_of(*gather_core(held[2], got[2]))
    got.append(gather_fourth(held[3]))
    x_second, got[3] = pin(x_second, got[3])
    vec_second, up_bias_second = spread_small(attn_second[2], attn_second[3], place_units)
    middle_second, heads_second, soft_second, mixed_second = attention_forward(length, x_second, attn_second, vec_second)
    units_second = [array[0] for array in gather_core(held[3], got[3])]
    out_second, active_second, slope_second = units_forward(middle_second, units_second, vec_second, up_bias_second)
    shared = share_outputs(placed_back(x_second), placed_back(out_second))

    grad_middle, units_own, units_peer, vec_grad_units, up_bias_grad = units_backward(
        grad_out, middle_second, active_second, slope_second, units_second, vec_second
    )
    units_got = exchange(units_peer, "c")
    second_grad, attn_own, attn_peer, out_own, out_peer, vec_grad = attention_backward(
        grad_middle, x_second, heads_second, soft_second, mixed_second, attn_second, vec_second
    )
    small_own, small_peer = gather_small(vec_grad_units + vec_grad, up_bias_grad, place_units)
    out_own = jnp.concatenate([out_own, small_own], -1)
    out_peer = jnp.concatenate([out_peer, small_peer], -1)
    attn_got = send_core([attn_peer, out_peer])
    second_grad, units_got, shared = pin(second_grad, units_got, shared)
    section_output = order_outputs(shared)
    second_kept, second_sent = fold_layer([attn_own, out_own], attn_got, units_own, units_got, "fold_second")
    second_grad, second_kept, second_sent = pin(second_grad, second_kept, second_sent)
    second_got = send_parts(second_sent, 3)

    grad_middle, units_own, units_peer, vec_grad_units, up_bias_grad = units_backward(
        second_grad, middle_first, active_first, slope_first, units_first, vec_first
    )
    units_got = exchange(units_peer, "c")
    first_grad, attn_own, attn_peer, out_own, out_peer, vec_grad = attention_backward(
        grad_middle, x_first, heads_first, soft_first, mixed_first, attn_first, vec_first
    )
    attn_own, attn_peer, units_got, second_got = pin(attn_own, attn_peer, units_got, second_got)
    units_kept, units_sent = fold_units(units_own, units_got, "fold_units")
    units_got = send_parts(units_sent, 3)
    small_own, small_peer = gather_small(vec_grad_units + vec_grad, up_bias_grad, place_units)
    out_own = jnp.concatenate([out_own, small_own], -1)
    out_peer = jnp.concatenate([out_peer, small_peer], -1)
    attn_got = send_core([attn_peer, out_peer])
    attn_kept, attn_sent = fold_attention([attn_own, out_own], attn_got, "fold_attention")
    attn_got = send_parts(attn_sent, 3)
    input_grad = order_outputs(share_outputs(placed_back(first_grad), placed_back(second_grad)))

    kept, sent = fold_both((attn_kept, attn_got), (units_kept, units_got), (second_kept, second_got))
    kept, sent = fold_on(kept, send_parts(sent, 2), "fold_four")
    kept, sent = fold_on(kept, send_parts(sent, 1), "fold_two")
    halves = scatter_end(kept, send_parts(sent, 0))
    grads, bias, vectors = unpack_share(halves)
    grads = grads + [bias[0], bias[1], vectors[0], bias[2]] + vectors[1:]
    return (section_output, input_grad) + tuple(grad[None] for grad in grads)


def solution(mesh):
    fine = Mesh(mesh.devices.reshape(2, 4, 4, 2, 2), ("pipe", "z", "x", "core", "tensor"))
    shard = ("z", "x", "core")
    rows = P(None, shard, None)
    matrix = P("pipe", shard, "tensor")
    vector = P("pipe", shard)
    params = (matrix,) * 8 + (vector, matrix) + (vector,) * 5
    return jax.shard_map(
        local,
        mesh=fine,
        in_specs=(rows, rows, P(None, shard)) + params,
        out_specs=(P("pipe", None, shard, None),) * 2 + params,
        check_vma=False,
    )
```

```python
import functools

import jax
import jax.numpy as jnp
import numpy as np
from jax import lax
from jax.experimental import pallas as pl
from jax.experimental.pallas import tpu as pltpu
from jax.sharding import Mesh
from jax.sharding import PartitionSpec as P

HEAD = 64
bf16 = jnp.bfloat16
f32 = jnp.float32

half_root = 0.7071067811865476
gauss_factor = 0.3989422804014327


EXCHANGES = {"xu": ("x", 4, 1), "xv": ("x", 4, 3), "zu": ("z", 4, 1), "zv": ("z", 4, 3), "c": ("core", 2, 1)}
BLOCK_BITS = ("zv", "zu", "xv", "xu")
BIT_MASK = {"xu": 1, "xv": 3, "zu": 4, "zv": 12}
ORDERS = (
    ("xu", "xv", "zu", "zv"),
    ("xv", "xu", "zv", "zu"),
    ("zu", "zv", "xu", "xv"),
    ("zv", "zu", "xv", "xu"),
)
MASKS = np.zeros(16, np.int32)
for _index in range(16):
    for _place, _bit in enumerate(BLOCK_BITS):
        if (_index >> (3 - _place)) & 1:
            MASKS[_index] ^= BIT_MASK[_bit]
ATTN_COLS = (384, 384, 384, 512)


def block_place(part, index):
    place = 0
    for step in range(4):
        if (index >> step) & 1:
            place += 8 >> BLOCK_BITS.index(ORDERS[part][step])
    return place


def dot(left_side, right_side):
    return lax.dot_general(left_side, right_side, (((1,), (0,)), ((), ())), preferred_element_type=f32)


def dot_rows(left_side, right_side):
    return lax.dot_general(left_side, right_side, (((0,), (0,)), ((), ())), preferred_element_type=f32)


def dot_cols(left_side, right_side):
    return lax.dot_general(left_side, right_side, (((1,), (1,)), ((), ())), preferred_element_type=f32)


def norm_parts(values):
    center = values - jnp.mean(values, -1, keepdims=True)
    rescale = lax.rsqrt(jnp.mean(center * center, -1, keepdims=True) + 1e-05)
    return center * rescale, rescale


def norm_backward(grad_rows, normed, rescale, norm_gain):
    scaled = grad_rows * norm_gain
    inner = (
        scaled
        - jnp.mean(scaled, -1, keepdims=True)
        - normed * jnp.mean(scaled * normed, -1, keepdims=True)
    )
    return rescale * inner


def put_blocks(out_ref, part, slot, value):
    value = value.astype(bf16)
    for index in range(16):
        place = 48 * block_place(part, index)
        rows = value[place : place + 48]
        if slot is None:
            out_ref[index] = rows
        else:
            out_ref[slot, index] = rows


def attention_forward_kernel(
    length_ref, x_ref, own_ref, peer_ref, own_out_ref, peer_out_ref, place_ref,
    middle_ref, heads_ref, soft_ref, mixed_ref, vec_ref, up_bias_ref,
):
    length = length_ref[0]
    vec_ref[0:6] = own_out_ref[:, 384:].astype(f32).T[0:6]
    units = []
    for out_ref in (own_out_ref, peer_out_ref):
        rows = dot(place_ref[...], out_ref[:, 384:]).T
        units += [rows[:64], rows[64:]]
    for row, first in ((6, 8), (7, 11)):
        pieces = [rows[first + i : first + i + 1] for rows in units for i in range(3)]
        vec_ref[row : row + 1] = jnp.concatenate(pieces, 1)
    pieces = [rows[14 + i : 15 + i] for rows in units for i in range(12)]
    for i in range(24):
        up_bias_ref[0:1, 128 * i : 128 * i + 128] = jnp.concatenate(pieces[2 * i : 2 * i + 2], 1)
    normed, _ = norm_parts(x_ref[...].astype(f32))
    normed_b = (normed * vec_ref[2:3] + vec_ref[3:4]).astype(bf16)
    for j in range(3):
        for half, weight_ref in enumerate((own_ref, peer_ref)):
            cols = slice(384 * half, 384 * half + 384)
            rows = dot(normed_b, weight_ref[j])
            if j != 1:
                rows = rows + vec_ref[6 + j // 2 : 7 + j // 2, cols]
            heads_ref[j, :, cols] = rows.astype(bf16)
    count = x_ref.shape[0]
    live_keys = lax.broadcasted_iota(jnp.int32, (count, count), 1) < length
    for pair in range(6):
        both = []
        for head in (2 * pair, 2 * pair + 1):
            cols = slice(HEAD * head, HEAD * head + HEAD)
            scores = dot_cols(heads_ref[0, :, cols], heads_ref[1, :, cols]) * HEAD ** (-0.5)
            scores = jnp.where(live_keys, scores, -1e30)
            powers = jnp.exp(scores - jnp.max(scores, -1, keepdims=True))
            soft = powers / jnp.sum(powers, -1, keepdims=True)
            soft_ref[head] = soft
            both.append(dot(soft.astype(bf16), heads_ref[2, :, cols]))
        mixed_ref[:, 128 * pair : 128 * pair + 128] = jnp.concatenate(both, 1).astype(bf16)
    total = dot_cols(mixed_ref[:, :384], own_out_ref[:, :384])
    total = total + dot_cols(mixed_ref[:, 384:], peer_out_ref[:, :384])
    middle_ref[...] = x_ref[...].astype(f32) + total + vec_ref[0:1]


def units_forward_kernel(middle_ref, own_ref, peer_ref, vec_ref, up_bias_ref, result_ref, active_ref, slope_ref):
    middle = middle_ref[...]
    normed, _ = norm_parts(middle)
    normed_b = (normed * vec_ref[4:5] + vec_ref[5:6]).astype(bf16)
    total = middle + vec_ref[1:2]
    for half, weight_ref in enumerate((own_ref, peer_ref)):
        for j in range(2):
            cols = slice(768 * (2 * half + j), 768 * (2 * half + j) + 768)
            pre_active = dot(normed_b, weight_ref[j]) + up_bias_ref[0:1, cols]
            below = 0.5 * (1.0 + lax.erf(pre_active * half_root))
            active_b = (pre_active * below).astype(bf16)
            active_ref[:, cols] = active_b
            slope_ref[:, cols] = below + pre_active * jnp.exp(-0.5 * pre_active * pre_active) * gauss_factor
            total = total + dot_cols(active_b, weight_ref[2 + j])
    result_ref[...] = total.astype(bf16)


def units_backward_kernel(
    grad_ref, middle_ref, active_ref, slope_ref, own_ref, peer_ref, vec_ref,
    grad_middle_ref, grad_own_ref, grad_peer_ref, vec_grad_ref, up_bias_grad_ref,
):
    grad_b = grad_ref[...]
    grad_rows = grad_b.astype(f32)
    normed, rescale = norm_parts(middle_ref[...])
    normed_b = (normed * vec_ref[4:5] + vec_ref[5:6]).astype(bf16)
    normed_t = normed_b.T
    grad_t = grad_b.T
    grad_normed = None
    for half, weight_ref, out_ref in ((1, peer_ref, grad_peer_ref), (0, own_ref, grad_own_ref)):
        for j in range(2):
            cols = slice(768 * (2 * half + j), 768 * (2 * half + j) + 768)
            put_blocks(out_ref, 2 + j, 2 + j, dot(grad_t, active_ref[:, cols]))
            grad_upper = (dot(grad_b, weight_ref[2 + j]) * slope_ref[:, cols]).astype(bf16)
            up_bias_grad_ref[0:1, cols] = jnp.sum(grad_upper.astype(f32), 0, keepdims=True)
            put_blocks(out_ref, j, j, dot(normed_t, grad_upper))
            term = dot_cols(grad_upper, weight_ref[j])
            grad_normed = term if grad_normed is None else grad_normed + term
    grad_middle = grad_rows + norm_backward(grad_normed, normed, rescale, vec_ref[4:5])
    grad_middle_ref[...] = grad_middle
    vec_grad_ref[...] = jnp.zeros_like(vec_grad_ref)
    vec_grad_ref[0:1] = jnp.sum(grad_middle, 0, keepdims=True)
    vec_grad_ref[1:2] = jnp.sum(grad_rows, 0, keepdims=True)
    vec_grad_ref[4:5] = jnp.sum(grad_normed * normed, 0, keepdims=True)
    vec_grad_ref[5:6] = jnp.sum(grad_normed, 0, keepdims=True)


def attention_backward_kernel(
    grad_ref, x_ref, heads_ref, soft_ref, mixed_ref, own_ref, peer_ref, own_out_ref, peer_out_ref, vec_ref,
    units_vec_ref, up_bias_grad_ref, place_ref,
    grad_in_ref, grad_own_ref, grad_peer_ref, grad_own_out_ref, grad_peer_out_ref,
    grad_mixed_ref, grad_heads_ref, cols_ref, small_ref,
):
    grad_b = grad_ref[...].astype(bf16)
    grad_t = grad_b.T
    grad_mixed_ref[:, :384] = dot(grad_b, own_out_ref[:, :384]).astype(bf16)
    grad_mixed_ref[:, 384:] = dot(grad_b, peer_out_ref[:, :384]).astype(bf16)
    factor = HEAD ** (-0.5)
    for pair in range(6):
        found = ([], [], [])
        for head in (2 * pair, 2 * pair + 1):
            cols = slice(HEAD * head, HEAD * head + HEAD)
            soft = soft_ref[head]
            grad_head = grad_mixed_ref[:, cols]
            grad_soft = dot_cols(grad_head, heads_ref[2, :, cols])
            inner = jnp.sum(grad_soft * soft, -1, keepdims=True)
            grad_scores = (soft * (grad_soft - inner)).astype(bf16)
            found[0].append(dot(grad_scores, heads_ref[1, :, cols]) * factor)
            found[1].append(dot_rows(grad_scores, heads_ref[0, :, cols]) * factor)
            found[2].append(dot_rows(soft.astype(bf16), grad_head))
        for j in range(3):
            grad_heads_ref[j, :, 128 * pair : 128 * pair + 128] = jnp.concatenate(found[j], 1).astype(bf16)
    normed, rescale = norm_parts(x_ref[...].astype(f32))
    normed_b = (normed * vec_ref[2:3] + vec_ref[3:4]).astype(bf16)
    normed_t = normed_b.T
    grad_normed = None
    for half, weight_ref, out_ref in ((1, peer_ref, grad_peer_ref), (0, own_ref, grad_own_ref)):
        for j in range(3):
            rows = grad_heads_ref[j, :, 384 * half : 384 * half + 384]
            put_blocks(out_ref, j, j, dot(normed_t, rows))
            term = dot_cols(rows, weight_ref[j])
            grad_normed = term if grad_normed is None else grad_normed + term
    grad_in = grad_ref[...] + norm_backward(grad_normed, normed, rescale, vec_ref[2:3])
    grad_in_ref[...] = grad_in.astype(bf16)
    cols_ref[...] = jnp.zeros_like(cols_ref)
    cols_ref[0:2] = units_vec_ref[0:2]
    cols_ref[2:3] = jnp.sum(grad_normed * normed, 0, keepdims=True)
    cols_ref[3:4] = jnp.sum(grad_normed, 0, keepdims=True)
    cols_ref[4:6] = units_vec_ref[4:6]
    cols_ref[64:70] = cols_ref[0:6]
    cols = cols_ref[...].T
    query_bias = jnp.sum(grad_heads_ref[0].astype(f32), 0, keepdims=True)
    value_bias = jnp.sum(grad_heads_ref[2].astype(f32), 0, keepdims=True)
    for half, out_ref in ((1, grad_peer_out_ref), (0, grad_own_out_ref)):
        small_ref[...] = jnp.zeros_like(small_ref)
        for t in range(2):
            base = 64 * t
            for i in range(3):
                at = HEAD * (6 * half + 3 * t + i)
                small_ref[base + 8 + i : base + 9 + i] = query_bias[:, at : at + HEAD]
                small_ref[base + 11 + i : base + 12 + i] = value_bias[:, at : at + HEAD]
            for i in range(12):
                at = HEAD * (24 * half + 12 * t + i)
                small_ref[base + 14 + i : base + 15 + i] = up_bias_grad_ref[0:1, at : at + HEAD]
        small = dot_cols(place_ref[...], small_ref[...].astype(bf16)) + cols
        weight = dot(grad_t, mixed_ref[:, 384 * half : 384 * half + 384])
        put_blocks(out_ref, 3, None, jnp.concatenate([weight, small], 1))


def kernel_call(kernel, name, inputs, outputs, scratch=(), scalar=False):
    whole = pl.BlockSpec(memory_space=pltpu.VMEM)
    specs = [whole] * len(inputs)
    if scalar:
        specs[0] = pl.BlockSpec(memory_space=pltpu.SMEM)
    shapes = [jax.ShapeDtypeStruct(shape, dtype) for shape, dtype in outputs]
    return pl.pallas_call(
        kernel,
        name=name,
        out_shape=shapes,
        in_specs=specs,
        out_specs=[whole] * len(shapes),
        scratch_shapes=list(scratch),
        cost_estimate=pl.CostEstimate(flops=1, bytes_accessed=1, transcendentals=0),
        compiler_params=pltpu.CompilerParams(vmem_limit_bytes=52 * 2**20),
    )(*inputs)


ROWS = (192, 768)
HEADS_SHAPE = (3, 192, 768)
UNITS_SHAPE = (4, 16, 48, 768)
ATTN_SHAPE = (3, 16, 48, 384)
OUT_SHAPE = (16, 48, 512)


def attention_forward(length, x, attn, place_units):
    own, peer, own_out, peer_out = attn
    return kernel_call(
        attention_forward_kernel, "attention_forward",
        [length, x, own, peer, own_out, peer_out, place_units],
        [(ROWS, f32), (HEADS_SHAPE, bf16), ((12, 192, 192), f32), (ROWS, bf16), ((8, 768), f32), ((1, 3072), f32)],
        scalar=True,
    )


def units_forward(middle, units, vec, up_bias):
    own, peer = units
    return kernel_call(
        units_forward_kernel, "units_forward", [middle, own, peer, vec, up_bias],
        [(ROWS, bf16), ((192, 3072), bf16), ((192, 3072), f32)],
    )


def units_backward(grad_b, middle, active, slope, units, vec):
    own, peer = units
    return kernel_call(
        units_backward_kernel, "units_backward", [grad_b, middle, active, slope, own, peer, vec],
        [(ROWS, f32), (UNITS_SHAPE, bf16), (UNITS_SHAPE, bf16), ((8, 768), f32), ((1, 3072), f32)],
    )


def attention_backward(grad_middle, x, heads, soft, mixed, attn, vec, units_vec, up_bias_grad, place_units):
    own, peer, own_out, peer_out = attn
    return kernel_call(
        attention_backward_kernel, "attention_backward",
        [grad_middle, x, heads, soft, mixed, own, peer, own_out, peer_out, vec, units_vec, up_bias_grad, place_units],
        [(ROWS, bf16), (ATTN_SHAPE, bf16), (ATTN_SHAPE, bf16), (OUT_SHAPE, bf16), (OUT_SHAPE, bf16)],
        scratch=[pltpu.VMEM(ROWS, bf16), pltpu.VMEM(HEADS_SHAPE, bf16), pltpu.VMEM((128, 768), f32), pltpu.VMEM((128, 64), f32)],
    )


def exchange(value, bit):
    axis, size, flip = EXCHANGES[bit]
    return lax.ppermute(value, axis, [(i, i ^ flip) for i in range(size)])


def exchange_pipe(value):
    return lax.ppermute(value, "pipe", [(0, 1), (1, 0)])


def exchange_both(value):
    return lax.ppermute(value, ("pipe", "tensor"), [(i, i ^ 3) for i in range(4)])


def exchange_tensor(value):
    return lax.ppermute(value, "tensor", [(0, 1), (1, 0)])


def pin(*values):
    return lax.optimization_barrier(values)


def assemble_kernel(count, *refs):
    held, got, outs = refs[:4], refs[4:8], refs[8:]
    for part in range(4):
        for index in range(16):
            rows = (held if index < 8 else got)[part][index % 8]
            place = slice(48 * block_place(part, index), 48 * block_place(part, index) + 48)
            if part < count:
                outs[0][part, place] = rows
            else:
                outs[1][place] = rows


def assemble(held, got):
    cols = [part.shape[-1] for part in held]
    if cols[0] == cols[3]:
        shapes = [(4, 768, cols[0])]
    else:
        shapes = [(3, 768, cols[0]), (768, cols[3])]
    kernel = functools.partial(assemble_kernel, shapes[0][0])
    return kernel_call(kernel, "assemble", [*held, *got], [(shape, bf16) for shape in shapes])


def pack_kernel(*refs):
    w_query, w_key, w_value, w_out, w_up, w_down, b_query, b_value = refs[:8]
    b_up = refs[9]
    vectors = [refs[8], *refs[10:15]]
    out_ref, vec_ref, small_ref = refs[15:]
    vec_ref[...] = jnp.zeros_like(vec_ref)
    for i, vector in enumerate(vectors):
        vec_ref[i : i + 1, 0:24] = vector[...].astype(f32)
    cols = vec_ref[...].T[0:24, 0:8]
    for half in range(2):
        small_ref[...] = jnp.zeros_like(small_ref)
        small_ref[:, 0:8] = cols
        small_ref[0:2, 8:11] = b_query[0, :, 3 * half : 3 * half + 3].astype(f32)
        small_ref[0:2, 11:14] = b_value[0, :, 3 * half : 3 * half + 3].astype(f32)
        small_ref[0:2, 14:26] = b_up[0, :, 12 * half : 12 * half + 12].astype(f32)
        small = small_ref[...].astype(bf16)
        wide, whole = slice(768 * half, 768 * half + 768), slice(192 * half, 192 * half + 192)
        first = jnp.concatenate([w_query[0, :, whole].astype(f32), w_key[0, :, whole].astype(f32)], 1).astype(bf16)
        second = jnp.concatenate([w_value[0, :, whole].astype(f32), w_out[0, :, whole].astype(f32)], 1).astype(bf16)
        for k in range(4):
            out = out_ref.at[2 * k + half]
            out[:, 0:768] = w_up[0, :, wide]
            out[:, 768:1536] = w_down[0, :, wide]
            out[:, 1536:1920] = first
            out[:, 1920:2304] = second
            out[:, 2304:2368] = small


def gather_start(params):
    tensor = lax.axis_index("tensor")
    rows = kernel_call(
        pack_kernel, "pack", list(params), [((8, 24, 2368), bf16)],
        scratch=[pltpu.VMEM((8, 128), f32), pltpu.VMEM((24, 64), f32)],
    )[0]
    rows = lax.all_to_all(rows, ("pipe", "tensor", "core"), 0, 0, tiled=True)
    rows = rows.reshape(2, 2, 48, 2368)
    a = jnp.where(tensor == 0, rows[:, 0], rows[:, 1])
    b = jnp.where(tensor == 0, rows[:, 1], rows[:, 0])
    parts = [
        [a[..., 1536:1728], b[..., 1536:1728], a[..., :768]],
        [a[..., 1728:1920], b[..., 1728:1920], b[..., :768]],
        [a[..., 1920:2112], b[..., 1920:2112], a[..., 768:1536]],
        [a[..., 2112:2304], b[..., 2112:2304], a[..., 2304:], b[..., 2304:], b[..., 768:1536]],
    ]
    parts = [jnp.concatenate(part, -1)[:, None] for part in parts]
    for step in range(2):
        got = [exchange(part, ORDERS[i][step]) for i, part in enumerate(parts)]
        parts = [jnp.concatenate([x, y], 1) for x, y in zip(parts, got)]
    return parts, [exchange(part, ORDERS[i][2]) for i, part in enumerate(parts)]


def gather_group(parts, got, layer, units):
    out = []
    for i in range(4):
        cols = slice(ATTN_COLS[i], None) if units else slice(ATTN_COLS[i])
        out.append(jnp.concatenate([parts[i][layer, :, :, cols], got[i][layer, :, :, cols]], 0))
    return out


def gather_fourth(held):
    return [exchange(part, ORDERS[i][3]) for i, part in enumerate(held)]


def gather_core(held, got):
    own = assemble(held, got)
    return own, [exchange(array, "c") for array in own]


def fold_kernel(outputs, *refs):
    pairs, outs = refs[: -len(outputs)], refs[-len(outputs) :]
    for out, places in zip(outs, outputs):
        for pair, index, layer, start in places:
            x, y = pairs[2 * pair], pairs[2 * pair + 1]
            total = (x[(*index, 0, 0)].astype(f32) + y[(*index, 0, 0)].astype(f32)).astype(bf16)
            cols = slice(start, start + total.shape[-1])
            if layer is None:
                out[0, :, cols] = total
            else:
                out[layer, 0, :, cols] = total


def fold_side(pairs, outputs, layers, name, side):
    arrays, specs = [], []
    for pair in pairs:
        for array in pair:
            lead, (n, rows, cols) = array.shape[:-3], array.shape[-3:]
            n //= 2
            arrays.append(array.reshape(*lead, 2, n, rows, cols))
            zeros = (0,) * len(lead)
            specs.append(pl.BlockSpec((*lead, 1, 1, rows, cols), lambda b, zeros=zeros: (*zeros, side, b, 0, 0)))
    shapes, out_specs = [], []
    for places in outputs:
        width = max(start + pairs[pair][0].shape[-1] for pair, _, _, start in places)
        lead = () if layers is None else (layers,)
        zeros = (0,) * len(lead)
        shapes.append(jax.ShapeDtypeStruct((*lead, n, 48, width), bf16))
        out_specs.append(pl.BlockSpec((*lead, 1, 48, width), lambda b, zeros=zeros: (*zeros, b, 0, 0)))
    return pl.pallas_call(
        functools.partial(fold_kernel, outputs),
        name=name + ("_kept", "_sent")[side],
        grid=(n,),
        out_shape=shapes,
        in_specs=specs,
        out_specs=out_specs,
        cost_estimate=pl.CostEstimate(flops=1, bytes_accessed=1, transcendentals=0),
        compiler_params=pltpu.CompilerParams(vmem_limit_bytes=52 * 2**20),
    )(*arrays)


def fold(pairs, outputs, layers, name):
    sent = fold_side(pairs, outputs, layers, name, 1)
    return fold_side(pairs, outputs, layers, name, 0), sent


def send_parts(parts, step):
    return [exchange(part, ORDERS[i][step]) for i, part in enumerate(parts)]


def send_core(arrays):
    return [exchange(array, "c") for array in arrays]


def fold_attention(own, got, name):
    pairs = list(zip(own, got))
    return fold(pairs, [[(0, (i,), None, 0)] for i in range(3)] + [[(1, (), None, 0)]], None, name)


def fold_units(own, got, name):
    return fold([(own, got)], [[(0, (i,), None, 0)] for i in range(4)], None, name)


def fold_both(attn, units, attn_second, units_second):
    pairs = []
    outputs = []
    for i in range(4):
        pairs += [(group[0][i], group[1][i]) for group in (attn, units, attn_second, units_second)]
        outputs.append([(4 * i + k, (), k // 2, ATTN_COLS[i] * (k % 2)) for k in range(4)])
    return fold(pairs, outputs, 2, "fold_both")


def fold_on(kept, got, name):
    pairs = list(zip(kept, got))
    return fold(pairs, [[(i, (layer,), layer, 0) for layer in range(2)] for i in range(4)], 2, name)


def collect_kernel(tensor_ref, *refs):
    kept, got, out_ref = refs[:4], refs[4:8], refs[8]
    for layer in range(2):
        p = [x[layer, 0].astype(f32) + y[layer, 0].astype(f32) for x, y in zip(kept, got)]
        for t in range(2):
            at = slice(192 * t, 192 * t + 192)
            values = [
                (0, p[t][:, 384:]),
                (768, p[2][:, 384:] if t == 0 else p[3][:, 512:]),
                (1536, jnp.concatenate([p[0][:, at], p[1][:, at]], 1)),
                (1920, jnp.concatenate([p[2][:, at], p[3][:, at]], 1)),
                (2304, p[3][:, 384 + 64 * t : 448 + 64 * t]),
            ]
            place = 4 * layer + 2 * (t ^ tensor_ref[0])
            for core in range(2):
                out = out_ref.at[place + core]
                for start, value in values:
                    out[:, start : start + value.shape[1]] = value[24 * core : 24 * core + 24].astype(bf16)


def finish_kernel(rows_ref, *refs):
    g_query, g_key, g_value, g_out, g_up, g_down, gb_query, gb_value = refs[:8]
    gb_up = refs[9]
    vectors = [refs[8], *refs[10:15]]
    small_ref = refs[15]
    halves = []
    for core in range(2):
        total = rows_ref[core].astype(f32)
        for k in range(1, 4):
            total = total + rows_ref[2 * k + core].astype(f32)
        halves.append(total)
        g_up[0, :, 768 * core : 768 * core + 768] = total[:, 0:768]
        g_down[0, :, 768 * core : 768 * core + 768] = total[:, 768:1536]
    for i, out in enumerate((g_query, g_key, g_value, g_out)):
        start = 1536 + 192 * i
        out[0] = jnp.concatenate([half[:, start : start + 192] for half in halves], 1)
    for out, lo, hi in ((gb_query, 8, 11), (gb_value, 11, 14), (gb_up, 14, 26)):
        out[0] = jnp.concatenate([half[0:2, 2304 + lo : 2304 + hi] for half in halves], 1)
    small_ref[...] = jnp.zeros_like(small_ref)
    small_ref[0:24, 0:64] = halves[0][:, 2304:2368]
    cols = small_ref[...].T
    for i, out in enumerate(vectors):
        out[...] = cols[i : i + 1, 0:24]


def scatter_end(kept, got):
    tensor = lax.axis_index("tensor").astype(jnp.int32).reshape(1)
    rows = kernel_call(collect_kernel, "collect", [tensor, *kept, *got], [((8, 24, 2368), bf16)], scalar=True)[0]
    rows = lax.all_to_all(rows, ("pipe", "tensor", "core"), 0, 0, tiled=True)
    shapes = [(1, 24, 384)] * 4 + [(1, 24, 1536)] * 2 + [(1, 2, 6)] * 2 + [(1, 24), (1, 2, 24)] + [(1, 24)] * 5
    return kernel_call(
        finish_kernel, "finish", [rows], [(shape, f32) for shape in shapes], scratch=[pltpu.VMEM((128, 128), f32)]
    )


def share_outputs(first_rows, second_rows):
    pipe, tensor = lax.axis_index("pipe"), lax.axis_index("tensor")
    keep = jnp.where(pipe == 0, first_rows, second_rows)
    send = jnp.where(pipe == 0, second_rows, first_rows)
    return keep, exchange_tensor(keep), exchange_pipe(send), exchange_both(send)


def order_outputs(rows):
    pipe, tensor = lax.axis_index("pipe"), lax.axis_index("tensor")
    a, b, c, d = rows
    a, b = jnp.where(tensor == 0, a, b), jnp.where(tensor == 0, b, a)
    c, d = jnp.where(tensor == 0, c, d), jnp.where(tensor == 0, d, c)
    a, c = jnp.where(pipe == 0, a, c), jnp.where(pipe == 0, c, a)
    b, d = jnp.where(pipe == 0, b, d), jnp.where(pipe == 0, d, b)
    return jnp.stack([a, b, c, d])[None]


def local(clip_frames, out_cotangent, clip_lengths, *params):
    micro = lax.axis_index("pipe") * 2 + lax.axis_index("tensor")
    chip = lax.axis_index("z") * 4 + lax.axis_index("x")

    parts, third = gather_start(params)
    held = [gather_group(parts, third, i // 2, i % 2) for i in range(4)]

    blocks = (chip ^ jnp.asarray(MASKS))[:, None]
    rows_at = (blocks * 48 + jnp.arange(48)[None]).reshape(-1)
    place_rows = (jnp.arange(768)[:, None] == rows_at[None]).astype(bf16)
    within = np.arange(48)
    units_at = np.where(within % 24 < 2, within // 24 * 2 + within % 24, 1000)
    units_at = (blocks * 4 + jnp.asarray(units_at)[None]).reshape(-1)
    place_units = (jnp.arange(64)[:, None] == units_at[None]).astype(bf16)
    place_back = (units_at[:, None] == jnp.arange(64)[None]).astype(bf16)

    frames = lax.dynamic_index_in_dim(clip_frames, micro, 0, keepdims=False)
    cotangent = lax.dynamic_index_in_dim(out_cotangent, micro, 0, keepdims=False)
    length = lax.dynamic_index_in_dim(clip_lengths, micro, 0, keepdims=False)
    x_first = dot(frames, place_rows).astype(bf16)
    grad_out = dot(cotangent, place_rows).astype(bf16)

    def placed_back(rows):
        return dot_cols(rows, place_rows).astype(bf16)

    def attn_of(own, peer):
        return own[0], peer[0], own[1], peer[1]

    got = [gather_fourth(held[0]), gather_fourth(held[1])]
    attn_first = attn_of(*gather_core(held[0], got[0]))
    middle_first, heads_first, soft_first, mixed_first, vec_first, up_bias_first = attention_forward(
        length, x_first, attn_first, place_units
    )
    units_first = [array[0] for array in gather_core(held[1], got[1])]
    got.append(gather_fourth(held[2]))
    middle_first, got[2] = pin(middle_first, got[2])
    x_second, active_first, slope_first = units_forward(middle_first, units_first, vec_first, up_bias_first)
    attn_second = attn_of(*gather_core(held[2], got[2]))
    got.append(gather_fourth(held[3]))
    x_second, got[3] = pin(x_second, got[3])
    middle_second, heads_second, soft_second, mixed_second, vec_second, up_bias_second = attention_forward(
        length, x_second, attn_second, place_units
    )
    units_second = [array[0] for array in gather_core(held[3], got[3])]
    out_second, active_second, slope_second = units_forward(middle_second, units_second, vec_second, up_bias_second)
    shared = share_outputs(placed_back(x_second), placed_back(out_second))

    grad_middle, units_own, units_peer, units_vec, up_bias_grad = units_backward(
        grad_out, middle_second, active_second, slope_second, units_second, vec_second
    )
    units_got = exchange(units_peer, "c")
    attn = attention_backward(
        grad_middle, x_second, heads_second, soft_second, mixed_second, attn_second, vec_second, units_vec,
        up_bias_grad, place_back,
    )
    attn, units_got = pin(attn, units_got)
    second_grad, attn_own, attn_peer, out_own, out_peer = attn
    units_kept_second, sent = fold_units(units_own, units_got, "fold_units")
    units_got_second = send_parts(sent, 3)
    attn_got = send_core([attn_peer, out_peer])

    units = units_backward(second_grad, middle_first, active_first, slope_first, units_first, vec_first)
    units, attn_got, units_got_second, shared = pin(units, attn_got, units_got_second, shared)
    section_output = order_outputs(shared)
    grad_middle, units_own, units_peer, units_vec, up_bias_grad = units
    attn_kept_second, sent = fold_attention([attn_own, out_own], attn_got, "fold_attention")
    attn_got_second = send_parts(sent, 3)
    units_got = exchange(units_peer, "c")

    attn = attention_backward(
        grad_middle, x_first, heads_first, soft_first, mixed_first, attn_first, vec_first, units_vec,
        up_bias_grad, place_back,
    )
    attn, units_got, attn_got_second = pin(attn, units_got, attn_got_second)
    first_grad, attn_own, attn_peer, out_own, out_peer = attn
    units_kept, sent = fold_units(units_own, units_got, "fold_units")
    units_got = send_parts(sent, 3)
    attn_got = send_core([attn_peer, out_peer])
    attn_kept, sent = fold_attention([attn_own, out_own], attn_got, "fold_attention")
    attn_got = send_parts(sent, 3)
    input_grad = order_outputs(share_outputs(placed_back(first_grad), placed_back(second_grad)))

    kept, sent = fold_both(
        (attn_kept, attn_got), (units_kept, units_got),
        (attn_kept_second, attn_got_second), (units_kept_second, units_got_second),
    )
    kept, sent = fold_on(kept, send_parts(sent, 2), "fold_four")
    kept, sent = fold_on(kept, send_parts(sent, 1), "fold_two")
    return (section_output, input_grad, *scatter_end(kept, send_parts(sent, 0)))


def solution(mesh):
    fine = Mesh(mesh.devices.reshape(2, 4, 4, 2, 2), ("pipe", "z", "x", "core", "tensor"))
    shard = ("z", "x", "core")
    rows = P(None, shard, None)
    matrix = P("pipe", shard, "tensor")
    vector = P("pipe", shard)
    params = (matrix,) * 8 + (vector, matrix) + (vector,) * 5
    return jax.shard_map(
        local,
        mesh=fine,
        in_specs=(rows, rows, P(None, shard)) + params,
        out_specs=(P("pipe", None, shard, None),) * 2 + params,
        check_vma=False,
    )
```

```python
import functools

import jax
import jax.numpy as jnp
import numpy as np
from jax import lax
from jax.experimental import pallas as pl
from jax.experimental.pallas import tpu as pltpu
from jax.sharding import Mesh
from jax.sharding import PartitionSpec as P

HEAD = 64
bf16 = jnp.bfloat16
f32 = jnp.float32

half_root = 0.7071067811865476
gauss_factor = 0.3989422804014327


EXCHANGES = {"xu": ("x", 4, 1), "xv": ("x", 4, 3), "zu": ("z", 4, 1), "zv": ("z", 4, 3), "c": ("core", 2, 1)}
BLOCK_BITS = ("zv", "zu", "xv", "xu")
BIT_MASK = {"xu": 1, "xv": 3, "zu": 4, "zv": 12}
ORDERS = (
    ("xu", "xv", "zu", "zv"),
    ("xv", "xu", "zv", "zu"),
    ("zu", "zv", "xu", "xv"),
    ("zv", "zu", "xv", "xu"),
)
MASKS = np.zeros(16, np.int32)
for _index in range(16):
    for _place, _bit in enumerate(BLOCK_BITS):
        if (_index >> (3 - _place)) & 1:
            MASKS[_index] ^= BIT_MASK[_bit]
ATTN_COLS = (384, 384, 384, 512)


def block_place(part, index):
    place = 0
    for step in range(4):
        if (index >> step) & 1:
            place += 8 >> BLOCK_BITS.index(ORDERS[part][step])
    return place


def dot(left_side, right_side):
    return lax.dot_general(left_side, right_side, (((1,), (0,)), ((), ())), preferred_element_type=f32)


def dot_rows(left_side, right_side):
    return lax.dot_general(left_side, right_side, (((0,), (0,)), ((), ())), preferred_element_type=f32)


def dot_cols(left_side, right_side):
    return lax.dot_general(left_side, right_side, (((1,), (1,)), ((), ())), preferred_element_type=f32)


def norm_parts(values):
    center = values - jnp.mean(values, -1, keepdims=True)
    rescale = lax.rsqrt(jnp.mean(center * center, -1, keepdims=True) + 1e-05)
    return center * rescale, rescale


def norm_backward(grad_rows, normed, rescale, norm_gain):
    scaled = grad_rows * norm_gain
    inner = (
        scaled
        - jnp.mean(scaled, -1, keepdims=True)
        - normed * jnp.mean(scaled * normed, -1, keepdims=True)
    )
    return rescale * inner


def put_blocks(out_ref, part, slot, value):
    value = value.astype(bf16)
    for index in range(16):
        place = 48 * block_place(part, index)
        out_ref[slot, index] = value[place : place + 48]


def put_columns(out_ref, part, start, value):
    value = value.astype(bf16)
    for index in range(16):
        place = 48 * block_place(part, index)
        out_ref[index, :, start : start + value.shape[1]] = value[place : place + 48]


def attention_forward_kernel(
    length_ref, x_ref, own_ref, peer_ref, place_ref,
    middle_ref, heads_ref, soft_ref, mixed_ref, vec_ref, up_bias_ref,
):
    length = length_ref[0]
    vec_ref[0:6] = own_ref[:, 1536:].astype(f32).T[0:6]
    units = []
    for weight_ref in (own_ref, peer_ref):
        rows = dot(place_ref[...], weight_ref[:, 1536:]).T
        units += [rows[:64], rows[64:]]
    for row, first in ((6, 8), (7, 11)):
        pieces = [rows[first + i : first + i + 1] for rows in units for i in range(3)]
        vec_ref[row : row + 1] = jnp.concatenate(pieces, 1)
    pieces = [rows[14 + i : 15 + i] for rows in units for i in range(12)]
    for i in range(24):
        up_bias_ref[0:1, 128 * i : 128 * i + 128] = jnp.concatenate(pieces[2 * i : 2 * i + 2], 1)
    normed, _ = norm_parts(x_ref[...].astype(f32))
    normed_b = (normed * vec_ref[2:3] + vec_ref[3:4]).astype(bf16)
    for j in range(3):
        for half, weight_ref in enumerate((own_ref, peer_ref)):
            cols = slice(384 * half, 384 * half + 384)
            rows = dot(normed_b, weight_ref[:, 384 * j : 384 * j + 384])
            if j != 1:
                rows = rows + vec_ref[6 + j // 2 : 7 + j // 2, cols]
            heads_ref[j, :, cols] = rows.astype(bf16)
    count = x_ref.shape[0]
    live_keys = lax.broadcasted_iota(jnp.int32, (count, count), 1) < length
    for pair in range(6):
        both = []
        for head in (2 * pair, 2 * pair + 1):
            cols = slice(HEAD * head, HEAD * head + HEAD)
            scores = dot_cols(heads_ref[0, :, cols], heads_ref[1, :, cols]) * HEAD ** (-0.5)
            scores = jnp.where(live_keys, scores, -1e30)
            powers = jnp.exp(scores - jnp.max(scores, -1, keepdims=True))
            soft = powers / jnp.sum(powers, -1, keepdims=True)
            soft_ref[head] = soft
            both.append(dot(soft.astype(bf16), heads_ref[2, :, cols]))
        mixed_ref[:, 128 * pair : 128 * pair + 128] = jnp.concatenate(both, 1).astype(bf16)
    total = dot_cols(mixed_ref[:, :384], own_ref[:, 1152:1536])
    total = total + dot_cols(mixed_ref[:, 384:], peer_ref[:, 1152:1536])
    middle_ref[...] = x_ref[...].astype(f32) + total + vec_ref[0:1]


def units_forward_kernel(middle_ref, own_ref, peer_ref, vec_ref, up_bias_ref, result_ref, active_ref, slope_ref):
    middle = middle_ref[...]
    normed, _ = norm_parts(middle)
    normed_b = (normed * vec_ref[4:5] + vec_ref[5:6]).astype(bf16)
    total = middle + vec_ref[1:2]
    for half, weight_ref in enumerate((own_ref, peer_ref)):
        for j in range(2):
            cols = slice(768 * (2 * half + j), 768 * (2 * half + j) + 768)
            pre_active = dot(normed_b, weight_ref[j]) + up_bias_ref[0:1, cols]
            below = 0.5 * (1.0 + lax.erf(pre_active * half_root))
            active_b = (pre_active * below).astype(bf16)
            active_ref[:, cols] = active_b
            slope_ref[:, cols] = below + pre_active * jnp.exp(-0.5 * pre_active * pre_active) * gauss_factor
            total = total + dot_cols(active_b, weight_ref[2 + j])
    result_ref[...] = total.astype(bf16)


def units_backward_kernel(
    grad_ref, middle_ref, active_ref, slope_ref, own_ref, peer_ref, vec_ref,
    grad_middle_ref, grad_own_ref, grad_peer_ref, vec_grad_ref, up_bias_grad_ref,
):
    grad_b = grad_ref[...]
    grad_rows = grad_b.astype(f32)
    normed, rescale = norm_parts(middle_ref[...])
    normed_b = (normed * vec_ref[4:5] + vec_ref[5:6]).astype(bf16)
    normed_t = normed_b.T
    grad_t = grad_b.T
    grad_normed = None
    for half, weight_ref, out_ref in ((1, peer_ref, grad_peer_ref), (0, own_ref, grad_own_ref)):
        for j in range(2):
            cols = slice(768 * (2 * half + j), 768 * (2 * half + j) + 768)
            put_blocks(out_ref, 2 + j, 2 + j, dot(grad_t, active_ref[:, cols]))
            grad_upper = (dot(grad_b, weight_ref[2 + j]) * slope_ref[:, cols]).astype(bf16)
            up_bias_grad_ref[0:1, cols] = jnp.sum(grad_upper.astype(f32), 0, keepdims=True)
            put_blocks(out_ref, j, j, dot(normed_t, grad_upper))
            term = dot_cols(grad_upper, weight_ref[j])
            grad_normed = term if grad_normed is None else grad_normed + term
    grad_middle = grad_rows + norm_backward(grad_normed, normed, rescale, vec_ref[4:5])
    grad_middle_ref[...] = grad_middle
    vec_grad_ref[...] = jnp.zeros_like(vec_grad_ref)
    vec_grad_ref[0:1] = jnp.sum(grad_middle, 0, keepdims=True)
    vec_grad_ref[1:2] = jnp.sum(grad_rows, 0, keepdims=True)
    vec_grad_ref[4:5] = jnp.sum(grad_normed * normed, 0, keepdims=True)
    vec_grad_ref[5:6] = jnp.sum(grad_normed, 0, keepdims=True)


def attention_backward_kernel(
    grad_ref, x_ref, heads_ref, soft_ref, mixed_ref, own_ref, peer_ref, vec_ref,
    units_vec_ref, up_bias_grad_ref, place_ref,
    grad_in_ref, grad_own_ref, grad_peer_ref,
    grad_mixed_ref, grad_heads_ref, cols_ref, small_ref,
):
    grad_b = grad_ref[...].astype(bf16)
    grad_t = grad_b.T
    grad_mixed_ref[:, :384] = dot(grad_b, own_ref[:, 1152:1536]).astype(bf16)
    grad_mixed_ref[:, 384:] = dot(grad_b, peer_ref[:, 1152:1536]).astype(bf16)
    factor = HEAD ** (-0.5)
    for pair in range(6):
        found = ([], [], [])
        for head in (2 * pair, 2 * pair + 1):
            cols = slice(HEAD * head, HEAD * head + HEAD)
            soft = soft_ref[head]
            grad_head = grad_mixed_ref[:, cols]
            grad_soft = dot_cols(grad_head, heads_ref[2, :, cols])
            inner = jnp.sum(grad_soft * soft, -1, keepdims=True)
            grad_scores = (soft * (grad_soft - inner)).astype(bf16)
            found[0].append(dot(grad_scores, heads_ref[1, :, cols]) * factor)
            found[1].append(dot_rows(grad_scores, heads_ref[0, :, cols]) * factor)
            found[2].append(dot_rows(soft.astype(bf16), grad_head))
        for j in range(3):
            grad_heads_ref[j, :, 128 * pair : 128 * pair + 128] = jnp.concatenate(found[j], 1).astype(bf16)
    normed, rescale = norm_parts(x_ref[...].astype(f32))
    normed_b = (normed * vec_ref[2:3] + vec_ref[3:4]).astype(bf16)
    normed_t = normed_b.T
    grad_normed = None
    for half, weight_ref, out_ref in ((1, peer_ref, grad_peer_ref), (0, own_ref, grad_own_ref)):
        for j in range(3):
            rows = grad_heads_ref[j, :, 384 * half : 384 * half + 384]
            put_columns(out_ref, j, 384 * j, dot(normed_t, rows))
            term = dot_cols(rows, weight_ref[:, 384 * j : 384 * j + 384])
            grad_normed = term if grad_normed is None else grad_normed + term
    grad_in = grad_ref[...] + norm_backward(grad_normed, normed, rescale, vec_ref[2:3])
    grad_in_ref[...] = grad_in.astype(bf16)
    cols_ref[...] = jnp.zeros_like(cols_ref)
    cols_ref[0:2] = units_vec_ref[0:2]
    cols_ref[2:3] = jnp.sum(grad_normed * normed, 0, keepdims=True)
    cols_ref[3:4] = jnp.sum(grad_normed, 0, keepdims=True)
    cols_ref[4:6] = units_vec_ref[4:6]
    cols_ref[64:70] = cols_ref[0:6]
    cols = cols_ref[...].T
    query_bias = jnp.sum(grad_heads_ref[0].astype(f32), 0, keepdims=True)
    value_bias = jnp.sum(grad_heads_ref[2].astype(f32), 0, keepdims=True)
    for half, out_ref in ((1, grad_peer_ref), (0, grad_own_ref)):
        small_ref[...] = jnp.zeros_like(small_ref)
        for t in range(2):
            base = 64 * t
            for i in range(3):
                at = HEAD * (6 * half + 3 * t + i)
                small_ref[base + 8 + i : base + 9 + i] = query_bias[:, at : at + HEAD]
                small_ref[base + 11 + i : base + 12 + i] = value_bias[:, at : at + HEAD]
            for i in range(12):
                at = HEAD * (24 * half + 12 * t + i)
                small_ref[base + 14 + i : base + 15 + i] = up_bias_grad_ref[0:1, at : at + HEAD]
        small = dot_cols(place_ref[...], small_ref[...].astype(bf16)) + cols
        weight = dot(grad_t, mixed_ref[:, 384 * half : 384 * half + 384])
        put_columns(out_ref, 3, 1152, jnp.concatenate([weight, small], 1))


def kernel_call(kernel, name, inputs, outputs, scratch=(), scalar=False, blocks=None):
    whole = pl.BlockSpec(memory_space=pltpu.VMEM)
    specs = [whole] * len(inputs)
    out_specs = [whole] * len(outputs)
    if blocks is not None:
        specs = [pl.BlockSpec(shape, lambda i, at=at: at) for shape, at in blocks]
        out_specs = [pl.BlockSpec(shape, lambda i, n=len(shape): (0,) * n) for shape, _ in outputs]
    if scalar:
        specs[0] = pl.BlockSpec(memory_space=pltpu.SMEM)
    shapes = [jax.ShapeDtypeStruct(shape, dtype) for shape, dtype in outputs]
    return pl.pallas_call(
        kernel,
        name=name,
        out_shape=shapes,
        in_specs=specs,
        out_specs=out_specs,
        grid=() if blocks is None else (1,),
        scratch_shapes=list(scratch),
        cost_estimate=pl.CostEstimate(flops=1, bytes_accessed=1, transcendentals=0),
        compiler_params=pltpu.CompilerParams(vmem_limit_bytes=52 * 2**20),
    )(*inputs)


ROWS = (192, 768)
HEADS_SHAPE = (3, 192, 768)
UNITS_SHAPE = (4, 16, 48, 768)
ATTN_SHAPE = (16, 48, 1664)


def attention_forward(length, x, attn, place_units):
    own, peer = attn
    return kernel_call(
        attention_forward_kernel, "attention_forward",
        [length, x, own, peer, place_units],
        [(ROWS, f32), (HEADS_SHAPE, bf16), ((12, 192, 192), f32), (ROWS, bf16), ((8, 768), f32), ((1, 3072), f32)],
        scalar=True,
    )


def units_forward(middle, units, vec, up_bias):
    own, peer = units
    return kernel_call(
        units_forward_kernel, "units_forward", [middle, own, peer, vec, up_bias],
        [(ROWS, bf16), ((192, 3072), bf16), ((192, 3072), f32)],
    )


def units_backward(grad_b, middle, active, slope, units, vec):
    own, peer = units
    return kernel_call(
        units_backward_kernel, "units_backward", [grad_b, middle, active, slope, own, peer, vec],
        [(ROWS, f32), (UNITS_SHAPE, bf16), (UNITS_SHAPE, bf16), ((8, 768), f32), ((1, 3072), f32)],
    )


def attention_backward(grad_middle, x, heads, soft, mixed, attn, vec, units_vec, up_bias_grad, place_units):
    own, peer = attn
    return kernel_call(
        attention_backward_kernel, "attention_backward",
        [grad_middle, x, heads, soft, mixed, own, peer, vec, units_vec, up_bias_grad, place_units],
        [(ROWS, bf16), (ATTN_SHAPE, bf16), (ATTN_SHAPE, bf16)],
        scratch=[pltpu.VMEM(ROWS, bf16), pltpu.VMEM(HEADS_SHAPE, bf16), pltpu.VMEM((128, 768), f32), pltpu.VMEM((128, 64), f32)],
    )


def exchange(value, bit):
    axis, size, flip = EXCHANGES[bit]
    return lax.ppermute(value, axis, [(i, i ^ flip) for i in range(size)])


def exchange_pipe(value):
    return lax.ppermute(value, "pipe", [(0, 1), (1, 0)])


def exchange_both(value):
    return lax.ppermute(value, ("pipe", "tensor"), [(i, i ^ 3) for i in range(4)])


def exchange_tensor(value):
    return lax.ppermute(value, "tensor", [(0, 1), (1, 0)])


def pin(*values):
    return lax.optimization_barrier(values)


def assemble_kernel(slots, *refs):
    count = len(slots)
    out = refs[-1]
    for number, (part, slot, start) in enumerate(slots):
        for index in range(16):
            rows = refs[number + (0 if index < 8 else count)][index % 8]
            place = slice(48 * block_place(part, index), 48 * block_place(part, index) + 48)
            cols = slice(start, start + rows.shape[1])
            if slot is None:
                out[place, cols] = rows
            else:
                out[slot, place, cols] = rows


def assemble(held, got, units):
    inputs, blocks, slots = [], [], []
    for part in range(4):
        width = (384, 256)[part // 3] if units else ATTN_COLS[part]
        first = ATTN_COLS[part] // width if units else 0
        for k in range(768 // width if units else 1):
            inputs.append(part)
            blocks.append(((8, 48, width), (0, 0, first + k)))
            slots.append((part, part, width * k) if units else (part, None, 384 * part))
    arrays = [held[part] for part in inputs] + [got[part] for part in inputs]
    shape = (4, 768, 768) if units else (768, 1664)
    kernel = functools.partial(assemble_kernel, slots)
    name = "assemble_units" if units else "assemble_attention"
    return kernel_call(kernel, name, arrays, [(shape, bf16)], blocks=blocks * 2)[0]


def pack_kernel(*refs):
    w_query, w_key, w_value, w_out, w_up, w_down, b_query, b_value = refs[:8]
    b_up = refs[9]
    vectors = [refs[8], *refs[10:15]]
    out_ref, vec_ref, small_ref = refs[15:]
    vec_ref[...] = jnp.zeros_like(vec_ref)
    for i, vector in enumerate(vectors):
        vec_ref[i : i + 1, 0:24] = vector[...].astype(f32)
    cols = vec_ref[...].T[0:24, 0:8]
    for half in range(2):
        small_ref[...] = jnp.zeros_like(small_ref)
        small_ref[:, 0:8] = cols
        small_ref[0:2, 8:11] = b_query[0, :, 3 * half : 3 * half + 3].astype(f32)
        small_ref[0:2, 11:14] = b_value[0, :, 3 * half : 3 * half + 3].astype(f32)
        small_ref[0:2, 14:26] = b_up[0, :, 12 * half : 12 * half + 12].astype(f32)
        small = small_ref[...].astype(bf16)
        wide, whole = slice(768 * half, 768 * half + 768), slice(192 * half, 192 * half + 192)
        first = jnp.concatenate([w_query[0, :, whole].astype(f32), w_key[0, :, whole].astype(f32)], 1).astype(bf16)
        second = jnp.concatenate([w_value[0, :, whole].astype(f32), w_out[0, :, whole].astype(f32)], 1).astype(bf16)
        for k in range(4):
            out = out_ref.at[2 * k + half]
            out[:, 0:768] = w_up[0, :, wide]
            out[:, 768:1536] = w_down[0, :, wide]
            out[:, 1536:1920] = first
            out[:, 1920:2304] = second
            out[:, 2304:2368] = small


def gather_start(params):
    tensor = lax.axis_index("tensor")
    rows = kernel_call(
        pack_kernel, "pack", list(params), [((8, 24, 2368), bf16)],
        scratch=[pltpu.VMEM((8, 128), f32), pltpu.VMEM((24, 64), f32)],
        blocks=[(param.shape, (0,) * param.ndim) for param in params],
    )[0]
    rows = lax.all_to_all(rows, ("pipe", "tensor", "core"), 0, 0, tiled=True)
    rows = rows.reshape(2, 2, 48, 2368)
    a = jnp.where(tensor == 0, rows[:, 0], rows[:, 1])
    b = jnp.where(tensor == 0, rows[:, 1], rows[:, 0])
    parts = [
        [a[..., 1536:1728], b[..., 1536:1728], a[..., :768]],
        [a[..., 1728:1920], b[..., 1728:1920], b[..., :768]],
        [a[..., 1920:2112], b[..., 1920:2112], a[..., 768:1536]],
        [a[..., 2112:2304], b[..., 2112:2304], a[..., 2304:], b[..., 2304:], b[..., 768:1536]],
    ]
    parts = [jnp.concatenate(part, -1)[:, None] for part in parts]
    for step in range(2):
        got = [exchange(part, ORDERS[i][step]) for i, part in enumerate(parts)]
        parts = [jnp.concatenate([x, y], 1) for x, y in zip(parts, got)]
    return parts, [exchange(part, ORDERS[i][2]) for i, part in enumerate(parts)]


def gather_layer(parts, got, layer):
    return [jnp.concatenate([x[layer], y[layer]], 0) for x, y in zip(parts, got)]


def gather_fourth(held):
    return [exchange(part, ORDERS[i][3]) for i, part in enumerate(held)]


def gather_core(held, got, units):
    own = assemble(held, got, units)
    return own, exchange(own, "c")


def fold_kernel(fixed, outputs, *refs):
    terms, outs = refs[: len(fixed)], refs[len(fixed) :]
    for out, places in zip(outs, outputs):
        for sources, layer, start in places:
            total = None
            for term, index, first, width in sources:
                value = terms[term][(*index, *(0,) * fixed[term], slice(None), slice(None), slice(first, first + width))]
                total = value.astype(f32) if total is None else total + value.astype(f32)
            cols = slice(start, start + total.shape[-1])
            if layer is None:
                out[:, :, cols] = total.astype(bf16)
            else:
                out[layer, :, :, cols] = total.astype(bf16)


def fold(terms, outputs, layers, grid, name):
    arrays, specs, shapes, out_specs = [], [], [], []
    for array, bits in terms:
        lead, (n, rows, cols) = array.shape[:-3], array.shape[-3:]
        n >>= len(bits)
        arrays.append(array.reshape(*lead, *(2,) * len(bits), n, rows, cols))
        block = (*lead, *(1,) * len(bits), n // grid, rows, cols)
        specs.append(pl.BlockSpec(block, lambda b, at=(0,) * len(lead) + tuple(bits): (*at, b, 0, 0)))
    for places in outputs:
        width = max(start + sources[0][3] for sources, _, start in places)
        lead = () if layers is None else (layers,)
        shapes.append(jax.ShapeDtypeStruct((*lead, n, 48, width), bf16))
        out_specs.append(pl.BlockSpec((*lead, n // grid, 48, width), lambda b, at=(0,) * len(lead): (*at, b, 0, 0)))
    return pl.pallas_call(
        functools.partial(fold_kernel, [len(bits) for _, bits in terms], outputs),
        name=name,
        grid=(grid,),
        out_shape=shapes,
        in_specs=specs,
        out_specs=out_specs,
        cost_estimate=pl.CostEstimate(flops=1, bytes_accessed=1, transcendentals=0),
        compiler_params=pltpu.CompilerParams(vmem_limit_bytes=52 * 2**20),
    )(*arrays)


def send_parts(parts, step):
    return [exchange(part, ORDERS[i][step]) for i, part in enumerate(parts)]


def fold_attention(own, got):
    outputs = [[([(k, (), 384 * i, ATTN_COLS[i]) for k in range(2)], None, 0)] for i in range(4)]
    return fold([(own, (1,)), (got, (1,))], outputs, None, 2, "fold_attention")


def fold_units(own, got):
    outputs = [[([(k, (i,), 0, 768) for k in range(2)], None, 0)] for i in range(4)]
    return fold([(own, (1,)), (got, (1,))], outputs, None, 2, "fold_units")


def fold_both(groups, side):
    terms = []
    outputs = [[] for _ in range(4)]
    for number, (own, got, received) in enumerate(groups):
        base, units = len(terms), number % 2
        terms += [(own, (0, side)), (got, (0, side))] + [(part, (side,)) for part in received]
        for i in range(4):
            width = 768 if units else ATTN_COLS[i]
            index, first = ((i,), 0) if units else ((), 384 * i)
            sources = [(base, index, first, width), (base + 1, index, first, width), (base + 2 + i, (), 0, width)]
            outputs[i].append((sources, number // 2, ATTN_COLS[i] * units))
    return fold(terms, outputs, 2, 2, ("fold_both_kept", "fold_both_sent")[side])


def fold_on(kept, got, side, name):
    terms = [(part, (side,)) for pair in zip(kept, got) for part in pair]
    outputs = []
    for i in range(4):
        width = kept[i].shape[-1]
        outputs.append([([(2 * i + k, (layer,), 0, width) for k in range(2)], layer, 0) for layer in range(2)])
    return fold(terms, outputs, 2, 1, name + ("_kept", "_sent")[side])


def collect_kernel(tensor_ref, *refs):
    kept, got, out_ref = refs[:4], refs[4:8], refs[8]
    for layer in range(2):
        p = [x[layer, 0].astype(f32) + y[layer, 0].astype(f32) for x, y in zip(kept, got)]
        for t in range(2):
            at = slice(192 * t, 192 * t + 192)
            values = [
                (0, p[t][:, 384:]),
                (768, p[2][:, 384:] if t == 0 else p[3][:, 512:]),
                (1536, jnp.concatenate([p[0][:, at], p[1][:, at]], 1)),
                (1920, jnp.concatenate([p[2][:, at], p[3][:, at]], 1)),
                (2304, p[3][:, 384 + 64 * t : 448 + 64 * t]),
            ]
            place = 4 * layer + 2 * (t ^ tensor_ref[0])
            for core in range(2):
                out = out_ref.at[place + core]
                for start, value in values:
                    out[:, start : start + value.shape[1]] = value[24 * core : 24 * core + 24].astype(bf16)


def finish_kernel(rows_ref, *refs):
    g_query, g_key, g_value, g_out, g_up, g_down, gb_query, gb_value = refs[:8]
    gb_up = refs[9]
    vectors = [refs[8], *refs[10:15]]
    small_ref = refs[15]
    halves = []
    for core in range(2):
        total = rows_ref[core].astype(f32)
        for k in range(1, 4):
            total = total + rows_ref[2 * k + core].astype(f32)
        halves.append(total)
        g_up[0, :, 768 * core : 768 * core + 768] = total[:, 0:768]
        g_down[0, :, 768 * core : 768 * core + 768] = total[:, 768:1536]
    for i, out in enumerate((g_query, g_key, g_value, g_out)):
        start = 1536 + 192 * i
        out[0] = jnp.concatenate([half[:, start : start + 192] for half in halves], 1)
    for out, lo, hi in ((gb_query, 8, 11), (gb_value, 11, 14), (gb_up, 14, 26)):
        out[0] = jnp.concatenate([half[0:2, 2304 + lo : 2304 + hi] for half in halves], 1)
    small_ref[...] = jnp.zeros_like(small_ref)
    small_ref[0:24, 0:64] = halves[0][:, 2304:2368]
    cols = small_ref[...].T
    for i, out in enumerate(vectors):
        out[...] = cols[i : i + 1, 0:24]


def scatter_end(kept, got):
    tensor = lax.axis_index("tensor").astype(jnp.int32).reshape(1)
    rows = kernel_call(collect_kernel, "collect", [tensor, *kept, *got], [((8, 24, 2368), bf16)], scalar=True)[0]
    rows = lax.all_to_all(rows, ("pipe", "tensor", "core"), 0, 0, tiled=True)
    shapes = [(1, 24, 384)] * 4 + [(1, 24, 1536)] * 2 + [(1, 2, 6)] * 2 + [(1, 24), (1, 2, 24)] + [(1, 24)] * 5
    return kernel_call(
        finish_kernel, "finish", [rows], [(shape, f32) for shape in shapes], scratch=[pltpu.VMEM((128, 128), f32)]
    )


def share_outputs(first_rows, second_rows):
    pipe, tensor = lax.axis_index("pipe"), lax.axis_index("tensor")
    keep = jnp.where(pipe == 0, first_rows, second_rows)
    send = jnp.where(pipe == 0, second_rows, first_rows)
    return keep, exchange_tensor(keep), exchange_pipe(send), exchange_both(send)


def order_outputs(rows):
    pipe, tensor = lax.axis_index("pipe"), lax.axis_index("tensor")
    a, b, c, d = rows
    a, b = jnp.where(tensor == 0, a, b), jnp.where(tensor == 0, b, a)
    c, d = jnp.where(tensor == 0, c, d), jnp.where(tensor == 0, d, c)
    a, c = jnp.where(pipe == 0, a, c), jnp.where(pipe == 0, c, a)
    b, d = jnp.where(pipe == 0, b, d), jnp.where(pipe == 0, d, b)
    return jnp.stack([a, b, c, d])[None]


def local(clip_frames, out_cotangent, clip_lengths, *params):
    micro = lax.axis_index("pipe") * 2 + lax.axis_index("tensor")
    chip = lax.axis_index("z") * 4 + lax.axis_index("x")

    parts, third = gather_start(params)
    held = [gather_layer(parts, third, layer) for layer in range(2)]
    got = [gather_fourth(held[0])]
    got[0], held[1] = pin(got[0], held[1])
    got.append(gather_fourth(held[1]))

    blocks = (chip ^ jnp.asarray(MASKS))[:, None]
    rows_at = (blocks * 48 + jnp.arange(48)[None]).reshape(-1)
    place_rows = (jnp.arange(768)[:, None] == rows_at[None]).astype(bf16)
    within = np.arange(48)
    units_at = np.where(within % 24 < 2, within // 24 * 2 + within % 24, 1000)
    units_at = (blocks * 4 + jnp.asarray(units_at)[None]).reshape(-1)
    place_units = (jnp.arange(64)[:, None] == units_at[None]).astype(bf16)
    place_back = (units_at[:, None] == jnp.arange(64)[None]).astype(bf16)

    frames = lax.dynamic_index_in_dim(clip_frames, micro, 0, keepdims=False)
    cotangent = lax.dynamic_index_in_dim(out_cotangent, micro, 0, keepdims=False)
    length = lax.dynamic_index_in_dim(clip_lengths, micro, 0, keepdims=False)
    x_first = dot(frames, place_rows).astype(bf16)
    grad_out = dot(cotangent, place_rows).astype(bf16)

    def placed_back(rows):
        return dot_cols(rows, place_rows).astype(bf16)

    attn_first = gather_core(held[0], got[0], False)
    own, got[0] = pin(attn_first[0], got[0])
    attn_first = (own, attn_first[1])
    middle_first, heads_first, soft_first, mixed_first, vec_first, up_bias_first = attention_forward(
        length, x_first, attn_first, place_units
    )
    units_first = gather_core(held[0], got[0], True)
    x_second, active_first, slope_first = units_forward(middle_first, units_first, vec_first, up_bias_first)
    x_second, got[1] = pin(x_second, got[1])
    attn_second = gather_core(held[1], got[1], False)
    own, got[1] = pin(attn_second[0], got[1])
    attn_second = (own, attn_second[1])
    middle_second, heads_second, soft_second, mixed_second, vec_second, up_bias_second = attention_forward(
        length, x_second, attn_second, place_units
    )
    units_second = gather_core(held[1], got[1], True)
    out_second, active_second, slope_second = units_forward(middle_second, units_second, vec_second, up_bias_second)
    shared = share_outputs(placed_back(x_second), placed_back(out_second))

    grad_middle, units_own_second, units_peer, units_vec, up_bias_grad = units_backward(
        grad_out, middle_second, active_second, slope_second, units_second, vec_second
    )
    units_got_second = exchange(units_peer, "c")
    attn = attention_backward(
        grad_middle, x_second, heads_second, soft_second, mixed_second, attn_second, vec_second, units_vec,
        up_bias_grad, place_back,
    )
    attn, units_got_second, shared = pin(attn, units_got_second, shared)
    section_output = order_outputs(shared)
    second_grad, attn_own_second, attn_peer = attn
    units_fourth_second = send_parts(fold_units(units_own_second, units_got_second), 3)
    attn_got_second = exchange(attn_peer, "c")

    units = units_backward(second_grad, middle_first, active_first, slope_first, units_first, vec_first)
    units, attn_got_second, units_fourth_second = pin(units, attn_got_second, units_fourth_second)
    grad_middle, units_own, units_peer, units_vec, up_bias_grad = units
    attn_fourth_second = send_parts(fold_attention(attn_own_second, attn_got_second), 3)
    units_got = exchange(units_peer, "c")

    attn = attention_backward(
        grad_middle, x_first, heads_first, soft_first, mixed_first, attn_first, vec_first, units_vec,
        up_bias_grad, place_back,
    )
    attn, units_got, attn_fourth_second = pin(attn, units_got, attn_fourth_second)
    first_grad, attn_own, attn_peer = attn
    units_fourth = send_parts(fold_units(units_own, units_got), 3)
    attn_got = exchange(attn_peer, "c")
    attn_fourth = send_parts(fold_attention(attn_own, attn_got), 3)
    input_grad = order_outputs(share_outputs(placed_back(first_grad), placed_back(second_grad)))

    groups = (
        (attn_own, attn_got, attn_fourth), (units_own, units_got, units_fourth),
        (attn_own_second, attn_got_second, attn_fourth_second),
        (units_own_second, units_got_second, units_fourth_second),
    )
    kept, got = fold_both(groups, 0), send_parts(fold_both(groups, 1), 2)
    kept, got = fold_on(kept, got, 0, "fold_four"), send_parts(fold_on(kept, got, 1, "fold_four"), 1)
    kept, got = fold_on(kept, got, 0, "fold_two"), send_parts(fold_on(kept, got, 1, "fold_two"), 0)
    return (section_output, input_grad, *scatter_end(kept, got))


def solution(mesh):
    fine = Mesh(mesh.devices.reshape(2, 4, 4, 2, 2), ("pipe", "z", "x", "core", "tensor"))
    shard = ("z", "x", "core")
    rows = P(None, shard, None)
    matrix = P("pipe", shard, "tensor")
    vector = P("pipe", shard)
    params = (matrix,) * 8 + (vector, matrix) + (vector,) * 5
    return jax.shard_map(
        local,
        mesh=fine,
        in_specs=(rows, rows, P(None, shard)) + params,
        out_specs=(P("pipe", None, shard, None),) * 2 + params,
        check_vma=False,
    )
```

```python
import functools

import jax
import jax.numpy as jnp
import numpy as np
from jax import lax
from jax.experimental import pallas as pl
from jax.experimental.pallas import tpu as pltpu
from jax.sharding import Mesh
from jax.sharding import PartitionSpec as P

HEAD = 64
bf16 = jnp.bfloat16
f32 = jnp.float32

half_root = 0.7071067811865476
gauss_factor = 0.3989422804014327


EXCHANGES = {"xu": ("x", 4, 1), "xv": ("x", 4, 3), "zu": ("z", 4, 1), "zv": ("z", 4, 3), "c": ("core", 2, 1)}
BLOCK_BITS = ("zv", "zu", "xv", "xu")
BIT_MASK = {"xu": 1, "xv": 3, "zu": 4, "zv": 12}
ORDERS = (
    ("xu", "xv", "zu", "zv"),
    ("xv", "xu", "zv", "zu"),
    ("zu", "zv", "xu", "xv"),
    ("zv", "zu", "xv", "xu"),
)
MASKS = np.zeros(16, np.int32)
for _index in range(16):
    for _place, _bit in enumerate(BLOCK_BITS):
        if (_index >> (3 - _place)) & 1:
            MASKS[_index] ^= BIT_MASK[_bit]
ATTN_COLS = (384, 384, 384, 512)


def block_place(part, index):
    place = 0
    for step in range(4):
        if (index >> step) & 1:
            place += 8 >> BLOCK_BITS.index(ORDERS[part][step])
    return place


def dot(left_side, right_side):
    return lax.dot_general(left_side, right_side, (((1,), (0,)), ((), ())), preferred_element_type=f32)


def dot_rows(left_side, right_side):
    return lax.dot_general(left_side, right_side, (((0,), (0,)), ((), ())), preferred_element_type=f32)


def dot_cols(left_side, right_side):
    return lax.dot_general(left_side, right_side, (((1,), (1,)), ((), ())), preferred_element_type=f32)


def norm_parts(values):
    center = values - jnp.mean(values, -1, keepdims=True)
    rescale = lax.rsqrt(jnp.mean(center * center, -1, keepdims=True) + 1e-05)
    return center * rescale, rescale


def norm_backward(grad_rows, normed, rescale, norm_gain):
    scaled = grad_rows * norm_gain
    inner = (
        scaled
        - jnp.mean(scaled, -1, keepdims=True)
        - normed * jnp.mean(scaled * normed, -1, keepdims=True)
    )
    return rescale * inner


def put_blocks(out_ref, part, slot, value):
    value = value.astype(bf16)
    for index in range(16):
        place = 48 * block_place(part, index)
        out_ref[slot, index] = value[place : place + 48]


def put_columns(out_ref, part, start, value):
    value = value.astype(bf16)
    for index in range(16):
        place = 48 * block_place(part, index)
        out_ref[index, :, start : start + value.shape[1]] = value[place : place + 48]


def attention_forward_kernel(
    length_ref, x_ref, own_ref, peer_ref, place_ref,
    middle_ref, heads_ref, soft_ref, mixed_ref, vec_ref, up_bias_ref,
):
    length = length_ref[0]
    vec_ref[0:6] = own_ref[:, 1536:].astype(f32).T[0:6]
    units = []
    for weight_ref in (own_ref, peer_ref):
        rows = dot(place_ref[...], weight_ref[:, 1536:]).T
        units += [rows[:64], rows[64:]]
    for row, first in ((6, 8), (7, 11)):
        pieces = [rows[first + i : first + i + 1] for rows in units for i in range(3)]
        vec_ref[row : row + 1] = jnp.concatenate(pieces, 1)
    pieces = [rows[14 + i : 15 + i] for rows in units for i in range(12)]
    for i in range(24):
        up_bias_ref[0:1, 128 * i : 128 * i + 128] = jnp.concatenate(pieces[2 * i : 2 * i + 2], 1)
    normed, _ = norm_parts(x_ref[...].astype(f32))
    normed_b = (normed * vec_ref[2:3] + vec_ref[3:4]).astype(bf16)
    for j in range(3):
        for half, weight_ref in enumerate((own_ref, peer_ref)):
            cols = slice(384 * half, 384 * half + 384)
            rows = dot(normed_b, weight_ref[:, 384 * j : 384 * j + 384])
            if j != 1:
                rows = rows + vec_ref[6 + j // 2 : 7 + j // 2, cols]
            heads_ref[j, :, cols] = rows.astype(bf16)
    count = x_ref.shape[0]
    live_keys = lax.broadcasted_iota(jnp.int32, (count, count), 1) < length
    for pair in range(6):
        both = []
        for head in (2 * pair, 2 * pair + 1):
            cols = slice(HEAD * head, HEAD * head + HEAD)
            scores = dot_cols(heads_ref[0, :, cols], heads_ref[1, :, cols]) * HEAD ** (-0.5)
            scores = jnp.where(live_keys, scores, -1e30)
            powers = jnp.exp(scores - jnp.max(scores, -1, keepdims=True))
            soft = powers / jnp.sum(powers, -1, keepdims=True)
            soft_ref[head] = soft
            both.append(dot(soft.astype(bf16), heads_ref[2, :, cols]))
        mixed_ref[:, 128 * pair : 128 * pair + 128] = jnp.concatenate(both, 1).astype(bf16)
    total = dot_cols(mixed_ref[:, :384], own_ref[:, 1152:1536])
    total = total + dot_cols(mixed_ref[:, 384:], peer_ref[:, 1152:1536])
    middle_ref[...] = x_ref[...].astype(f32) + total + vec_ref[0:1]


def units_forward_kernel(middle_ref, own_ref, peer_ref, vec_ref, up_bias_ref, result_ref, active_ref, slope_ref):
    middle = middle_ref[...]
    normed, _ = norm_parts(middle)
    normed_b = (normed * vec_ref[4:5] + vec_ref[5:6]).astype(bf16)
    total = middle + vec_ref[1:2]
    for half, weight_ref in enumerate((own_ref, peer_ref)):
        for j in range(2):
            cols = slice(768 * (2 * half + j), 768 * (2 * half + j) + 768)
            pre_active = dot(normed_b, weight_ref[j]) + up_bias_ref[0:1, cols]
            below = 0.5 * (1.0 + lax.erf(pre_active * half_root))
            active_b = (pre_active * below).astype(bf16)
            active_ref[:, cols] = active_b
            slope_ref[:, cols] = below + pre_active * jnp.exp(-0.5 * pre_active * pre_active) * gauss_factor
            total = total + dot_cols(active_b, weight_ref[2 + j])
    result_ref[...] = total.astype(bf16)


def units_backward_kernel(
    grad_ref, middle_ref, active_ref, slope_ref, own_ref, peer_ref, vec_ref,
    grad_middle_ref, grad_own_ref, grad_peer_ref, vec_grad_ref, up_bias_grad_ref,
):
    grad_b = grad_ref[...]
    grad_rows = grad_b.astype(f32)
    normed, rescale = norm_parts(middle_ref[...])
    normed_b = (normed * vec_ref[4:5] + vec_ref[5:6]).astype(bf16)
    normed_t = normed_b.T
    grad_t = grad_b.T
    grad_normed = None
    for half, weight_ref, out_ref in ((1, peer_ref, grad_peer_ref), (0, own_ref, grad_own_ref)):
        for j in range(2):
            cols = slice(768 * (2 * half + j), 768 * (2 * half + j) + 768)
            put_blocks(out_ref, 2 + j, 2 + j, dot(grad_t, active_ref[:, cols]))
            grad_upper = (dot(grad_b, weight_ref[2 + j]) * slope_ref[:, cols]).astype(bf16)
            up_bias_grad_ref[0:1, cols] = jnp.sum(grad_upper.astype(f32), 0, keepdims=True)
            put_blocks(out_ref, j, j, dot(normed_t, grad_upper))
            term = dot_cols(grad_upper, weight_ref[j])
            grad_normed = term if grad_normed is None else grad_normed + term
    grad_middle = grad_rows + norm_backward(grad_normed, normed, rescale, vec_ref[4:5])
    grad_middle_ref[...] = grad_middle
    vec_grad_ref[...] = jnp.zeros_like(vec_grad_ref)
    vec_grad_ref[0:1] = jnp.sum(grad_middle, 0, keepdims=True)
    vec_grad_ref[1:2] = jnp.sum(grad_rows, 0, keepdims=True)
    vec_grad_ref[4:5] = jnp.sum(grad_normed * normed, 0, keepdims=True)
    vec_grad_ref[5:6] = jnp.sum(grad_normed, 0, keepdims=True)


def attention_backward_kernel(
    grad_ref, x_ref, heads_ref, soft_ref, mixed_ref, own_ref, peer_ref, vec_ref,
    units_vec_ref, up_bias_grad_ref, place_ref,
    grad_in_ref, grad_own_ref, grad_peer_ref,
    grad_mixed_ref, grad_heads_ref, cols_ref, small_ref,
):
    grad_b = grad_ref[...].astype(bf16)
    grad_t = grad_b.T
    grad_mixed_ref[:, :384] = dot(grad_b, own_ref[:, 1152:1536]).astype(bf16)
    grad_mixed_ref[:, 384:] = dot(grad_b, peer_ref[:, 1152:1536]).astype(bf16)
    factor = HEAD ** (-0.5)
    for pair in range(6):
        found = ([], [], [])
        for head in (2 * pair, 2 * pair + 1):
            cols = slice(HEAD * head, HEAD * head + HEAD)
            soft = soft_ref[head]
            grad_head = grad_mixed_ref[:, cols]
            grad_soft = dot_cols(grad_head, heads_ref[2, :, cols])
            inner = jnp.sum(grad_soft * soft, -1, keepdims=True)
            grad_scores = (soft * (grad_soft - inner)).astype(bf16)
            found[0].append(dot(grad_scores, heads_ref[1, :, cols]) * factor)
            found[1].append(dot_rows(grad_scores, heads_ref[0, :, cols]) * factor)
            found[2].append(dot_rows(soft.astype(bf16), grad_head))
        for j in range(3):
            grad_heads_ref[j, :, 128 * pair : 128 * pair + 128] = jnp.concatenate(found[j], 1).astype(bf16)
    normed, rescale = norm_parts(x_ref[...].astype(f32))
    normed_b = (normed * vec_ref[2:3] + vec_ref[3:4]).astype(bf16)
    normed_t = normed_b.T
    grad_normed = None
    for half, weight_ref, out_ref in ((1, peer_ref, grad_peer_ref), (0, own_ref, grad_own_ref)):
        for j in range(3):
            rows = grad_heads_ref[j, :, 384 * half : 384 * half + 384]
            put_columns(out_ref, j, 384 * j, dot(normed_t, rows))
            term = dot_cols(rows, weight_ref[:, 384 * j : 384 * j + 384])
            grad_normed = term if grad_normed is None else grad_normed + term
    grad_in = grad_ref[...] + norm_backward(grad_normed, normed, rescale, vec_ref[2:3])
    grad_in_ref[...] = grad_in.astype(bf16)
    cols_ref[...] = jnp.zeros_like(cols_ref)
    cols_ref[0:2] = units_vec_ref[0:2]
    cols_ref[2:3] = jnp.sum(grad_normed * normed, 0, keepdims=True)
    cols_ref[3:4] = jnp.sum(grad_normed, 0, keepdims=True)
    cols_ref[4:6] = units_vec_ref[4:6]
    cols_ref[64:70] = cols_ref[0:6]
    cols = cols_ref[...].T
    query_bias = jnp.sum(grad_heads_ref[0].astype(f32), 0, keepdims=True)
    value_bias = jnp.sum(grad_heads_ref[2].astype(f32), 0, keepdims=True)
    for half, out_ref in ((1, grad_peer_ref), (0, grad_own_ref)):
        small_ref[...] = jnp.zeros_like(small_ref)
        for t in range(2):
            base = 64 * t
            for i in range(3):
                at = HEAD * (6 * half + 3 * t + i)
                small_ref[base + 8 + i : base + 9 + i] = query_bias[:, at : at + HEAD]
                small_ref[base + 11 + i : base + 12 + i] = value_bias[:, at : at + HEAD]
            for i in range(12):
                at = HEAD * (24 * half + 12 * t + i)
                small_ref[base + 14 + i : base + 15 + i] = up_bias_grad_ref[0:1, at : at + HEAD]
        small = dot_cols(place_ref[...], small_ref[...].astype(bf16)) + cols
        weight = dot(grad_t, mixed_ref[:, 384 * half : 384 * half + 384])
        put_columns(out_ref, 3, 1152, jnp.concatenate([weight, small], 1))


def kernel_call(kernel, name, inputs, outputs, scratch=(), scalar=False, blocks=None, large=True):
    whole = pl.BlockSpec(memory_space=pltpu.VMEM)
    specs = [whole] * len(inputs)
    out_specs = [whole] * len(outputs)
    if blocks is not None:
        specs = [pl.BlockSpec(shape, lambda i, at=at: at) for shape, at in blocks]
        out_specs = [pl.BlockSpec(shape, lambda i, n=len(shape): (0,) * n) for shape, _ in outputs]
    if scalar:
        specs[0] = pl.BlockSpec(memory_space=pltpu.SMEM)
    shapes = [jax.ShapeDtypeStruct(shape, dtype) for shape, dtype in outputs]
    return pl.pallas_call(
        kernel,
        name=name,
        out_shape=shapes,
        in_specs=specs,
        out_specs=out_specs,
        grid=() if blocks is None else (1,),
        scratch_shapes=list(scratch),
        cost_estimate=pl.CostEstimate(flops=1, bytes_accessed=1, transcendentals=0),
        compiler_params=pltpu.CompilerParams(vmem_limit_bytes=52 * 2**20 if large else None),
    )(*inputs)


ROWS = (192, 768)
HEADS_SHAPE = (3, 192, 768)
UNITS_SHAPE = (4, 16, 48, 768)
ATTN_SHAPE = (16, 48, 1664)


def attention_forward(length, x, attn, place_units):
    own, peer = attn
    return kernel_call(
        attention_forward_kernel, "attention_forward",
        [length, x, own, peer, place_units],
        [(ROWS, f32), (HEADS_SHAPE, bf16), ((12, 192, 192), f32), (ROWS, bf16), ((8, 768), f32), ((1, 3072), f32)],
        scalar=True,
    )


def units_forward(middle, units, vec, up_bias):
    own, peer = units
    return kernel_call(
        units_forward_kernel, "units_forward", [middle, own, peer, vec, up_bias],
        [(ROWS, bf16), ((192, 3072), bf16), ((192, 3072), f32)],
    )


def units_backward(grad_b, middle, active, slope, units, vec):
    own, peer = units
    return kernel_call(
        units_backward_kernel, "units_backward", [grad_b, middle, active, slope, own, peer, vec],
        [(ROWS, f32), (UNITS_SHAPE, bf16), (UNITS_SHAPE, bf16), ((8, 768), f32), ((1, 3072), f32)],
    )


def attention_backward(grad_middle, x, heads, soft, mixed, attn, vec, units_vec, up_bias_grad, place_units):
    own, peer = attn
    return kernel_call(
        attention_backward_kernel, "attention_backward",
        [grad_middle, x, heads, soft, mixed, own, peer, vec, units_vec, up_bias_grad, place_units],
        [(ROWS, bf16), (ATTN_SHAPE, bf16), (ATTN_SHAPE, bf16)],
        scratch=[pltpu.VMEM(ROWS, bf16), pltpu.VMEM(HEADS_SHAPE, bf16), pltpu.VMEM((128, 768), f32), pltpu.VMEM((128, 64), f32)],
    )


def exchange(value, bit):
    axis, size, flip = EXCHANGES[bit]
    return lax.ppermute(value, axis, [(i, i ^ flip) for i in range(size)])


def exchange_pipe(value):
    return lax.ppermute(value, "pipe", [(0, 1), (1, 0)])


def exchange_both(value):
    return lax.ppermute(value, ("pipe", "tensor"), [(i, i ^ 3) for i in range(4)])


def exchange_tensor(value):
    return lax.ppermute(value, "tensor", [(0, 1), (1, 0)])


def pin(*values):
    return lax.optimization_barrier(values)


def assemble_kernel(slots, *refs):
    count = len(slots)
    out = refs[-1]
    for number, (part, slot, start) in enumerate(slots):
        for index in range(16):
            rows = refs[number + (0 if index < 8 else count)][index % 8]
            place = slice(48 * block_place(part, index), 48 * block_place(part, index) + 48)
            cols = slice(start, start + rows.shape[1])
            if slot is None:
                out[place, cols] = rows
            else:
                out[slot, place, cols] = rows


def assemble(held, got, units):
    inputs, blocks, slots = [], [], []
    for part in range(4):
        width = (384, 256)[part // 3] if units else ATTN_COLS[part]
        first = ATTN_COLS[part] // width if units else 0
        for k in range(768 // width if units else 1):
            inputs.append(part)
            blocks.append(((8, 48, width), (0, 0, first + k)))
            slots.append((part, part, width * k) if units else (part, None, 384 * part))
    arrays = [held[part] for part in inputs] + [got[part] for part in inputs]
    shape = (4, 768, 768) if units else (768, 1664)
    kernel = functools.partial(assemble_kernel, slots)
    name = "assemble_units" if units else "assemble_attention"
    return kernel_call(kernel, name, arrays, [(shape, bf16)], blocks=blocks * 2)[0]


def pack_kernel(*refs):
    w_query, w_key, w_value, w_out, w_up, w_down, b_query, b_value = refs[:8]
    b_up = refs[9]
    vectors = [refs[8], *refs[10:15]]
    out_ref, vec_ref, small_ref = refs[15:]
    vec_ref[...] = jnp.zeros_like(vec_ref)
    for i, vector in enumerate(vectors):
        vec_ref[i : i + 1, 0:24] = vector[...].astype(f32)
    cols = vec_ref[...].T[0:24, 0:8]
    for half in range(2):
        small_ref[...] = jnp.zeros_like(small_ref)
        small_ref[:, 0:8] = cols
        small_ref[0:2, 8:11] = b_query[0, :, 3 * half : 3 * half + 3].astype(f32)
        small_ref[0:2, 11:14] = b_value[0, :, 3 * half : 3 * half + 3].astype(f32)
        small_ref[0:2, 14:26] = b_up[0, :, 12 * half : 12 * half + 12].astype(f32)
        small = small_ref[...].astype(bf16)
        wide, whole = slice(768 * half, 768 * half + 768), slice(192 * half, 192 * half + 192)
        first = jnp.concatenate([w_query[0, :, whole].astype(f32), w_key[0, :, whole].astype(f32)], 1).astype(bf16)
        second = jnp.concatenate([w_value[0, :, whole].astype(f32), w_out[0, :, whole].astype(f32)], 1).astype(bf16)
        for k in range(4):
            out = out_ref.at[2 * k + half]
            out[:, 0:768] = w_up[0, :, wide]
            out[:, 768:1536] = w_down[0, :, wide]
            out[:, 1536:1920] = first
            out[:, 1920:2304] = second
            out[:, 2304:2368] = small


def gather_start(params):
    tensor = lax.axis_index("tensor")
    rows = kernel_call(
        pack_kernel, "pack", list(params), [((8, 24, 2368), bf16)],
        scratch=[pltpu.VMEM((8, 128), f32), pltpu.VMEM((24, 64), f32)],
        blocks=[(param.shape, (0,) * param.ndim) for param in params], large=False,
    )[0]
    rows = lax.all_to_all(rows, ("pipe", "tensor", "core"), 0, 0, tiled=True)
    rows = rows.reshape(2, 2, 48, 2368)
    a = jnp.where(tensor == 0, rows[:, 0], rows[:, 1])
    b = jnp.where(tensor == 0, rows[:, 1], rows[:, 0])
    parts = [
        [a[..., 1536:1728], b[..., 1536:1728], a[..., :768]],
        [a[..., 1728:1920], b[..., 1728:1920], b[..., :768]],
        [a[..., 1920:2112], b[..., 1920:2112], a[..., 768:1536]],
        [a[..., 2112:2304], b[..., 2112:2304], a[..., 2304:], b[..., 2304:], b[..., 768:1536]],
    ]
    parts = [jnp.concatenate(part, -1)[:, None] for part in parts]
    for step in range(2):
        got = [exchange(part, ORDERS[i][step]) for i, part in enumerate(parts)]
        parts = [jnp.concatenate([x, y], 1) for x, y in zip(parts, got)]
    return parts, [exchange(part, ORDERS[i][2]) for i, part in enumerate(parts)]


def gather_layer(parts, got, layer):
    return [jnp.concatenate([x[layer], y[layer]], 0) for x, y in zip(parts, got)]


def gather_fourth(held):
    return [exchange(part, ORDERS[i][3]) for i, part in enumerate(held)]


def fold_kernel(fixed, outputs, *refs):
    terms, outs = refs[: len(fixed)], refs[len(fixed) :]
    for out, places in zip(outs, outputs):
        for sources, layer, start in places:
            total = None
            for term, index, first, width in sources:
                value = terms[term][(*index, *(0,) * fixed[term], slice(None), slice(None), slice(first, first + width))]
                total = value.astype(f32) if total is None else total + value.astype(f32)
            cols = slice(start, start + total.shape[-1])
            if layer is None:
                out[:, :, cols] = total.astype(bf16)
            else:
                out[layer, :, :, cols] = total.astype(bf16)


def fold(terms, outputs, layers, grid, name):
    arrays, specs, shapes, out_specs = [], [], [], []
    for array, bits in terms:
        lead, (n, rows, cols) = array.shape[:-3], array.shape[-3:]
        n >>= len(bits)
        arrays.append(array.reshape(*lead, *(2,) * len(bits), n, rows, cols))
        block = (*lead, *(1,) * len(bits), n // grid, rows, cols)
        specs.append(pl.BlockSpec(block, lambda b, at=(0,) * len(lead) + tuple(bits): (*at, b, 0, 0)))
    for places in outputs:
        width = max(start + sources[0][3] for sources, _, start in places)
        lead = () if layers is None else (layers,)
        shapes.append(jax.ShapeDtypeStruct((*lead, n, 48, width), bf16))
        out_specs.append(pl.BlockSpec((*lead, n // grid, 48, width), lambda b, at=(0,) * len(lead): (*at, b, 0, 0)))
    return pl.pallas_call(
        functools.partial(fold_kernel, [len(bits) for _, bits in terms], outputs),
        name=name,
        grid=(grid,),
        out_shape=shapes,
        in_specs=specs,
        out_specs=out_specs,
        cost_estimate=pl.CostEstimate(flops=1, bytes_accessed=1, transcendentals=0),
        compiler_params=pltpu.CompilerParams(vmem_limit_bytes=52 * 2**20),
    )(*arrays)


def send_parts(parts, step):
    return [exchange(part, ORDERS[i][step]) for i, part in enumerate(parts)]


def fold_attention(own, got):
    outputs = [[([(k, (), 384 * i, ATTN_COLS[i]) for k in range(2)], None, 0)] for i in range(4)]
    return fold([(own, (1,)), (got, (1,))], outputs, None, 2, "fold_attention")


def fold_units(own, got):
    outputs = [[([(k, (i,), 0, 768) for k in range(2)], None, 0)] for i in range(4)]
    return fold([(own, (1,)), (got, (1,))], outputs, None, 2, "fold_units")


def fold_both(groups, side):
    terms = []
    outputs = [[] for _ in range(4)]
    for number, (own, got, received) in enumerate(groups):
        base, units = len(terms), number % 2
        terms += [(own, (0, side)), (got, (0, side))] + [(part, (side,)) for part in received]
        for i in range(4):
            width = 768 if units else ATTN_COLS[i]
            index, first = ((i,), 0) if units else ((), 384 * i)
            sources = [(base, index, first, width), (base + 1, index, first, width), (base + 2 + i, (), 0, width)]
            outputs[i].append((sources, number // 2, ATTN_COLS[i] * units))
    return fold(terms, outputs, 2, 2, ("fold_both_kept", "fold_both_sent")[side])


def fold_on(kept, got, side, name):
    terms = [(part, (side,)) for pair in zip(kept, got) for part in pair]
    outputs = []
    for i in range(4):
        width = kept[i].shape[-1]
        outputs.append([([(2 * i + k, (layer,), 0, width) for k in range(2)], layer, 0) for layer in range(2)])
    return fold(terms, outputs, 2, 1, name + ("_kept", "_sent")[side])


def collect_kernel(tensor_ref, *refs):
    kept, got, out_ref = refs[:4], refs[4:8], refs[8]
    for layer in range(2):
        p = [x[layer, 0].astype(f32) + y[layer, 0].astype(f32) for x, y in zip(kept, got)]
        for t in range(2):
            at = slice(192 * t, 192 * t + 192)
            values = [
                (0, p[t][:, 384:]),
                (768, p[2][:, 384:] if t == 0 else p[3][:, 512:]),
                (1536, jnp.concatenate([p[0][:, at], p[1][:, at]], 1)),
                (1920, jnp.concatenate([p[2][:, at], p[3][:, at]], 1)),
                (2304, p[3][:, 384 + 64 * t : 448 + 64 * t]),
            ]
            place = 4 * layer + 2 * (t ^ tensor_ref[0])
            for core in range(2):
                out = out_ref.at[place + core]
                for start, value in values:
                    out[:, start : start + value.shape[1]] = value[24 * core : 24 * core + 24].astype(bf16)


def finish_kernel(rows_ref, *refs):
    g_query, g_key, g_value, g_out, g_up, g_down, gb_query, gb_value = refs[:8]
    gb_up = refs[9]
    vectors = [refs[8], *refs[10:15]]
    small_ref = refs[15]
    halves = []
    for core in range(2):
        total = rows_ref[core].astype(f32)
        for k in range(1, 4):
            total = total + rows_ref[2 * k + core].astype(f32)
        halves.append(total)
        g_up[0, :, 768 * core : 768 * core + 768] = total[:, 0:768]
        g_down[0, :, 768 * core : 768 * core + 768] = total[:, 768:1536]
    for i, out in enumerate((g_query, g_key, g_value, g_out)):
        start = 1536 + 192 * i
        out[0] = jnp.concatenate([half[:, start : start + 192] for half in halves], 1)
    for out, lo, hi in ((gb_query, 8, 11), (gb_value, 11, 14), (gb_up, 14, 26)):
        out[0] = jnp.concatenate([half[0:2, 2304 + lo : 2304 + hi] for half in halves], 1)
    small_ref[...] = jnp.zeros_like(small_ref)
    small_ref[0:24, 0:64] = halves[0][:, 2304:2368]
    cols = small_ref[...].T
    for i, out in enumerate(vectors):
        out[...] = cols[i : i + 1, 0:24]


def scatter_end(kept, got):
    tensor = lax.axis_index("tensor").astype(jnp.int32).reshape(1)
    rows = kernel_call(collect_kernel, "collect", [tensor, *kept, *got], [((8, 24, 2368), bf16)], scalar=True)[0]
    rows = lax.all_to_all(rows, ("pipe", "tensor", "core"), 0, 0, tiled=True)
    shapes = [(1, 24, 384)] * 4 + [(1, 24, 1536)] * 2 + [(1, 2, 6)] * 2 + [(1, 24), (1, 2, 24)] + [(1, 24)] * 5
    return kernel_call(
        finish_kernel, "finish", [rows], [(shape, f32) for shape in shapes], scratch=[pltpu.VMEM((128, 128), f32)]
    )


def share_outputs(first_rows, second_rows):
    pipe, tensor = lax.axis_index("pipe"), lax.axis_index("tensor")
    keep = jnp.where(pipe == 0, first_rows, second_rows)
    send = jnp.where(pipe == 0, second_rows, first_rows)
    return keep, exchange_tensor(keep), exchange_pipe(send), exchange_both(send)


def order_outputs(rows):
    pipe, tensor = lax.axis_index("pipe"), lax.axis_index("tensor")
    a, b, c, d = rows
    a, b = jnp.where(tensor == 0, a, b), jnp.where(tensor == 0, b, a)
    c, d = jnp.where(tensor == 0, c, d), jnp.where(tensor == 0, d, c)
    a, c = jnp.where(pipe == 0, a, c), jnp.where(pipe == 0, c, a)
    b, d = jnp.where(pipe == 0, b, d), jnp.where(pipe == 0, d, b)
    return jnp.stack([a, b, c, d])[None]


def local(clip_frames, out_cotangent, clip_lengths, *params):
    micro = lax.axis_index("pipe") * 2 + lax.axis_index("tensor")
    chip = lax.axis_index("z") * 4 + lax.axis_index("x")

    parts, third = gather_start(params)
    held = [gather_layer(parts, third, layer) for layer in range(2)]
    got = [gather_fourth(held[0])]
    got[0], held[1] = pin(got[0], held[1])
    got.append(gather_fourth(held[1]))

    blocks = (chip ^ jnp.asarray(MASKS))[:, None]
    rows_at = (blocks * 48 + jnp.arange(48)[None]).reshape(-1)
    place_rows = (jnp.arange(768)[:, None] == rows_at[None]).astype(bf16)
    within = np.arange(48)
    units_at = np.where(within % 24 < 2, within // 24 * 2 + within % 24, 1000)
    units_at = (blocks * 4 + jnp.asarray(units_at)[None]).reshape(-1)
    place_units = (jnp.arange(64)[:, None] == units_at[None]).astype(bf16)
    place_back = (units_at[:, None] == jnp.arange(64)[None]).astype(bf16)

    frames = lax.dynamic_index_in_dim(clip_frames, micro, 0, keepdims=False)
    cotangent = lax.dynamic_index_in_dim(out_cotangent, micro, 0, keepdims=False)
    length = lax.dynamic_index_in_dim(clip_lengths, micro, 0, keepdims=False)
    x_first = dot(frames, place_rows).astype(bf16)
    grad_out = dot(cotangent, place_rows).astype(bf16)

    def placed_back(rows):
        return dot_cols(rows, place_rows).astype(bf16)

    attn_own = assemble(held[0], got[0], False)
    attn_own, got[0] = pin(attn_own, got[0])
    attn_peer = exchange(attn_own, "c")
    units_own = assemble(held[0], got[0], True)
    attn_peer, units_own = pin(attn_peer, units_own)
    attn_first = attn_own, attn_peer
    units_first = units_own, exchange(units_own, "c")
    middle_first, heads_first, soft_first, mixed_first, vec_first, up_bias_first = attention_forward(
        length, x_first, attn_first, place_units
    )
    x_second, active_first, slope_first = units_forward(middle_first, units_first, vec_first, up_bias_first)
    x_second, got[1] = pin(x_second, got[1])
    attn_own = assemble(held[1], got[1], False)
    attn_own, got[1] = pin(attn_own, got[1])
    attn_peer = exchange(attn_own, "c")
    units_own = assemble(held[1], got[1], True)
    attn_peer, units_own = pin(attn_peer, units_own)
    attn_second = attn_own, attn_peer
    units_second = units_own, exchange(units_own, "c")
    middle_second, heads_second, soft_second, mixed_second, vec_second, up_bias_second = attention_forward(
        length, x_second, attn_second, place_units
    )
    out_second, active_second, slope_second = units_forward(middle_second, units_second, vec_second, up_bias_second)
    shared = share_outputs(placed_back(x_second), placed_back(out_second))

    grad_middle, units_own_second, units_peer, units_vec, up_bias_grad = units_backward(
        grad_out, middle_second, active_second, slope_second, units_second, vec_second
    )
    units_got_second = exchange(units_peer, "c")
    attn = attention_backward(
        grad_middle, x_second, heads_second, soft_second, mixed_second, attn_second, vec_second, units_vec,
        up_bias_grad, place_back,
    )
    attn, units_got_second, shared = pin(attn, units_got_second, shared)
    section_output = order_outputs(shared)
    second_grad, attn_own_second, attn_peer = attn
    units_fourth_second = send_parts(fold_units(units_own_second, units_got_second), 3)
    attn_got_second = exchange(attn_peer, "c")

    units = units_backward(second_grad, middle_first, active_first, slope_first, units_first, vec_first)
    units, attn_got_second, units_fourth_second = pin(units, attn_got_second, units_fourth_second)
    grad_middle, units_own, units_peer, units_vec, up_bias_grad = units
    attn_fourth_second = send_parts(fold_attention(attn_own_second, attn_got_second), 3)
    units_got = exchange(units_peer, "c")

    attn = attention_backward(
        grad_middle, x_first, heads_first, soft_first, mixed_first, attn_first, vec_first, units_vec,
        up_bias_grad, place_back,
    )
    attn, units_got, attn_fourth_second = pin(attn, units_got, attn_fourth_second)
    first_grad, attn_own, attn_peer = attn
    units_fourth = send_parts(fold_units(units_own, units_got), 3)
    attn_got = exchange(attn_peer, "c")
    attn_fourth = send_parts(fold_attention(attn_own, attn_got), 3)
    input_grad = order_outputs(share_outputs(placed_back(first_grad), placed_back(second_grad)))

    groups = (
        (attn_own, attn_got, attn_fourth), (units_own, units_got, units_fourth),
        (attn_own_second, attn_got_second, attn_fourth_second),
        (units_own_second, units_got_second, units_fourth_second),
    )
    kept, got = fold_both(groups, 0), send_parts(fold_both(groups, 1), 2)
    kept, got = fold_on(kept, got, 0, "fold_four"), send_parts(fold_on(kept, got, 1, "fold_four"), 1)
    kept, got = fold_on(kept, got, 0, "fold_two"), send_parts(fold_on(kept, got, 1, "fold_two"), 0)
    return (section_output, input_grad, *scatter_end(kept, got))


def solution(mesh):
    fine = Mesh(mesh.devices.reshape(2, 4, 4, 2, 2), ("pipe", "z", "x", "core", "tensor"))
    shard = ("z", "x", "core")
    rows = P(None, shard, None)
    matrix = P("pipe", shard, "tensor")
    vector = P("pipe", shard)
    params = (matrix,) * 8 + (vector, matrix) + (vector,) * 5
    return jax.shard_map(
        local,
        mesh=fine,
        in_specs=(rows, rows, P(None, shard)) + params,
        out_specs=(P("pipe", None, shard, None),) * 2 + params,
        check_vma=False,
    )
```

```python
import functools

import jax
import jax.numpy as jnp
import numpy as np
from jax import lax
from jax.experimental import pallas as pl
from jax.experimental.pallas import tpu as pltpu
from jax.sharding import Mesh
from jax.sharding import PartitionSpec as P

HEAD = 64
bf16 = jnp.bfloat16
f32 = jnp.float32

half_root = 0.7071067811865476
gauss_factor = 0.3989422804014327


EXCHANGES = {"xu": ("x", 4, 1), "xv": ("x", 4, 3), "zu": ("z", 4, 1), "zv": ("z", 4, 3), "c": ("core", 2, 1)}
BLOCK_BITS = ("zv", "zu", "xv", "xu")
BIT_MASK = {"xu": 1, "xv": 3, "zu": 4, "zv": 12}
ORDERS = (
    ("xu", "xv", "zu", "zv"),
    ("xv", "xu", "zv", "zu"),
    ("zu", "zv", "xu", "xv"),
    ("zv", "zu", "xv", "xu"),
)
MASKS = np.zeros(16, np.int32)
for _index in range(16):
    for _place, _bit in enumerate(BLOCK_BITS):
        if (_index >> (3 - _place)) & 1:
            MASKS[_index] ^= BIT_MASK[_bit]
ATTN_COLS = (384, 384, 384, 512)


def block_place(part, index):
    place = 0
    for step in range(4):
        if (index >> step) & 1:
            place += 8 >> BLOCK_BITS.index(ORDERS[part][step])
    return place


def dot(left_side, right_side):
    return lax.dot_general(left_side, right_side, (((1,), (0,)), ((), ())), preferred_element_type=f32)


def dot_rows(left_side, right_side):
    return lax.dot_general(left_side, right_side, (((0,), (0,)), ((), ())), preferred_element_type=f32)


def dot_cols(left_side, right_side):
    return lax.dot_general(left_side, right_side, (((1,), (1,)), ((), ())), preferred_element_type=f32)


def norm_parts(values):
    center = values - jnp.mean(values, -1, keepdims=True)
    rescale = lax.rsqrt(jnp.mean(center * center, -1, keepdims=True) + 1e-05)
    return center * rescale, rescale


def norm_backward(grad_rows, normed, rescale, norm_gain):
    scaled = grad_rows * norm_gain
    inner = (
        scaled
        - jnp.mean(scaled, -1, keepdims=True)
        - normed * jnp.mean(scaled * normed, -1, keepdims=True)
    )
    return rescale * inner


def put_blocks(out_ref, part, half, slot, start, value, where_ref):
    value = value.astype(bf16)
    for index in range(16):
        if where_ref is None:
            place = 48 * block_place(part, index)
            block = out_ref.at[index] if slot is None else out_ref.at[slot, index]
        else:
            place = 48 * index
            block = out_ref.at[2 * (where_ref[0] ^ int(MASKS[index])) + (where_ref[1] ^ half)]
        block[:, start : start + value.shape[1]] = value[place : place + 48]


def attention_forward_kernel(
    length_ref, x_ref, own_ref, peer_ref, place_ref,
    middle_ref, heads_ref, soft_ref, mixed_ref, vec_ref, up_bias_ref,
):
    length = length_ref[0]
    vec_ref[0:6] = own_ref[:, 1536:].astype(f32).T[0:6]
    units = []
    for weight_ref in (own_ref, peer_ref):
        rows = dot(place_ref[...], weight_ref[:, 1536:]).T
        units += [rows[:64], rows[64:]]
    for row, first in ((6, 8), (7, 11)):
        pieces = [rows[first + i : first + i + 1] for rows in units for i in range(3)]
        vec_ref[row : row + 1] = jnp.concatenate(pieces, 1)
    pieces = [rows[14 + i : 15 + i] for rows in units for i in range(12)]
    for i in range(24):
        up_bias_ref[0:1, 128 * i : 128 * i + 128] = jnp.concatenate(pieces[2 * i : 2 * i + 2], 1)
    normed, _ = norm_parts(x_ref[...].astype(f32))
    normed_b = (normed * vec_ref[2:3] + vec_ref[3:4]).astype(bf16)
    for j in range(3):
        for half, weight_ref in enumerate((own_ref, peer_ref)):
            cols = slice(384 * half, 384 * half + 384)
            rows = dot(normed_b, weight_ref[:, 384 * j : 384 * j + 384])
            if j != 1:
                rows = rows + vec_ref[6 + j // 2 : 7 + j // 2, cols]
            heads_ref[j, :, cols] = rows.astype(bf16)
    count = x_ref.shape[0]
    live_keys = lax.broadcasted_iota(jnp.int32, (count, count), 1) < length
    for pair in range(6):
        both = []
        for head in (2 * pair, 2 * pair + 1):
            cols = slice(HEAD * head, HEAD * head + HEAD)
            scores = dot_cols(heads_ref[0, :, cols], heads_ref[1, :, cols]) * HEAD ** (-0.5)
            scores = jnp.where(live_keys, scores, -1e30)
            powers = jnp.exp(scores - jnp.max(scores, -1, keepdims=True))
            soft = powers / jnp.sum(powers, -1, keepdims=True)
            soft_ref[head] = soft
            both.append(dot(soft.astype(bf16), heads_ref[2, :, cols]))
        mixed_ref[:, 128 * pair : 128 * pair + 128] = jnp.concatenate(both, 1).astype(bf16)
    total = dot_cols(mixed_ref[:, :384], own_ref[:, 1152:1536])
    total = total + dot_cols(mixed_ref[:, 384:], peer_ref[:, 1152:1536])
    middle_ref[...] = x_ref[...].astype(f32) + total + vec_ref[0:1]


def units_forward_kernel(middle_ref, own_ref, peer_ref, vec_ref, up_bias_ref, result_ref, active_ref, slope_ref):
    middle = middle_ref[...]
    normed, _ = norm_parts(middle)
    normed_b = (normed * vec_ref[4:5] + vec_ref[5:6]).astype(bf16)
    total = middle + vec_ref[1:2]
    for half, weight_ref in enumerate((own_ref, peer_ref)):
        for j in range(2):
            cols = slice(768 * (2 * half + j), 768 * (2 * half + j) + 768)
            pre_active = dot(normed_b, weight_ref[j]) + up_bias_ref[0:1, cols]
            below = 0.5 * (1.0 + lax.erf(pre_active * half_root))
            active_b = (pre_active * below).astype(bf16)
            active_ref[:, cols] = active_b
            slope_ref[:, cols] = below + pre_active * jnp.exp(-0.5 * pre_active * pre_active) * gauss_factor
            total = total + dot_cols(active_b, weight_ref[2 + j])
    result_ref[...] = total.astype(bf16)


def units_backward_kernel(placed, *refs):
    where_ref, refs = (refs[0], refs[1:]) if placed else (None, refs)
    grad_ref, middle_ref, active_ref, slope_ref, own_ref, peer_ref, vec_ref = refs[:7]
    grad_middle_ref, vec_grad_ref, up_bias_grad_ref, grad_own_ref = refs[7:11]
    grad_peer_ref = grad_own_ref if placed else refs[11]
    grad_b = grad_ref[...]
    grad_rows = grad_b.astype(f32)
    normed, rescale = norm_parts(middle_ref[...])
    normed_b = (normed * vec_ref[4:5] + vec_ref[5:6]).astype(bf16)
    normed_t = normed_b.T
    grad_t = grad_b.T
    grad_normed = None
    for half, weight_ref, out_ref in ((1, peer_ref, grad_peer_ref), (0, own_ref, grad_own_ref)):
        for j in range(2):
            cols = slice(768 * (2 * half + j), 768 * (2 * half + j) + 768)
            slot, start = (None, 768 * j) if placed else (j, 0)
            value = dot(grad_t, active_ref[:, cols])
            put_blocks(out_ref, 2 + j, half, None if placed else 2 + j, 1536 + start if placed else 0, value, where_ref)
            grad_upper = (dot(grad_b, weight_ref[2 + j]) * slope_ref[:, cols]).astype(bf16)
            up_bias_grad_ref[0:1, cols] = jnp.sum(grad_upper.astype(f32), 0, keepdims=True)
            put_blocks(out_ref, j, half, slot, start, dot(normed_t, grad_upper), where_ref)
            term = dot_cols(grad_upper, weight_ref[j])
            grad_normed = term if grad_normed is None else grad_normed + term
    grad_middle = grad_rows + norm_backward(grad_normed, normed, rescale, vec_ref[4:5])
    grad_middle_ref[...] = grad_middle
    vec_grad_ref[...] = jnp.zeros_like(vec_grad_ref)
    vec_grad_ref[0:1] = jnp.sum(grad_middle, 0, keepdims=True)
    vec_grad_ref[1:2] = jnp.sum(grad_rows, 0, keepdims=True)
    vec_grad_ref[4:5] = jnp.sum(grad_normed * normed, 0, keepdims=True)
    vec_grad_ref[5:6] = jnp.sum(grad_normed, 0, keepdims=True)


def attention_backward_kernel(placed, *refs):
    where_ref, refs = (refs[0], refs[1:]) if placed else (None, refs)
    grad_ref, x_ref, heads_ref, soft_ref, mixed_ref, own_ref, peer_ref, vec_ref = refs[:8]
    units_vec_ref, up_bias_grad_ref, place_ref, grad_in_ref, grad_own_ref = refs[8:13]
    grad_peer_ref = grad_own_ref if placed else refs[13]
    grad_mixed_ref, grad_heads_ref, cols_ref, small_ref = refs[-4:]
    grad_b = grad_ref[...].astype(bf16)
    grad_t = grad_b.T
    grad_mixed_ref[:, :384] = dot(grad_b, own_ref[:, 1152:1536]).astype(bf16)
    grad_mixed_ref[:, 384:] = dot(grad_b, peer_ref[:, 1152:1536]).astype(bf16)
    factor = HEAD ** (-0.5)
    for pair in range(6):
        found = ([], [], [])
        for head in (2 * pair, 2 * pair + 1):
            cols = slice(HEAD * head, HEAD * head + HEAD)
            soft = soft_ref[head]
            grad_head = grad_mixed_ref[:, cols]
            grad_soft = dot_cols(grad_head, heads_ref[2, :, cols])
            inner = jnp.sum(grad_soft * soft, -1, keepdims=True)
            grad_scores = (soft * (grad_soft - inner)).astype(bf16)
            found[0].append(dot(grad_scores, heads_ref[1, :, cols]) * factor)
            found[1].append(dot_rows(grad_scores, heads_ref[0, :, cols]) * factor)
            found[2].append(dot_rows(soft.astype(bf16), grad_head))
        for j in range(3):
            grad_heads_ref[j, :, 128 * pair : 128 * pair + 128] = jnp.concatenate(found[j], 1).astype(bf16)
    normed, rescale = norm_parts(x_ref[...].astype(f32))
    normed_b = (normed * vec_ref[2:3] + vec_ref[3:4]).astype(bf16)
    normed_t = normed_b.T
    grad_normed = None
    for half, weight_ref, out_ref in ((1, peer_ref, grad_peer_ref), (0, own_ref, grad_own_ref)):
        for j in range(3):
            rows = grad_heads_ref[j, :, 384 * half : 384 * half + 384]
            put_blocks(out_ref, j, half, None, 384 * j, dot(normed_t, rows), where_ref)
            term = dot_cols(rows, weight_ref[:, 384 * j : 384 * j + 384])
            grad_normed = term if grad_normed is None else grad_normed + term
    grad_in = grad_ref[...] + norm_backward(grad_normed, normed, rescale, vec_ref[2:3])
    grad_in_ref[...] = grad_in.astype(bf16)
    cols_ref[...] = jnp.zeros_like(cols_ref)
    cols_ref[0:2] = units_vec_ref[0:2]
    cols_ref[2:3] = jnp.sum(grad_normed * normed, 0, keepdims=True)
    cols_ref[3:4] = jnp.sum(grad_normed, 0, keepdims=True)
    cols_ref[4:6] = units_vec_ref[4:6]
    cols_ref[64:70] = cols_ref[0:6]
    cols = cols_ref[...].T
    query_bias = jnp.sum(grad_heads_ref[0].astype(f32), 0, keepdims=True)
    value_bias = jnp.sum(grad_heads_ref[2].astype(f32), 0, keepdims=True)
    for half, out_ref in ((1, grad_peer_ref), (0, grad_own_ref)):
        small_ref[...] = jnp.zeros_like(small_ref)
        for t in range(2):
            base = 64 * t
            for i in range(3):
                at = HEAD * (6 * half + 3 * t + i)
                small_ref[base + 8 + i : base + 9 + i] = query_bias[:, at : at + HEAD]
                small_ref[base + 11 + i : base + 12 + i] = value_bias[:, at : at + HEAD]
            for i in range(12):
                at = HEAD * (24 * half + 12 * t + i)
                small_ref[base + 14 + i : base + 15 + i] = up_bias_grad_ref[0:1, at : at + HEAD]
        small = dot_cols(place_ref[...], small_ref[...].astype(bf16)) + cols
        weight = dot(grad_t, mixed_ref[:, 384 * half : 384 * half + 384])
        put_blocks(out_ref, 3, half, None, 1152, jnp.concatenate([weight, small], 1), where_ref)


def kernel_call(kernel, name, inputs, outputs, scratch=(), scalar=False, blocks=None, large=True):
    whole = pl.BlockSpec(memory_space=pltpu.VMEM)
    specs = [whole] * len(inputs)
    out_specs = [whole] * len(outputs)
    if blocks is not None:
        specs = [pl.BlockSpec(shape, lambda i, at=at: at) for shape, at in blocks]
        out_specs = [pl.BlockSpec(shape, lambda i, n=len(shape): (0,) * n) for shape, _ in outputs]
    if scalar:
        specs[0] = pl.BlockSpec(memory_space=pltpu.SMEM)
    shapes = [jax.ShapeDtypeStruct(shape, dtype) for shape, dtype in outputs]
    return pl.pallas_call(
        kernel,
        name=name,
        out_shape=shapes,
        in_specs=specs,
        out_specs=out_specs,
        grid=() if blocks is None else (1,),
        scratch_shapes=list(scratch),
        cost_estimate=pl.CostEstimate(flops=1, bytes_accessed=1, transcendentals=0),
        compiler_params=pltpu.CompilerParams(vmem_limit_bytes=52 * 2**20 if large else None),
    )(*inputs)


ROWS = (192, 768)
HEADS_SHAPE = (3, 192, 768)
UNITS_SHAPE = (4, 16, 48, 768)
ATTN_SHAPE = (16, 48, 1664)
PLACED_UNITS = (32, 48, 3072)
PLACED_ATTN = (32, 48, 1664)


def attention_forward(length, x, attn, place_units):
    own, peer = attn
    return kernel_call(
        attention_forward_kernel, "attention_forward",
        [length, x, own, peer, place_units],
        [(ROWS, f32), (HEADS_SHAPE, bf16), ((12, 192, 192), f32), (ROWS, bf16), ((8, 768), f32), ((1, 3072), f32)],
        scalar=True,
    )


def units_forward(middle, units, vec, up_bias):
    own, peer = units
    return kernel_call(
        units_forward_kernel, "units_forward", [middle, own, peer, vec, up_bias],
        [(ROWS, bf16), ((192, 3072), bf16), ((192, 3072), f32)],
    )


def units_backward(grad_b, middle, active, slope, units, vec, where=None):
    own, peer = units
    placed = where is not None
    shapes = [PLACED_UNITS] if placed else [UNITS_SHAPE] * 2
    return kernel_call(
        functools.partial(units_backward_kernel, placed), "units_backward",
        [where] * placed + [grad_b, middle, active, slope, own, peer, vec],
        [(ROWS, f32), ((8, 768), f32), ((1, 3072), f32)] + [(shape, bf16) for shape in shapes], scalar=placed,
    )


def attention_backward(
    grad_middle, x, heads, soft, mixed, attn, vec, units_vec, up_bias_grad, place_units, where=None
):
    own, peer = attn
    placed = where is not None
    shapes = [PLACED_ATTN] if placed else [ATTN_SHAPE] * 2
    return kernel_call(
        functools.partial(attention_backward_kernel, placed), "attention_backward",
        [where] * placed
        + [grad_middle, x, heads, soft, mixed, own, peer, vec, units_vec, up_bias_grad, place_units],
        [(ROWS, bf16)] + [(shape, bf16) for shape in shapes], scalar=placed,
        scratch=[
            pltpu.VMEM(ROWS, bf16), pltpu.VMEM(HEADS_SHAPE, bf16), pltpu.VMEM((128, 768), f32),
            pltpu.VMEM((128, 64), f32),
        ],
    )


def exchange(value, bit):
    axis, size, flip = EXCHANGES[bit]
    return lax.ppermute(value, axis, [(i, i ^ flip) for i in range(size)])


def exchange_pipe(value):
    return lax.ppermute(value, "pipe", [(0, 1), (1, 0)])


def exchange_both(value):
    return lax.ppermute(value, ("pipe", "tensor"), [(i, i ^ 3) for i in range(4)])


def exchange_tensor(value):
    return lax.ppermute(value, "tensor", [(0, 1), (1, 0)])


def pin(*values):
    return lax.optimization_barrier(values)


def assemble_kernel(slots, *refs):
    count = len(slots)
    out = refs[-1]
    for number, (part, slot, start) in enumerate(slots):
        for index in range(16):
            rows = refs[number + (0 if index < 8 else count)][index % 8]
            place = slice(48 * block_place(part, index), 48 * block_place(part, index) + 48)
            cols = slice(start, start + rows.shape[1])
            if slot is None:
                out[place, cols] = rows
            else:
                out[slot, place, cols] = rows


def assemble(held, got, units):
    inputs, blocks, slots = [], [], []
    for part in range(4):
        width = (384, 256)[part // 3] if units else ATTN_COLS[part]
        first = ATTN_COLS[part] // width if units else 0
        for k in range(768 // width if units else 1):
            inputs.append(part)
            blocks.append(((8, 48, width), (0, 0, first + k)))
            slots.append((part, part, width * k) if units else (part, None, 384 * part))
    arrays = [held[part] for part in inputs] + [got[part] for part in inputs]
    shape = (4, 768, 768) if units else (768, 1664)
    kernel = functools.partial(assemble_kernel, slots)
    name = "assemble_units" if units else "assemble_attention"
    return kernel_call(kernel, name, arrays, [(shape, bf16)], blocks=blocks * 2)[0]


def place_kernel(chip_ref, rows_ref, out_ref):
    for index in range(16):
        rows = rows_ref[chip_ref[0] ^ int(MASKS[index])]
        place = slice(48 * index, 48 * index + 48)
        if len(out_ref.shape) == 2:
            out_ref[place] = rows
        else:
            for j in range(4):
                out_ref[j, place] = rows[:, 768 * j : 768 * j + 768]


def place_blocks(where, rows, units):
    shape = (4, 768, 768) if units else (768, 1664)
    name = "place_units" if units else "place_attention"
    return kernel_call(place_kernel, name, [where, rows], [(shape, bf16)], scalar=True)[0]


def pack_kernel(*refs):
    w_query, w_key, w_value, w_out, w_up, w_down, b_query, b_value = refs[:8]
    b_up = refs[9]
    vectors = [refs[8], *refs[10:15]]
    out_ref, vec_ref, small_ref = refs[15:]
    vec_ref[...] = jnp.zeros_like(vec_ref)
    for i, vector in enumerate(vectors):
        vec_ref[i : i + 1, 0:24] = vector[...].astype(f32)
    cols = vec_ref[...].T[0:24, 0:8]
    for half in range(2):
        small_ref[...] = jnp.zeros_like(small_ref)
        small_ref[:, 0:8] = cols
        small_ref[0:2, 8:11] = b_query[0, :, 3 * half : 3 * half + 3].astype(f32)
        small_ref[0:2, 11:14] = b_value[0, :, 3 * half : 3 * half + 3].astype(f32)
        small_ref[0:2, 14:26] = b_up[0, :, 12 * half : 12 * half + 12].astype(f32)
        small = small_ref[...].astype(bf16)
        wide, whole = slice(768 * half, 768 * half + 768), slice(192 * half, 192 * half + 192)
        first = jnp.concatenate([w_query[0, :, whole].astype(f32), w_key[0, :, whole].astype(f32)], 1).astype(bf16)
        second = jnp.concatenate([w_value[0, :, whole].astype(f32), w_out[0, :, whole].astype(f32)], 1).astype(bf16)
        for k in range(4):
            out = out_ref.at[2 * k + half]
            out[:, 0:768] = w_up[0, :, wide]
            out[:, 768:1536] = w_down[0, :, wide]
            out[:, 1536:1920] = first
            out[:, 1920:2304] = second
            out[:, 2304:2368] = small


def gather_start(params):
    tensor = lax.axis_index("tensor")
    rows = kernel_call(
        pack_kernel, "pack", list(params), [((8, 24, 2368), bf16)],
        scratch=[pltpu.VMEM((8, 128), f32), pltpu.VMEM((24, 64), f32)],
        blocks=[(param.shape, (0,) * param.ndim) for param in params], large=False,
    )[0]
    rows = lax.all_to_all(rows, ("pipe", "tensor", "core"), 0, 0, tiled=True)
    rows = rows.reshape(2, 2, 48, 2368)
    a = jnp.where(tensor == 0, rows[:, 0], rows[:, 1])
    b = jnp.where(tensor == 0, rows[:, 1], rows[:, 0])
    both = jnp.stack([a, b])
    one = both[:, 1]
    pieces = [one[t, :, 1536 + 192 * i : 1728 + 192 * i] for i in range(4) for t in range(2)]
    attn = jnp.concatenate(pieces + [one[0, :, 2304:], one[1, :, 2304:]], -1)
    units = jnp.concatenate([one[0, :, :768], one[1, :, :768], one[0, :, 768:1536], one[1, :, 768:1536]], -1)
    second = [lax.all_gather(group, ("z", "x"), axis=0) for group in (attn, units)]
    a, b = both[0, 0], both[1, 0]
    parts = [
        [a[:, 1536:1728], b[:, 1536:1728], a[:, :768]],
        [a[:, 1728:1920], b[:, 1728:1920], b[:, :768]],
        [a[:, 1920:2112], b[:, 1920:2112], a[:, 768:1536]],
        [a[:, 2112:2304], b[:, 2112:2304], a[:, 2304:], b[:, 2304:], b[:, 768:1536]],
    ]
    parts = [jnp.concatenate(part, -1)[None] for part in parts]
    for step in range(3):
        got = [exchange(part, ORDERS[i][step]) for i, part in enumerate(parts)]
        parts = [jnp.concatenate([x, y], 0) for x, y in zip(parts, got)]
    return parts, second


def gather_fourth(held):
    return [exchange(part, ORDERS[i][3]) for i, part in enumerate(held)]


def fold_kernel(fixed, outputs, *refs):
    terms, outs = refs[: len(fixed)], refs[len(fixed) :]
    for out, places in zip(outs, outputs):
        for sources, layer, start in places:
            total = None
            for term, index, first, width in sources:
                value = terms[term][(*index, *(0,) * fixed[term], slice(None), slice(None), slice(first, first + width))]
                total = value.astype(f32) if total is None else total + value.astype(f32)
            cols = slice(start, start + total.shape[-1])
            if layer is None:
                out[:, :, cols] = total.astype(bf16)
            else:
                out[layer, :, :, cols] = total.astype(bf16)


def fold(terms, outputs, layers, grid, name):
    arrays, specs, shapes, out_specs = [], [], [], []
    for array, bits in terms:
        lead, (n, rows, cols) = array.shape[:-3], array.shape[-3:]
        n >>= len(bits)
        arrays.append(array.reshape(*lead, *(2,) * len(bits), n, rows, cols))
        block = (*lead, *(1,) * len(bits), n // grid, rows, cols)
        specs.append(pl.BlockSpec(block, lambda b, at=(0,) * len(lead) + tuple(bits): (*at, b, 0, 0)))
    for places in outputs:
        width = max(start + sources[0][3] for sources, _, start in places)
        lead = () if layers is None else (layers,)
        shapes.append(jax.ShapeDtypeStruct((*lead, n, 48, width), bf16))
        out_specs.append(pl.BlockSpec((*lead, n // grid, 48, width), lambda b, at=(0,) * len(lead): (*at, b, 0, 0)))
    return pl.pallas_call(
        functools.partial(fold_kernel, [len(bits) for _, bits in terms], outputs),
        name=name,
        grid=(grid,),
        out_shape=shapes,
        in_specs=specs,
        out_specs=out_specs,
        cost_estimate=pl.CostEstimate(flops=1, bytes_accessed=1, transcendentals=0),
        compiler_params=pltpu.CompilerParams(vmem_limit_bytes=52 * 2**20),
    )(*arrays)


def send_parts(parts, step):
    return [exchange(part, ORDERS[i][step]) for i, part in enumerate(parts)]


def fold_attention(own, got):
    outputs = [[([(k, (), 384 * i, ATTN_COLS[i]) for k in range(2)], None, 0)] for i in range(4)]
    return fold([(own, (1,)), (got, (1,))], outputs, None, 2, "fold_attention")


def fold_units(own, got):
    outputs = [[([(k, (i,), 0, 768) for k in range(2)], None, 0)] for i in range(4)]
    return fold([(own, (1,)), (got, (1,))], outputs, None, 2, "fold_units")


def fold_both(groups, side):
    terms = []
    outputs = [[] for _ in range(4)]
    for units, (own, got, received) in enumerate(groups):
        base = len(terms)
        terms += [(own, (0, side)), (got, (0, side))] + [(part, (side,)) for part in received]
        for i in range(4):
            width = 768 if units else ATTN_COLS[i]
            index, first = ((i,), 0) if units else ((), 384 * i)
            sources = [(base, index, first, width), (base + 1, index, first, width), (base + 2 + i, (), 0, width)]
            outputs[i].append((sources, None, ATTN_COLS[i] * units))
    return fold(terms, outputs, None, 2, ("fold_both_kept", "fold_both_sent")[side])


def fold_on(kept, got, side, name):
    terms = [(part, (side,)) for pair in zip(kept, got) for part in pair]
    outputs = []
    for i in range(4):
        width = kept[i].shape[-1]
        outputs.append([([(2 * i + k, (), 0, width) for k in range(2)], None, 0)])
    return fold(terms, outputs, None, 1, name + ("_kept", "_sent")[side])


def collect_kernel(tensor_ref, *refs):
    kept, got, attn, units, out_ref = refs[:4], refs[4:8], refs[8], refs[9], refs[10]
    p = [x[0].astype(f32) + y[0].astype(f32) for x, y in zip(kept, got)]
    first = [part[:, : ATTN_COLS[i]] for i, part in enumerate(p)]
    wide = [part[:, ATTN_COLS[i] :] for i, part in enumerate(p)]
    layers = [
        (first, wide),
        (
            [attn[0, :, 384 * i : 384 * i + ATTN_COLS[i]].astype(f32) for i in range(4)],
            [units[0, :, 768 * i : 768 * i + 768].astype(f32) for i in range(4)],
        ),
    ]
    for layer, (first, wide) in enumerate(layers):
        for t in range(2):
            at = slice(192 * t, 192 * t + 192)
            values = [
                (0, wide[t]),
                (768, wide[2 + t]),
                (1536, jnp.concatenate([first[0][:, at], first[1][:, at]], 1)),
                (1920, jnp.concatenate([first[2][:, at], first[3][:, at]], 1)),
                (2304, first[3][:, 384 + 64 * t : 448 + 64 * t]),
            ]
            place = 4 * layer + 2 * (t ^ tensor_ref[0])
            for core in range(2):
                out = out_ref.at[place + core]
                for start, value in values:
                    out[:, start : start + value.shape[1]] = value[24 * core : 24 * core + 24].astype(bf16)


def finish_kernel(rows_ref, *refs):
    g_query, g_key, g_value, g_out, g_up, g_down, gb_query, gb_value = refs[:8]
    gb_up = refs[9]
    vectors = [refs[8], *refs[10:15]]
    small_ref = refs[15]
    halves = []
    for core in range(2):
        total = rows_ref[core].astype(f32)
        for k in range(1, 4):
            total = total + rows_ref[2 * k + core].astype(f32)
        halves.append(total)
        g_up[0, :, 768 * core : 768 * core + 768] = total[:, 0:768]
        g_down[0, :, 768 * core : 768 * core + 768] = total[:, 768:1536]
    for i, out in enumerate((g_query, g_key, g_value, g_out)):
        start = 1536 + 192 * i
        out[0] = jnp.concatenate([half[:, start : start + 192] for half in halves], 1)
    for out, lo, hi in ((gb_query, 8, 11), (gb_value, 11, 14), (gb_up, 14, 26)):
        out[0] = jnp.concatenate([half[0:2, 2304 + lo : 2304 + hi] for half in halves], 1)
    small_ref[...] = jnp.zeros_like(small_ref)
    small_ref[0:24, 0:64] = halves[0][:, 2304:2368]
    cols = small_ref[...].T
    for i, out in enumerate(vectors):
        out[...] = cols[i : i + 1, 0:24]


def scatter_end(kept, got, second):
    tensor = lax.axis_index("tensor").astype(jnp.int32).reshape(1)
    rows = kernel_call(collect_kernel, "collect", [tensor, *kept, *got, *second], [((8, 24, 2368), bf16)], scalar=True)[0]
    rows = lax.all_to_all(rows, ("pipe", "tensor", "core"), 0, 0, tiled=True)
    shapes = [(1, 24, 384)] * 4 + [(1, 24, 1536)] * 2 + [(1, 2, 6)] * 2 + [(1, 24), (1, 2, 24)] + [(1, 24)] * 5
    return kernel_call(
        finish_kernel, "finish", [rows], [(shape, f32) for shape in shapes], scratch=[pltpu.VMEM((128, 128), f32)]
    )


def share_outputs(first_rows, second_rows):
    pipe, tensor = lax.axis_index("pipe"), lax.axis_index("tensor")
    keep = jnp.where(pipe == 0, first_rows, second_rows)
    send = jnp.where(pipe == 0, second_rows, first_rows)
    return keep, exchange_tensor(keep), exchange_pipe(send), exchange_both(send)


def order_outputs(rows):
    pipe, tensor = lax.axis_index("pipe"), lax.axis_index("tensor")
    a, b, c, d = rows
    a, b = jnp.where(tensor == 0, a, b), jnp.where(tensor == 0, b, a)
    c, d = jnp.where(tensor == 0, c, d), jnp.where(tensor == 0, d, c)
    a, c = jnp.where(pipe == 0, a, c), jnp.where(pipe == 0, c, a)
    b, d = jnp.where(pipe == 0, b, d), jnp.where(pipe == 0, d, b)
    return jnp.stack([a, b, c, d])[None]


def local(clip_frames, out_cotangent, clip_lengths, *params):
    micro = lax.axis_index("pipe") * 2 + lax.axis_index("tensor")
    chip = lax.axis_index("z") * 4 + lax.axis_index("x")

    where = jnp.stack([chip, lax.axis_index("core")]).astype(jnp.int32)

    held, second = gather_start(params)
    got = gather_fourth(held)

    blocks = (chip ^ jnp.asarray(MASKS))[:, None]
    rows_at = (blocks * 48 + jnp.arange(48)[None]).reshape(-1)
    place_rows = (jnp.arange(768)[:, None] == rows_at[None]).astype(bf16)
    within = np.arange(48)
    units_at = np.where(within % 24 < 2, within // 24 * 2 + within % 24, 1000)
    units_at = (blocks * 4 + jnp.asarray(units_at)[None]).reshape(-1)
    place_units = (jnp.arange(64)[:, None] == units_at[None]).astype(bf16)
    place_back = (units_at[:, None] == jnp.arange(64)[None]).astype(bf16)

    frames = lax.dynamic_index_in_dim(clip_frames, micro, 0, keepdims=False)
    cotangent = lax.dynamic_index_in_dim(out_cotangent, micro, 0, keepdims=False)
    length = lax.dynamic_index_in_dim(clip_lengths, micro, 0, keepdims=False)
    x_first = dot(frames, place_rows).astype(bf16)
    grad_out = dot(cotangent, place_rows).astype(bf16)

    def placed_back(rows):
        return dot_cols(rows, place_rows).astype(bf16)

    attn_own = assemble(held, got, False)
    attn_own, got = pin(attn_own, got)
    attn_peer = exchange(attn_own, "c")
    units_own = assemble(held, got, True)
    attn_peer, units_own = pin(attn_peer, units_own)
    attn_first = attn_own, attn_peer
    units_first = units_own, exchange(units_own, "c")
    middle_first, heads_first, soft_first, mixed_first, vec_first, up_bias_first = attention_forward(
        length, x_first, attn_first, place_units
    )
    x_second, active_first, slope_first = units_forward(middle_first, units_first, vec_first, up_bias_first)
    x_second, second = pin(x_second, second)
    attn_own = place_blocks(where, second[0], False)
    attn_own, units_rows = pin(attn_own, second[1])
    attn_peer = exchange(attn_own, "c")
    units_own = place_blocks(where, units_rows, True)
    attn_peer, units_own = pin(attn_peer, units_own)
    attn_second = attn_own, attn_peer
    units_second = units_own, exchange(units_own, "c")
    middle_second, heads_second, soft_second, mixed_second, vec_second, up_bias_second = attention_forward(
        length, x_second, attn_second, place_units
    )
    out_second, active_second, slope_second = units_forward(middle_second, units_second, vec_second, up_bias_second)
    shared = share_outputs(placed_back(x_second), placed_back(out_second))

    shards = ("z", "x", "core")
    grad_middle, units_vec, up_bias_grad, units_placed = units_backward(
        grad_out, middle_second, active_second, slope_second, units_second, vec_second, where
    )
    units_total = lax.psum_scatter(units_placed, shards, scatter_dimension=0, tiled=True)
    second_grad, attn_placed = attention_backward(
        grad_middle, x_second, heads_second, soft_second, mixed_second, attn_second, vec_second, units_vec,
        up_bias_grad, place_back, where,
    )
    second_grad, attn_placed, shared = pin(second_grad, attn_placed, shared)
    attn_total = lax.psum_scatter(attn_placed, shards, scatter_dimension=0, tiled=True)
    section_output = order_outputs(shared)

    grad_middle, units_vec, up_bias_grad, units_own, units_peer = units_backward(
        second_grad, middle_first, active_first, slope_first, units_first, vec_first
    )
    units_got = exchange(units_peer, "c")
    attn = attention_backward(
        grad_middle, x_first, heads_first, soft_first, mixed_first, attn_first, vec_first, units_vec,
        up_bias_grad, place_back,
    )
    attn, units_got = pin(attn, units_got)
    first_grad, attn_own, attn_peer = attn
    units_fourth = send_parts(fold_units(units_own, units_got), 3)
    attn_got = exchange(attn_peer, "c")
    attn_fourth = send_parts(fold_attention(attn_own, attn_got), 3)
    input_grad = order_outputs(share_outputs(placed_back(first_grad), placed_back(second_grad)))

    groups = ((attn_own, attn_got, attn_fourth), (units_own, units_got, units_fourth))
    kept, got = fold_both(groups, 0), send_parts(fold_both(groups, 1), 2)
    kept, got = fold_on(kept, got, 0, "fold_four"), send_parts(fold_on(kept, got, 1, "fold_four"), 1)
    kept, got = fold_on(kept, got, 0, "fold_two"), send_parts(fold_on(kept, got, 1, "fold_two"), 0)
    return (section_output, input_grad, *scatter_end(kept, got, (attn_total, units_total)))


def solution(mesh):
    fine = Mesh(mesh.devices.reshape(2, 4, 4, 2, 2), ("pipe", "z", "x", "core", "tensor"))
    shard = ("z", "x", "core")
    rows = P(None, shard, None)
    matrix = P("pipe", shard, "tensor")
    vector = P("pipe", shard)
    params = (matrix,) * 8 + (vector, matrix) + (vector,) * 5
    return jax.shard_map(
        local,
        mesh=fine,
        in_specs=(rows, rows, P(None, shard)) + params,
        out_specs=(P("pipe", None, shard, None),) * 2 + params,
        check_vma=False,
    )
```

```python
import functools

import jax
import jax.numpy as jnp
import numpy as np
from jax import lax
from jax.experimental import pallas as pl
from jax.experimental.pallas import tpu as pltpu
from jax.sharding import Mesh
from jax.sharding import PartitionSpec as P

HEAD = 64
bf16 = jnp.bfloat16
f32 = jnp.float32

half_root = 0.7071067811865476
gauss_factor = 0.3989422804014327


EXCHANGES = {"xu": ("x", 4, 1), "xv": ("x", 4, 3), "zu": ("z", 4, 1), "zv": ("z", 4, 3), "c": ("core", 2, 1)}
BLOCK_BITS = ("zv", "zu", "xv", "xu")
BIT_MASK = {"xu": 1, "xv": 3, "zu": 4, "zv": 12}
ORDERS = (
    ("xu", "xv", "zu", "zv"),
    ("xv", "xu", "zv", "zu"),
    ("zu", "zv", "xu", "xv"),
    ("zv", "zu", "xv", "xu"),
)
MASKS = np.zeros(16, np.int32)
for _index in range(16):
    for _place, _bit in enumerate(BLOCK_BITS):
        if (_index >> (3 - _place)) & 1:
            MASKS[_index] ^= BIT_MASK[_bit]
ATTN_COLS = (384, 384, 384, 512)


def block_place(part, index):
    place = 0
    for step in range(4):
        if (index >> step) & 1:
            place += 8 >> BLOCK_BITS.index(ORDERS[part][step])
    return place


def dot(left_side, right_side):
    return lax.dot_general(left_side, right_side, (((1,), (0,)), ((), ())), preferred_element_type=f32)


def dot_rows(left_side, right_side):
    return lax.dot_general(left_side, right_side, (((0,), (0,)), ((), ())), preferred_element_type=f32)


def dot_cols(left_side, right_side):
    return lax.dot_general(left_side, right_side, (((1,), (1,)), ((), ())), preferred_element_type=f32)


def norm_parts(values):
    center = values - jnp.mean(values, -1, keepdims=True)
    rescale = lax.rsqrt(jnp.mean(center * center, -1, keepdims=True) + 1e-05)
    return center * rescale, rescale


def norm_backward(grad_rows, normed, rescale, norm_gain):
    scaled = grad_rows * norm_gain
    inner = (
        scaled
        - jnp.mean(scaled, -1, keepdims=True)
        - normed * jnp.mean(scaled * normed, -1, keepdims=True)
    )
    return rescale * inner


def put_blocks(out_ref, part, half, slot, start, value, where_ref):
    value = value.astype(bf16)
    for index in range(16):
        if where_ref is None:
            place = 48 * block_place(part, index)
            block = out_ref.at[index] if slot is None else out_ref.at[slot, index]
        else:
            place = 48 * index
            block = out_ref.at[2 * (where_ref[0] ^ int(MASKS[index])) + (where_ref[1] ^ half)]
        block[:, start : start + value.shape[1]] = value[place : place + 48]


def attention_forward_kernel(
    length_ref, x_ref, own_ref, peer_ref, place_ref,
    middle_ref, heads_ref, soft_ref, mixed_ref, vec_ref, up_bias_ref,
):
    length = length_ref[0]
    vec_ref[0:6] = own_ref[:, 1536:].astype(f32).T[0:6]
    units = []
    for weight_ref in (own_ref, peer_ref):
        rows = dot(place_ref[...], weight_ref[:, 1536:]).T
        units += [rows[:64], rows[64:]]
    for row, first in ((6, 8), (7, 11)):
        pieces = [rows[first + i : first + i + 1] for rows in units for i in range(3)]
        vec_ref[row : row + 1] = jnp.concatenate(pieces, 1)
    pieces = [rows[14 + i : 15 + i] for rows in units for i in range(12)]
    for i in range(24):
        up_bias_ref[0:1, 128 * i : 128 * i + 128] = jnp.concatenate(pieces[2 * i : 2 * i + 2], 1)
    normed, _ = norm_parts(x_ref[...].astype(f32))
    normed_b = (normed * vec_ref[2:3] + vec_ref[3:4]).astype(bf16)
    for j in range(3):
        for half, weight_ref in enumerate((own_ref, peer_ref)):
            cols = slice(384 * half, 384 * half + 384)
            rows = dot(normed_b, weight_ref[:, 384 * j : 384 * j + 384])
            if j != 1:
                rows = rows + vec_ref[6 + j // 2 : 7 + j // 2, cols]
            heads_ref[j, :, cols] = rows.astype(bf16)
    count = x_ref.shape[0]
    live_keys = lax.broadcasted_iota(jnp.int32, (count, count), 1) < length
    for pair in range(6):
        both = []
        for head in (2 * pair, 2 * pair + 1):
            cols = slice(HEAD * head, HEAD * head + HEAD)
            scores = dot_cols(heads_ref[0, :, cols], heads_ref[1, :, cols]) * HEAD ** (-0.5)
            scores = jnp.where(live_keys, scores, -1e30)
            powers = jnp.exp(scores - jnp.max(scores, -1, keepdims=True))
            soft = powers / jnp.sum(powers, -1, keepdims=True)
            soft_ref[head] = soft
            both.append(dot(soft.astype(bf16), heads_ref[2, :, cols]))
        mixed_ref[:, 128 * pair : 128 * pair + 128] = jnp.concatenate(both, 1).astype(bf16)
    total = dot_cols(mixed_ref[:, :384], own_ref[:, 1152:1536])
    total = total + dot_cols(mixed_ref[:, 384:], peer_ref[:, 1152:1536])
    middle_ref[...] = x_ref[...].astype(f32) + total + vec_ref[0:1]


def units_forward_kernel(middle_ref, own_ref, peer_ref, vec_ref, up_bias_ref, result_ref, active_ref, slope_ref):
    middle = middle_ref[...]
    normed, _ = norm_parts(middle)
    normed_b = (normed * vec_ref[4:5] + vec_ref[5:6]).astype(bf16)
    total = middle + vec_ref[1:2]
    for half, weight_ref in enumerate((own_ref, peer_ref)):
        for j in range(2):
            cols = slice(768 * (2 * half + j), 768 * (2 * half + j) + 768)
            pre_active = dot(normed_b, weight_ref[j]) + up_bias_ref[0:1, cols]
            below = 0.5 * (1.0 + lax.erf(pre_active * half_root))
            active_b = (pre_active * below).astype(bf16)
            active_ref[:, cols] = active_b
            slope_ref[:, cols] = below + pre_active * jnp.exp(-0.5 * pre_active * pre_active) * gauss_factor
            total = total + dot_cols(active_b, weight_ref[2 + j])
    result_ref[...] = total.astype(bf16)


def units_backward_kernel(placed, *refs):
    where_ref, refs = (refs[0], refs[1:]) if placed else (None, refs)
    grad_ref, middle_ref, active_ref, slope_ref, own_ref, peer_ref, vec_ref = refs[:7]
    grad_middle_ref, vec_grad_ref, up_bias_grad_ref = refs[7:10]
    grad_own_ref, grad_peer_ref = (refs[11], refs[11]) if placed else refs[10:12]
    grad_b = grad_ref[...]
    grad_rows = grad_b.astype(f32)
    normed, rescale = norm_parts(middle_ref[...])
    normed_b = (normed * vec_ref[4:5] + vec_ref[5:6]).astype(bf16)
    normed_t = normed_b.T
    grad_t = grad_b.T
    grad_normed = None
    for half, weight_ref, out_ref in ((1, peer_ref, grad_peer_ref), (0, own_ref, grad_own_ref)):
        for j in range(2):
            cols = slice(768 * (2 * half + j), 768 * (2 * half + j) + 768)
            slot, start = (None, 768 * j) if placed else (j, 0)
            value = dot(grad_t, active_ref[:, cols])
            put_blocks(out_ref, 2 + j, half, None if placed else 2 + j, 1536 + start if placed else 0, value, where_ref)
            grad_upper = (dot(grad_b, weight_ref[2 + j]) * slope_ref[:, cols]).astype(bf16)
            up_bias_grad_ref[0:1, cols] = jnp.sum(grad_upper.astype(f32), 0, keepdims=True)
            put_blocks(out_ref, j, half, slot, start, dot(normed_t, grad_upper), where_ref)
            term = dot_cols(grad_upper, weight_ref[j])
            grad_normed = term if grad_normed is None else grad_normed + term
    grad_middle = grad_rows + norm_backward(grad_normed, normed, rescale, vec_ref[4:5])
    grad_middle_ref[...] = grad_middle
    vec_grad_ref[...] = jnp.zeros_like(vec_grad_ref)
    vec_grad_ref[0:1] = jnp.sum(grad_middle, 0, keepdims=True)
    vec_grad_ref[1:2] = jnp.sum(grad_rows, 0, keepdims=True)
    vec_grad_ref[4:5] = jnp.sum(grad_normed * normed, 0, keepdims=True)
    vec_grad_ref[5:6] = jnp.sum(grad_normed, 0, keepdims=True)
    if placed:
        copy = pltpu.make_async_copy(grad_own_ref, refs[10].at[:, :, pl.ds(1664, 3072)], refs[12])
        copy.start()
        copy.wait()


def attention_backward_kernel(placed, *refs):
    where_ref, refs = (refs[0], refs[1:]) if placed else (None, refs)
    grad_ref, x_ref, heads_ref, soft_ref, mixed_ref, own_ref, peer_ref, vec_ref = refs[:8]
    units_vec_ref, up_bias_grad_ref, place_ref = refs[8:11]
    refs = refs[12:] if placed else refs[11:]
    grad_in_ref, grad_mixed_ref, grad_heads_ref, cols_ref, small_ref = refs[0], *refs[-4:]
    grad_own_ref, grad_peer_ref = (refs[2], refs[2]) if placed else refs[1:3]
    grad_b = grad_ref[...].astype(bf16)
    grad_t = grad_b.T
    grad_mixed_ref[:, :384] = dot(grad_b, own_ref[:, 1152:1536]).astype(bf16)
    grad_mixed_ref[:, 384:] = dot(grad_b, peer_ref[:, 1152:1536]).astype(bf16)
    factor = HEAD ** (-0.5)
    for pair in range(6):
        found = ([], [], [])
        for head in (2 * pair, 2 * pair + 1):
            cols = slice(HEAD * head, HEAD * head + HEAD)
            soft = soft_ref[head]
            grad_head = grad_mixed_ref[:, cols]
            grad_soft = dot_cols(grad_head, heads_ref[2, :, cols])
            inner = jnp.sum(grad_soft * soft, -1, keepdims=True)
            grad_scores = (soft * (grad_soft - inner)).astype(bf16)
            found[0].append(dot(grad_scores, heads_ref[1, :, cols]) * factor)
            found[1].append(dot_rows(grad_scores, heads_ref[0, :, cols]) * factor)
            found[2].append(dot_rows(soft.astype(bf16), grad_head))
        for j in range(3):
            grad_heads_ref[j, :, 128 * pair : 128 * pair + 128] = jnp.concatenate(found[j], 1).astype(bf16)
    normed, rescale = norm_parts(x_ref[...].astype(f32))
    normed_b = (normed * vec_ref[2:3] + vec_ref[3:4]).astype(bf16)
    normed_t = normed_b.T
    grad_normed = None
    for half, weight_ref, out_ref in ((1, peer_ref, grad_peer_ref), (0, own_ref, grad_own_ref)):
        for j in range(3):
            rows = grad_heads_ref[j, :, 384 * half : 384 * half + 384]
            put_blocks(out_ref, j, half, None, 384 * j, dot(normed_t, rows), where_ref)
            term = dot_cols(rows, weight_ref[:, 384 * j : 384 * j + 384])
            grad_normed = term if grad_normed is None else grad_normed + term
    grad_in = grad_ref[...] + norm_backward(grad_normed, normed, rescale, vec_ref[2:3])
    grad_in_ref[...] = grad_in.astype(bf16)
    cols_ref[...] = jnp.zeros_like(cols_ref)
    cols_ref[0:2] = units_vec_ref[0:2]
    cols_ref[2:3] = jnp.sum(grad_normed * normed, 0, keepdims=True)
    cols_ref[3:4] = jnp.sum(grad_normed, 0, keepdims=True)
    cols_ref[4:6] = units_vec_ref[4:6]
    cols_ref[64:70] = cols_ref[0:6]
    cols = cols_ref[...].T
    query_bias = jnp.sum(grad_heads_ref[0].astype(f32), 0, keepdims=True)
    value_bias = jnp.sum(grad_heads_ref[2].astype(f32), 0, keepdims=True)
    for half, out_ref in ((1, grad_peer_ref), (0, grad_own_ref)):
        small_ref[...] = jnp.zeros_like(small_ref)
        for t in range(2):
            base = 64 * t
            for i in range(3):
                at = HEAD * (6 * half + 3 * t + i)
                small_ref[base + 8 + i : base + 9 + i] = query_bias[:, at : at + HEAD]
                small_ref[base + 11 + i : base + 12 + i] = value_bias[:, at : at + HEAD]
            for i in range(12):
                at = HEAD * (24 * half + 12 * t + i)
                small_ref[base + 14 + i : base + 15 + i] = up_bias_grad_ref[0:1, at : at + HEAD]
        small = dot_cols(place_ref[...], small_ref[...].astype(bf16)) + cols
        weight = dot(grad_t, mixed_ref[:, 384 * half : 384 * half + 384])
        put_blocks(out_ref, 3, half, None, 1152, jnp.concatenate([weight, small], 1), where_ref)
    if placed:
        copy = pltpu.make_async_copy(grad_own_ref, refs[1].at[:, :, pl.ds(0, 1664)], refs[3])
        copy.start()
        copy.wait()


def kernel_call(kernel, name, inputs, outputs, scratch=(), scalar=False, blocks=None, large=True, apart=None, aliases=None):
    whole = pl.BlockSpec(memory_space=pltpu.VMEM)
    specs = [whole] * len(inputs)
    out_specs = [whole] * len(outputs)
    if blocks is not None:
        specs = [pl.BlockSpec(shape, lambda i, at=at: at) for shape, at in blocks]
        out_specs = [pl.BlockSpec(shape, lambda i, n=len(shape): (0,) * n) for shape, _ in outputs]
    if scalar:
        specs[0] = pl.BlockSpec(memory_space=pltpu.SMEM)
    if apart is not None:
        out_specs[apart] = pl.BlockSpec(memory_space=pl.ANY)
    for number in aliases or {}:
        specs[number] = pl.BlockSpec(memory_space=pl.ANY)
    shapes = [jax.ShapeDtypeStruct(shape, dtype) for shape, dtype in outputs]
    return pl.pallas_call(
        kernel,
        name=name,
        out_shape=shapes,
        in_specs=specs,
        out_specs=out_specs,
        grid=() if blocks is None else (1,),
        input_output_aliases=aliases or {},
        scratch_shapes=list(scratch),
        cost_estimate=pl.CostEstimate(flops=1, bytes_accessed=1, transcendentals=0),
        compiler_params=pltpu.CompilerParams(vmem_limit_bytes=52 * 2**20 if large else None),
    )(*inputs)


ROWS = (192, 768)
HEADS_SHAPE = (3, 192, 768)
UNITS_SHAPE = (4, 16, 48, 768)
ATTN_SHAPE = (16, 48, 1664)
PLACED_SHAPE = (32, 48, 4736)


def attention_forward(length, x, attn, place_units):
    own, peer = attn
    return kernel_call(
        attention_forward_kernel, "attention_forward",
        [length, x, own, peer, place_units],
        [(ROWS, f32), (HEADS_SHAPE, bf16), ((12, 192, 192), f32), (ROWS, bf16), ((8, 768), f32), ((1, 3072), f32)],
        scalar=True,
    )


def units_forward(middle, units, vec, up_bias):
    own, peer = units
    return kernel_call(
        units_forward_kernel, "units_forward", [middle, own, peer, vec, up_bias],
        [(ROWS, bf16), ((192, 3072), bf16), ((192, 3072), f32)],
    )


def units_backward(grad_b, middle, active, slope, units, vec, where=None):
    own, peer = units
    placed = where is not None
    shapes = [PLACED_SHAPE] if placed else [UNITS_SHAPE] * 2
    return kernel_call(
        functools.partial(units_backward_kernel, placed), "units_backward",
        [where] * placed + [grad_b, middle, active, slope, own, peer, vec],
        [(ROWS, f32), ((8, 768), f32), ((1, 3072), f32)] + [(shape, bf16) for shape in shapes], scalar=placed,
        scratch=[pltpu.VMEM((32, 48, 3072), bf16), pltpu.SemaphoreType.DMA(())] * placed,
        apart=3 if placed else None,
    )


def attention_backward(
    grad_middle, x, heads, soft, mixed, attn, vec, units_vec, up_bias_grad, place_units, where=None, placed_units=None
):
    own, peer = attn
    placed = where is not None
    shapes = [PLACED_SHAPE] if placed else [ATTN_SHAPE] * 2
    return kernel_call(
        functools.partial(attention_backward_kernel, placed), "attention_backward",
        [where] * placed
        + [grad_middle, x, heads, soft, mixed, own, peer, vec, units_vec, up_bias_grad, place_units]
        + [placed_units] * placed,
        [(ROWS, bf16)] + [(shape, bf16) for shape in shapes], scalar=placed,
        scratch=[pltpu.VMEM((32, 48, 1664), bf16), pltpu.SemaphoreType.DMA(())] * placed
        + [
            pltpu.VMEM(ROWS, bf16), pltpu.VMEM(HEADS_SHAPE, bf16), pltpu.VMEM((128, 768), f32),
            pltpu.VMEM((128, 64), f32),
        ],
        apart=1 if placed else None, aliases={12: 1} if placed else None,
    )


def exchange(value, bit):
    axis, size, flip = EXCHANGES[bit]
    return lax.ppermute(value, axis, [(i, i ^ flip) for i in range(size)])


def exchange_pipe(value):
    return lax.ppermute(value, "pipe", [(0, 1), (1, 0)])


def exchange_both(value):
    return lax.ppermute(value, ("pipe", "tensor"), [(i, i ^ 3) for i in range(4)])


def exchange_tensor(value):
    return lax.ppermute(value, "tensor", [(0, 1), (1, 0)])


def pin(*values):
    return lax.optimization_barrier(values)


def assemble_kernel(slots, *refs):
    count = len(slots)
    out = refs[-1]
    for number, (part, slot, start) in enumerate(slots):
        for index in range(16):
            rows = refs[number + (0 if index < 8 else count)][index % 8]
            place = slice(48 * block_place(part, index), 48 * block_place(part, index) + 48)
            cols = slice(start, start + rows.shape[1])
            if slot is None:
                out[place, cols] = rows
            else:
                out[slot, place, cols] = rows


def assemble(held, got, units):
    inputs, blocks, slots = [], [], []
    for part in range(4):
        width = (384, 256)[part // 3] if units else ATTN_COLS[part]
        first = ATTN_COLS[part] // width if units else 0
        for k in range(768 // width if units else 1):
            inputs.append(part)
            blocks.append(((8, 48, width), (0, 0, first + k)))
            slots.append((part, part, width * k) if units else (part, None, 384 * part))
    arrays = [held[part] for part in inputs] + [got[part] for part in inputs]
    shape = (4, 768, 768) if units else (768, 1664)
    kernel = functools.partial(assemble_kernel, slots)
    name = "assemble_units" if units else "assemble_attention"
    return kernel_call(kernel, name, arrays, [(shape, bf16)], blocks=blocks * 2)[0]


def place_kernel(chip_ref, rows_ref, out_ref):
    for index in range(16):
        block = rows_ref.at[chip_ref[0] ^ int(MASKS[index])]
        place = slice(48 * index, 48 * index + 48)
        if len(out_ref.shape) == 2:
            out_ref[place] = block[:, :1664]
        else:
            for j in range(4):
                out_ref[j, place] = block[:, 1664 + 768 * j : 2432 + 768 * j]


def place_blocks(where, rows, units):
    shape = (4, 768, 768) if units else (768, 1664)
    name = "place_units" if units else "place_attention"
    return kernel_call(place_kernel, name, [where, rows], [(shape, bf16)], scalar=True)[0]


def pack_kernel(*refs):
    w_query, w_key, w_value, w_out, w_up, w_down, b_query, b_value = refs[:8]
    b_up = refs[9]
    vectors = [refs[8], *refs[10:15]]
    out_ref, vec_ref, small_ref = refs[15:]
    vec_ref[...] = jnp.zeros_like(vec_ref)
    for i, vector in enumerate(vectors):
        vec_ref[i : i + 1, 0:24] = vector[...].astype(f32)
    cols = vec_ref[...].T[0:24, 0:8]
    for half in range(2):
        small_ref[...] = jnp.zeros_like(small_ref)
        small_ref[:, 0:8] = cols
        small_ref[0:2, 8:11] = b_query[0, :, 3 * half : 3 * half + 3].astype(f32)
        small_ref[0:2, 11:14] = b_value[0, :, 3 * half : 3 * half + 3].astype(f32)
        small_ref[0:2, 14:26] = b_up[0, :, 12 * half : 12 * half + 12].astype(f32)
        small = small_ref[...].astype(bf16)
        wide, whole = slice(768 * half, 768 * half + 768), slice(192 * half, 192 * half + 192)
        first = jnp.concatenate([w_query[0, :, whole].astype(f32), w_key[0, :, whole].astype(f32)], 1).astype(bf16)
        second = jnp.concatenate([w_value[0, :, whole].astype(f32), w_out[0, :, whole].astype(f32)], 1).astype(bf16)
        for k in range(4):
            out = out_ref.at[2 * k + half]
            out[:, 0:768] = w_up[0, :, wide]
            out[:, 768:1536] = w_down[0, :, wide]
            out[:, 1536:1920] = first
            out[:, 1920:2304] = second
            out[:, 2304:2368] = small


def gather_start(params):
    tensor = lax.axis_index("tensor")
    rows = kernel_call(
        pack_kernel, "pack", list(params), [((8, 24, 2368), bf16)],
        scratch=[pltpu.VMEM((8, 128), f32), pltpu.VMEM((24, 64), f32)],
        blocks=[(param.shape, (0,) * param.ndim) for param in params], large=False,
    )[0]
    rows = lax.all_to_all(rows, ("pipe", "tensor", "core"), 0, 0, tiled=True)
    rows = rows.reshape(2, 2, 48, 2368)
    a = jnp.where(tensor == 0, rows[:, 0], rows[:, 1])
    b = jnp.where(tensor == 0, rows[:, 1], rows[:, 0])
    both = jnp.stack([a, b])
    one = both[:, 1]
    pieces = [one[t, :, 1536 + 192 * i : 1728 + 192 * i] for i in range(4) for t in range(2)]
    pieces += [one[0, :, 2304:], one[1, :, 2304:]]
    pieces += [one[0, :, :768], one[1, :, :768], one[0, :, 768:1536], one[1, :, 768:1536]]
    second = lax.all_gather(jnp.concatenate(pieces, -1), ("z", "x"), axis=0)
    a, b = both[0, 0], both[1, 0]
    parts = [
        [a[:, 1536:1728], b[:, 1536:1728], a[:, :768]],
        [a[:, 1728:1920], b[:, 1728:1920], b[:, :768]],
        [a[:, 1920:2112], b[:, 1920:2112], a[:, 768:1536]],
        [a[:, 2112:2304], b[:, 2112:2304], a[:, 2304:], b[:, 2304:], b[:, 768:1536]],
    ]
    parts = [jnp.concatenate(part, -1)[None] for part in parts]
    for step in range(3):
        got = [exchange(part, ORDERS[i][step]) for i, part in enumerate(parts)]
        parts = [jnp.concatenate([x, y], 0) for x, y in zip(parts, got)]
    return parts, second


def gather_fourth(held):
    return [exchange(part, ORDERS[i][3]) for i, part in enumerate(held)]


def fold_kernel(fixed, outputs, *refs):
    terms, outs = refs[: len(fixed)], refs[len(fixed) :]
    for out, places in zip(outs, outputs):
        for sources, layer, start in places:
            total = None
            for term, index, first, width in sources:
                value = terms[term][(*index, *(0,) * fixed[term], slice(None), slice(None), slice(first, first + width))]
                total = value.astype(f32) if total is None else total + value.astype(f32)
            cols = slice(start, start + total.shape[-1])
            if layer is None:
                out[:, :, cols] = total.astype(bf16)
            else:
                out[layer, :, :, cols] = total.astype(bf16)


def fold(terms, outputs, layers, grid, name):
    arrays, specs, shapes, out_specs = [], [], [], []
    for array, bits in terms:
        lead, (n, rows, cols) = array.shape[:-3], array.shape[-3:]
        n >>= len(bits)
        arrays.append(array.reshape(*lead, *(2,) * len(bits), n, rows, cols))
        block = (*lead, *(1,) * len(bits), n // grid, rows, cols)
        specs.append(pl.BlockSpec(block, lambda b, at=(0,) * len(lead) + tuple(bits): (*at, b, 0, 0)))
    for places in outputs:
        width = max(start + sources[0][3] for sources, _, start in places)
        lead = () if layers is None else (layers,)
        shapes.append(jax.ShapeDtypeStruct((*lead, n, 48, width), bf16))
        out_specs.append(pl.BlockSpec((*lead, n // grid, 48, width), lambda b, at=(0,) * len(lead): (*at, b, 0, 0)))
    return pl.pallas_call(
        functools.partial(fold_kernel, [len(bits) for _, bits in terms], outputs),
        name=name,
        grid=(grid,),
        out_shape=shapes,
        in_specs=specs,
        out_specs=out_specs,
        cost_estimate=pl.CostEstimate(flops=1, bytes_accessed=1, transcendentals=0),
        compiler_params=pltpu.CompilerParams(vmem_limit_bytes=52 * 2**20),
    )(*arrays)


def send_parts(parts, step):
    return [exchange(part, ORDERS[i][step]) for i, part in enumerate(parts)]


def fold_attention(own, got):
    outputs = [[([(k, (), 384 * i, ATTN_COLS[i]) for k in range(2)], None, 0)] for i in range(4)]
    return fold([(own, (1,)), (got, (1,))], outputs, None, 2, "fold_attention")


def fold_units(own, got):
    outputs = [[([(k, (i,), 0, 768) for k in range(2)], None, 0)] for i in range(4)]
    return fold([(own, (1,)), (got, (1,))], outputs, None, 2, "fold_units")


def fold_both(groups, side):
    terms = []
    outputs = [[] for _ in range(4)]
    for units, (own, got, received) in enumerate(groups):
        base = len(terms)
        terms += [(own, (0, side)), (got, (0, side))] + [(part, (side,)) for part in received]
        for i in range(4):
            width = 768 if units else ATTN_COLS[i]
            index, first = ((i,), 0) if units else ((), 384 * i)
            sources = [(base, index, first, width), (base + 1, index, first, width), (base + 2 + i, (), 0, width)]
            outputs[i].append((sources, None, ATTN_COLS[i] * units))
    return fold(terms, outputs, None, 2, ("fold_both_kept", "fold_both_sent")[side])


def fold_on(kept, got, side, name):
    terms = [(part, (side,)) for pair in zip(kept, got) for part in pair]
    outputs = []
    for i in range(4):
        width = kept[i].shape[-1]
        outputs.append([([(2 * i + k, (), 0, width) for k in range(2)], None, 0)])
    return fold(terms, outputs, None, 1, name + ("_kept", "_sent")[side])


def collect_kernel(tensor_ref, *refs):
    kept, got, second, out_ref = refs[:4], refs[4:8], refs[8], refs[9]
    p = [x[0].astype(f32) + y[0].astype(f32) for x, y in zip(kept, got)]
    first = [part[:, : ATTN_COLS[i]] for i, part in enumerate(p)]
    wide = [part[:, ATTN_COLS[i] :] for i, part in enumerate(p)]
    layers = [
        (first, wide),
        (
            [second[0, :, 384 * i : 384 * i + ATTN_COLS[i]].astype(f32) for i in range(4)],
            [second[0, :, 1664 + 768 * i : 2432 + 768 * i].astype(f32) for i in range(4)],
        ),
    ]
    for layer, (first, wide) in enumerate(layers):
        for t in range(2):
            at = slice(192 * t, 192 * t + 192)
            values = [
                (0, wide[t]),
                (768, wide[2 + t]),
                (1536, jnp.concatenate([first[0][:, at], first[1][:, at]], 1)),
                (1920, jnp.concatenate([first[2][:, at], first[3][:, at]], 1)),
                (2304, first[3][:, 384 + 64 * t : 448 + 64 * t]),
            ]
            place = 4 * layer + 2 * (t ^ tensor_ref[0])
            for core in range(2):
                out = out_ref.at[place + core]
                for start, value in values:
                    out[:, start : start + value.shape[1]] = value[24 * core : 24 * core + 24].astype(bf16)


def finish_kernel(rows_ref, *refs):
    g_query, g_key, g_value, g_out, g_up, g_down, gb_query, gb_value = refs[:8]
    gb_up = refs[9]
    vectors = [refs[8], *refs[10:15]]
    small_ref = refs[15]
    halves = []
    for core in range(2):
        total = rows_ref[core].astype(f32)
        for k in range(1, 4):
            total = total + rows_ref[2 * k + core].astype(f32)
        halves.append(total)
        g_up[0, :, 768 * core : 768 * core + 768] = total[:, 0:768]
        g_down[0, :, 768 * core : 768 * core + 768] = total[:, 768:1536]
    for i, out in enumerate((g_query, g_key, g_value, g_out)):
        start = 1536 + 192 * i
        out[0] = jnp.concatenate([half[:, start : start + 192] for half in halves], 1)
    for out, lo, hi in ((gb_query, 8, 11), (gb_value, 11, 14), (gb_up, 14, 26)):
        out[0] = jnp.concatenate([half[0:2, 2304 + lo : 2304 + hi] for half in halves], 1)
    small_ref[...] = jnp.zeros_like(small_ref)
    small_ref[0:24, 0:64] = halves[0][:, 2304:2368]
    cols = small_ref[...].T
    for i, out in enumerate(vectors):
        out[...] = cols[i : i + 1, 0:24]


def scatter_end(kept, got, second):
    tensor = lax.axis_index("tensor").astype(jnp.int32).reshape(1)
    rows = kernel_call(collect_kernel, "collect", [tensor, *kept, *got, second], [((8, 24, 2368), bf16)], scalar=True)[0]
    rows = lax.all_to_all(rows, ("pipe", "tensor", "core"), 0, 0, tiled=True)
    shapes = [(1, 24, 384)] * 4 + [(1, 24, 1536)] * 2 + [(1, 2, 6)] * 2 + [(1, 24), (1, 2, 24)] + [(1, 24)] * 5
    return kernel_call(
        finish_kernel, "finish", [rows], [(shape, f32) for shape in shapes], scratch=[pltpu.VMEM((128, 128), f32)]
    )


def share_outputs(first_rows, second_rows):
    pipe, tensor = lax.axis_index("pipe"), lax.axis_index("tensor")
    keep = jnp.where(pipe == 0, first_rows, second_rows)
    send = jnp.where(pipe == 0, second_rows, first_rows)
    return keep, exchange_tensor(keep), exchange_pipe(send), exchange_both(send)


def order_outputs(rows):
    pipe, tensor = lax.axis_index("pipe"), lax.axis_index("tensor")
    a, b, c, d = rows
    a, b = jnp.where(tensor == 0, a, b), jnp.where(tensor == 0, b, a)
    c, d = jnp.where(tensor == 0, c, d), jnp.where(tensor == 0, d, c)
    a, c = jnp.where(pipe == 0, a, c), jnp.where(pipe == 0, c, a)
    b, d = jnp.where(pipe == 0, b, d), jnp.where(pipe == 0, d, b)
    return jnp.stack([a, b, c, d])[None]


def local(clip_frames, out_cotangent, clip_lengths, *params):
    micro = lax.axis_index("pipe") * 2 + lax.axis_index("tensor")
    chip = lax.axis_index("z") * 4 + lax.axis_index("x")

    where = jnp.stack([chip, lax.axis_index("core")]).astype(jnp.int32)

    held, second = gather_start(params)
    got = gather_fourth(held)

    blocks = (chip ^ jnp.asarray(MASKS))[:, None]
    rows_at = (blocks * 48 + jnp.arange(48)[None]).reshape(-1)
    place_rows = (jnp.arange(768)[:, None] == rows_at[None]).astype(bf16)
    within = np.arange(48)
    units_at = np.where(within % 24 < 2, within // 24 * 2 + within % 24, 1000)
    units_at = (blocks * 4 + jnp.asarray(units_at)[None]).reshape(-1)
    place_units = (jnp.arange(64)[:, None] == units_at[None]).astype(bf16)
    place_back = (units_at[:, None] == jnp.arange(64)[None]).astype(bf16)

    frames = lax.dynamic_index_in_dim(clip_frames, micro, 0, keepdims=False)
    cotangent = lax.dynamic_index_in_dim(out_cotangent, micro, 0, keepdims=False)
    length = lax.dynamic_index_in_dim(clip_lengths, micro, 0, keepdims=False)
    x_first = dot(frames, place_rows).astype(bf16)
    grad_out = dot(cotangent, place_rows).astype(bf16)

    def placed_back(rows):
        return dot_cols(rows, place_rows).astype(bf16)

    attn_own = assemble(held, got, False)
    attn_own, got = pin(attn_own, got)
    attn_peer = exchange(attn_own, "c")
    units_own = assemble(held, got, True)
    attn_peer, units_own = pin(attn_peer, units_own)
    attn_first = attn_own, attn_peer
    units_first = units_own, exchange(units_own, "c")
    middle_first, heads_first, soft_first, mixed_first, vec_first, up_bias_first = attention_forward(
        length, x_first, attn_first, place_units
    )
    x_second, active_first, slope_first = units_forward(middle_first, units_first, vec_first, up_bias_first)
    x_second, second = pin(x_second, second)
    attn_own = place_blocks(where, second, False)
    attn_own, second = pin(attn_own, second)
    attn_peer = exchange(attn_own, "c")
    units_own = place_blocks(where, second, True)
    attn_peer, units_own = pin(attn_peer, units_own)
    attn_second = attn_own, attn_peer
    units_second = units_own, exchange(units_own, "c")
    middle_second, heads_second, soft_second, mixed_second, vec_second, up_bias_second = attention_forward(
        length, x_second, attn_second, place_units
    )
    out_second, active_second, slope_second = units_forward(middle_second, units_second, vec_second, up_bias_second)
    shared = share_outputs(placed_back(x_second), placed_back(out_second))

    shards = ("z", "x", "core")
    grad_middle, units_vec, up_bias_grad, units_placed = units_backward(
        grad_out, middle_second, active_second, slope_second, units_second, vec_second, where
    )
    second_grad, placed = attention_backward(
        grad_middle, x_second, heads_second, soft_second, mixed_second, attn_second, vec_second, units_vec,
        up_bias_grad, place_back, where, units_placed,
    )
    second_grad, placed, shared = pin(second_grad, placed, shared)
    second_total = lax.psum_scatter(placed, shards, scatter_dimension=0, tiled=True)
    section_output = order_outputs(shared)

    grad_middle, units_vec, up_bias_grad, units_own, units_peer = units_backward(
        second_grad, middle_first, active_first, slope_first, units_first, vec_first
    )
    units_got = exchange(units_peer, "c")
    attn = attention_backward(
        grad_middle, x_first, heads_first, soft_first, mixed_first, attn_first, vec_first, units_vec,
        up_bias_grad, place_back,
    )
    attn, units_got = pin(attn, units_got)
    first_grad, attn_own, attn_peer = attn
    units_fourth = send_parts(fold_units(units_own, units_got), 3)
    attn_got = exchange(attn_peer, "c")
    attn_fourth = send_parts(fold_attention(attn_own, attn_got), 3)
    input_grad = order_outputs(share_outputs(placed_back(first_grad), placed_back(second_grad)))

    groups = ((attn_own, attn_got, attn_fourth), (units_own, units_got, units_fourth))
    kept, got = fold_both(groups, 0), send_parts(fold_both(groups, 1), 2)
    kept, got = fold_on(kept, got, 0, "fold_four"), send_parts(fold_on(kept, got, 1, "fold_four"), 1)
    kept, got = fold_on(kept, got, 0, "fold_two"), send_parts(fold_on(kept, got, 1, "fold_two"), 0)
    return (section_output, input_grad, *scatter_end(kept, got, second_total))


def solution(mesh):
    fine = Mesh(mesh.devices.reshape(2, 4, 4, 2, 2), ("pipe", "z", "x", "core", "tensor"))
    shard = ("z", "x", "core")
    rows = P(None, shard, None)
    matrix = P("pipe", shard, "tensor")
    vector = P("pipe", shard)
    params = (matrix,) * 8 + (vector, matrix) + (vector,) * 5
    return jax.shard_map(
        local,
        mesh=fine,
        in_specs=(rows, rows, P(None, shard)) + params,
        out_specs=(P("pipe", None, shard, None),) * 2 + params,
        check_vma=False,
    )
```

```python
import functools

import jax
import jax.numpy as jnp
import numpy as np
from jax import lax
from jax.experimental import pallas as pl
from jax.experimental.pallas import tpu as pltpu
from jax.sharding import Mesh
from jax.sharding import PartitionSpec as P

HEAD = 64
bf16 = jnp.bfloat16
f32 = jnp.float32

half_root = 0.7071067811865476
gauss_factor = 0.3989422804014327


EXCHANGES = {"xu": ("x", 4, 1), "xv": ("x", 4, 3), "zu": ("z", 4, 1), "zv": ("z", 4, 3), "c": ("core", 2, 1)}
BLOCK_BITS = ("zv", "zu", "xv", "xu")
BIT_MASK = {"xu": 1, "xv": 3, "zu": 4, "zv": 12}
ORDERS = (
    ("xu", "xv", "zu", "zv"),
    ("xv", "xu", "zv", "zu"),
    ("zu", "zv", "xu", "xv"),
    ("zv", "zu", "xv", "xu"),
)
MASKS = np.zeros(16, np.int32)
for _index in range(16):
    for _place, _bit in enumerate(BLOCK_BITS):
        if (_index >> (3 - _place)) & 1:
            MASKS[_index] ^= BIT_MASK[_bit]
ATTN_COLS = (384, 384, 384, 512)


def block_place(part, index):
    place = 0
    for step in range(4):
        if (index >> step) & 1:
            place += 8 >> BLOCK_BITS.index(ORDERS[part][step])
    return place


def dot(left_side, right_side):
    return lax.dot_general(left_side, right_side, (((1,), (0,)), ((), ())), preferred_element_type=f32)


def dot_rows(left_side, right_side):
    return lax.dot_general(left_side, right_side, (((0,), (0,)), ((), ())), preferred_element_type=f32)


def dot_cols(left_side, right_side):
    return lax.dot_general(left_side, right_side, (((1,), (1,)), ((), ())), preferred_element_type=f32)


def norm_parts(values):
    center = values - jnp.mean(values, -1, keepdims=True)
    rescale = lax.rsqrt(jnp.mean(center * center, -1, keepdims=True) + 1e-05)
    return center * rescale, rescale


def norm_backward(grad_rows, normed, rescale, norm_gain):
    scaled = grad_rows * norm_gain
    inner = (
        scaled
        - jnp.mean(scaled, -1, keepdims=True)
        - normed * jnp.mean(scaled * normed, -1, keepdims=True)
    )
    return rescale * inner


def put_blocks(out_ref, part, half, slot, start, value, where_ref):
    value = value.astype(bf16)
    for index in range(16):
        if where_ref is None:
            place = 48 * block_place(part, index)
            block = out_ref.at[index] if slot is None else out_ref.at[slot, index]
        else:
            place = 48 * index
            block = out_ref.at[2 * (where_ref[0] ^ int(MASKS[index])) + (where_ref[1] ^ half)]
        block[:, start : start + value.shape[1]] = value[place : place + 48]


def attention_forward_kernel(
    length_ref, x_ref, own_ref, peer_ref, place_ref,
    middle_ref, heads_ref, soft_ref, mixed_ref, vec_ref, up_bias_ref,
):
    length = length_ref[0]
    vec_ref[0:6] = own_ref[:, 1536:].astype(f32).T[0:6]
    units = []
    for weight_ref in (own_ref, peer_ref):
        rows = dot(place_ref[...], weight_ref[:, 1536:]).T
        units += [rows[:64], rows[64:]]
    for row, first in ((6, 8), (7, 11)):
        pieces = [rows[first + i : first + i + 1] for rows in units for i in range(3)]
        vec_ref[row : row + 1] = jnp.concatenate(pieces, 1)
    pieces = [rows[14 + i : 15 + i] for rows in units for i in range(12)]
    for i in range(24):
        up_bias_ref[0:1, 128 * i : 128 * i + 128] = jnp.concatenate(pieces[2 * i : 2 * i + 2], 1)
    normed, _ = norm_parts(x_ref[...].astype(f32))
    normed_b = (normed * vec_ref[2:3] + vec_ref[3:4]).astype(bf16)
    for j in range(3):
        for half, weight_ref in enumerate((own_ref, peer_ref)):
            cols = slice(384 * half, 384 * half + 384)
            rows = dot(normed_b, weight_ref[:, 384 * j : 384 * j + 384])
            if j != 1:
                rows = rows + vec_ref[6 + j // 2 : 7 + j // 2, cols]
            heads_ref[j, :, cols] = rows.astype(bf16)
    count = x_ref.shape[0]
    live_keys = lax.broadcasted_iota(jnp.int32, (count, count), 1) < length
    for pair in range(6):
        both = []
        for head in (2 * pair, 2 * pair + 1):
            cols = slice(HEAD * head, HEAD * head + HEAD)
            scores = dot_cols(heads_ref[0, :, cols], heads_ref[1, :, cols]) * HEAD ** (-0.5)
            scores = jnp.where(live_keys, scores, -1e30)
            powers = jnp.exp(scores - jnp.max(scores, -1, keepdims=True))
            soft = powers / jnp.sum(powers, -1, keepdims=True)
            soft_ref[head] = soft
            both.append(dot(soft.astype(bf16), heads_ref[2, :, cols]))
        mixed_ref[:, 128 * pair : 128 * pair + 128] = jnp.concatenate(both, 1).astype(bf16)
    total = dot_cols(mixed_ref[:, :384], own_ref[:, 1152:1536])
    total = total + dot_cols(mixed_ref[:, 384:], peer_ref[:, 1152:1536])
    middle_ref[...] = x_ref[...].astype(f32) + total + vec_ref[0:1]


def units_forward_kernel(middle_ref, own_ref, peer_ref, vec_ref, up_bias_ref, result_ref, active_ref, slope_ref):
    middle = middle_ref[...]
    normed, _ = norm_parts(middle)
    normed_b = (normed * vec_ref[4:5] + vec_ref[5:6]).astype(bf16)
    total = middle + vec_ref[1:2]
    for half, weight_ref in enumerate((own_ref, peer_ref)):
        for j in range(2):
            cols = slice(768 * (2 * half + j), 768 * (2 * half + j) + 768)
            pre_active = dot(normed_b, weight_ref[j]) + up_bias_ref[0:1, cols]
            below = 0.5 * (1.0 + lax.erf(pre_active * half_root))
            active_b = (pre_active * below).astype(bf16)
            active_ref[:, cols] = active_b
            slope_ref[:, cols] = below + pre_active * jnp.exp(-0.5 * pre_active * pre_active) * gauss_factor
            total = total + dot_cols(active_b, weight_ref[2 + j])
    result_ref[...] = total.astype(bf16)


def units_backward_kernel(placed, *refs):
    where_ref, refs = (refs[0], refs[1:]) if placed else (None, refs)
    grad_ref, middle_ref, active_ref, slope_ref, own_ref, peer_ref, vec_ref = refs[:7]
    grad_middle_ref, vec_grad_ref, up_bias_grad_ref, grad_own_ref = refs[7:11]
    grad_peer_ref = grad_own_ref if placed else refs[11]
    grad_b = grad_ref[...]
    grad_rows = grad_b.astype(f32)
    normed, rescale = norm_parts(middle_ref[...])
    normed_b = (normed * vec_ref[4:5] + vec_ref[5:6]).astype(bf16)
    normed_t = normed_b.T
    grad_t = grad_b.T
    grad_normed = None
    for half, weight_ref, out_ref in ((1, peer_ref, grad_peer_ref), (0, own_ref, grad_own_ref)):
        for j in range(2):
            cols = slice(768 * (2 * half + j), 768 * (2 * half + j) + 768)
            slot, start = (None, 768 * j) if placed else (j, 0)
            value = dot(grad_t, active_ref[:, cols])
            put_blocks(out_ref, 2 + j, half, None if placed else 2 + j, 1536 + start if placed else 0, value, where_ref)
            grad_upper = (dot(grad_b, weight_ref[2 + j]) * slope_ref[:, cols]).astype(bf16)
            up_bias_grad_ref[0:1, cols] = jnp.sum(grad_upper.astype(f32), 0, keepdims=True)
            put_blocks(out_ref, j, half, slot, start, dot(normed_t, grad_upper), where_ref)
            term = dot_cols(grad_upper, weight_ref[j])
            grad_normed = term if grad_normed is None else grad_normed + term
    grad_middle = grad_rows + norm_backward(grad_normed, normed, rescale, vec_ref[4:5])
    grad_middle_ref[...] = grad_middle
    vec_grad_ref[...] = jnp.zeros_like(vec_grad_ref)
    vec_grad_ref[0:1] = jnp.sum(grad_middle, 0, keepdims=True)
    vec_grad_ref[1:2] = jnp.sum(grad_rows, 0, keepdims=True)
    vec_grad_ref[4:5] = jnp.sum(grad_normed * normed, 0, keepdims=True)
    vec_grad_ref[5:6] = jnp.sum(grad_normed, 0, keepdims=True)


def attention_backward_kernel(*refs):
    grad_ref, x_ref, heads_ref, soft_ref, mixed_ref, own_ref, peer_ref, vec_ref = refs[:8]
    units_vec_ref, up_bias_grad_ref, place_ref, grad_in_ref, grad_own_ref, grad_peer_ref = refs[8:14]
    grad_mixed_ref, grad_heads_ref, cols_ref, small_ref = refs[14:]
    grad_b = grad_ref[...].astype(bf16)
    grad_t = grad_b.T
    grad_mixed_ref[:, :384] = dot(grad_b, own_ref[:, 1152:1536]).astype(bf16)
    grad_mixed_ref[:, 384:] = dot(grad_b, peer_ref[:, 1152:1536]).astype(bf16)
    factor = HEAD ** (-0.5)
    for pair in range(6):
        found = ([], [], [])
        for head in (2 * pair, 2 * pair + 1):
            cols = slice(HEAD * head, HEAD * head + HEAD)
            soft = soft_ref[head]
            grad_head = grad_mixed_ref[:, cols]
            grad_soft = dot_cols(grad_head, heads_ref[2, :, cols])
            inner = jnp.sum(grad_soft * soft, -1, keepdims=True)
            grad_scores = (soft * (grad_soft - inner)).astype(bf16)
            found[0].append(dot(grad_scores, heads_ref[1, :, cols]) * factor)
            found[1].append(dot_rows(grad_scores, heads_ref[0, :, cols]) * factor)
            found[2].append(dot_rows(soft.astype(bf16), grad_head))
        for j in range(3):
            grad_heads_ref[j, :, 128 * pair : 128 * pair + 128] = jnp.concatenate(found[j], 1).astype(bf16)
    normed, rescale = norm_parts(x_ref[...].astype(f32))
    normed_b = (normed * vec_ref[2:3] + vec_ref[3:4]).astype(bf16)
    normed_t = normed_b.T
    grad_normed = None
    for half, weight_ref, out_ref in ((1, peer_ref, grad_peer_ref), (0, own_ref, grad_own_ref)):
        for j in range(3):
            rows = grad_heads_ref[j, :, 384 * half : 384 * half + 384]
            put_blocks(out_ref, j, half, None, 384 * j, dot(normed_t, rows), None)
            term = dot_cols(rows, weight_ref[:, 384 * j : 384 * j + 384])
            grad_normed = term if grad_normed is None else grad_normed + term
    grad_in = grad_ref[...] + norm_backward(grad_normed, normed, rescale, vec_ref[2:3])
    grad_in_ref[...] = grad_in.astype(bf16)
    cols_ref[...] = jnp.zeros_like(cols_ref)
    cols_ref[0:2] = units_vec_ref[0:2]
    cols_ref[2:3] = jnp.sum(grad_normed * normed, 0, keepdims=True)
    cols_ref[3:4] = jnp.sum(grad_normed, 0, keepdims=True)
    cols_ref[4:6] = units_vec_ref[4:6]
    cols_ref[64:70] = cols_ref[0:6]
    cols = cols_ref[...].T
    query_bias = jnp.sum(grad_heads_ref[0].astype(f32), 0, keepdims=True)
    value_bias = jnp.sum(grad_heads_ref[2].astype(f32), 0, keepdims=True)
    for half, out_ref in ((1, grad_peer_ref), (0, grad_own_ref)):
        small_ref[...] = jnp.zeros_like(small_ref)
        for t in range(2):
            base = 64 * t
            for i in range(3):
                at = HEAD * (6 * half + 3 * t + i)
                small_ref[base + 8 + i : base + 9 + i] = query_bias[:, at : at + HEAD]
                small_ref[base + 11 + i : base + 12 + i] = value_bias[:, at : at + HEAD]
            for i in range(12):
                at = HEAD * (24 * half + 12 * t + i)
                small_ref[base + 14 + i : base + 15 + i] = up_bias_grad_ref[0:1, at : at + HEAD]
        small = dot_cols(place_ref[...], small_ref[...].astype(bf16)) + cols
        weight = dot(grad_t, mixed_ref[:, 384 * half : 384 * half + 384])
        put_blocks(out_ref, 3, half, None, 1152, jnp.concatenate([weight, small], 1), None)


def kernel_call(kernel, name, inputs, outputs, scratch=(), scalar=False, blocks=None, large=True):
    whole = pl.BlockSpec(memory_space=pltpu.VMEM)
    specs = [whole] * len(inputs)
    out_specs = [whole] * len(outputs)
    if blocks is not None:
        specs = [pl.BlockSpec(shape, lambda i, at=at: at) for shape, at in blocks]
        out_specs = [pl.BlockSpec(shape, lambda i, n=len(shape): (0,) * n) for shape, _ in outputs]
    if scalar:
        specs[0] = pl.BlockSpec(memory_space=pltpu.SMEM)
    shapes = [jax.ShapeDtypeStruct(shape, dtype) for shape, dtype in outputs]
    return pl.pallas_call(
        kernel,
        name=name,
        out_shape=shapes,
        in_specs=specs,
        out_specs=out_specs,
        grid=() if blocks is None else (1,),
        scratch_shapes=list(scratch),
        cost_estimate=pl.CostEstimate(flops=1, bytes_accessed=1, transcendentals=0),
        compiler_params=pltpu.CompilerParams(vmem_limit_bytes=52 * 2**20 if large else None),
    )(*inputs)


ROWS = (192, 768)
HEADS_SHAPE = (3, 192, 768)
UNITS_SHAPE = (4, 16, 48, 768)
ATTN_SHAPE = (16, 48, 1664)
PLACED_UNITS = (32, 48, 3072)


def attention_forward(length, x, attn, place_units):
    own, peer = attn
    return kernel_call(
        attention_forward_kernel, "attention_forward",
        [length, x, own, peer, place_units],
        [(ROWS, f32), (HEADS_SHAPE, bf16), ((12, 192, 192), f32), (ROWS, bf16), ((8, 768), f32), ((1, 3072), f32)],
        scalar=True,
    )


def units_forward(middle, units, vec, up_bias):
    own, peer = units
    return kernel_call(
        units_forward_kernel, "units_forward", [middle, own, peer, vec, up_bias],
        [(ROWS, bf16), ((192, 3072), bf16), ((192, 3072), f32)],
    )


def units_backward(grad_b, middle, active, slope, units, vec, where=None):
    own, peer = units
    placed = where is not None
    shapes = [PLACED_UNITS] if placed else [UNITS_SHAPE] * 2
    return kernel_call(
        functools.partial(units_backward_kernel, placed), "units_backward",
        [where] * placed + [grad_b, middle, active, slope, own, peer, vec],
        [(ROWS, f32), ((8, 768), f32), ((1, 3072), f32)] + [(shape, bf16) for shape in shapes], scalar=placed,
    )


def attention_backward(grad_middle, x, heads, soft, mixed, attn, vec, units_vec, up_bias_grad, place_units):
    own, peer = attn
    return kernel_call(
        attention_backward_kernel, "attention_backward",
        [grad_middle, x, heads, soft, mixed, own, peer, vec, units_vec, up_bias_grad, place_units],
        [(ROWS, bf16), (ATTN_SHAPE, bf16), (ATTN_SHAPE, bf16)],
        scratch=[pltpu.VMEM(ROWS, bf16), pltpu.VMEM(HEADS_SHAPE, bf16), pltpu.VMEM((128, 768), f32), pltpu.VMEM((128, 64), f32)],
    )


def exchange(value, bit):
    axis, size, flip = EXCHANGES[bit]
    return lax.ppermute(value, axis, [(i, i ^ flip) for i in range(size)])


def exchange_pipe(value):
    return lax.ppermute(value, "pipe", [(0, 1), (1, 0)])


def exchange_both(value):
    return lax.ppermute(value, ("pipe", "tensor"), [(i, i ^ 3) for i in range(4)])


def exchange_tensor(value):
    return lax.ppermute(value, "tensor", [(0, 1), (1, 0)])


def pin(*values):
    return lax.optimization_barrier(values)


def assemble_kernel(slots, *refs):
    count = len(slots)
    out = refs[-1]
    for number, (part, slot, start) in enumerate(slots):
        for index in range(16):
            rows = refs[number + (0 if index < 8 else count)][index % 8]
            place = slice(48 * block_place(part, index), 48 * block_place(part, index) + 48)
            cols = slice(start, start + rows.shape[1])
            if slot is None:
                out[place, cols] = rows
            else:
                out[slot, place, cols] = rows


def assemble(held, got, units):
    inputs, blocks, slots = [], [], []
    for part in range(4):
        width = (384, 256)[part // 3] if units else ATTN_COLS[part]
        first = ATTN_COLS[part] // width if units else 0
        for k in range(768 // width if units else 1):
            inputs.append(part)
            blocks.append(((8, 48, width), (0, 0, first + k)))
            slots.append((part, part, width * k) if units else (part, None, 384 * part))
    arrays = [held[part] for part in inputs] + [got[part] for part in inputs]
    shape = (4, 768, 768) if units else (768, 1664)
    kernel = functools.partial(assemble_kernel, slots)
    name = "assemble_units" if units else "assemble_attention"
    return kernel_call(kernel, name, arrays, [(shape, bf16)], blocks=blocks * 2)[0]


def pack_kernel(*refs):
    w_query, w_key, w_value, w_out, w_up, w_down, b_query, b_value = refs[:8]
    b_up = refs[9]
    vectors = [refs[8], *refs[10:15]]
    out_ref, vec_ref, small_ref = refs[15:]
    vec_ref[...] = jnp.zeros_like(vec_ref)
    for i, vector in enumerate(vectors):
        vec_ref[i : i + 1, 0:24] = vector[...].astype(f32)
    cols = vec_ref[...].T[0:24, 0:8]
    for half in range(2):
        small_ref[...] = jnp.zeros_like(small_ref)
        small_ref[:, 0:8] = cols
        small_ref[0:2, 8:11] = b_query[0, :, 3 * half : 3 * half + 3].astype(f32)
        small_ref[0:2, 11:14] = b_value[0, :, 3 * half : 3 * half + 3].astype(f32)
        small_ref[0:2, 14:26] = b_up[0, :, 12 * half : 12 * half + 12].astype(f32)
        small = small_ref[...].astype(bf16)
        wide, whole = slice(768 * half, 768 * half + 768), slice(192 * half, 192 * half + 192)
        first = jnp.concatenate([w_query[0, :, whole].astype(f32), w_key[0, :, whole].astype(f32)], 1).astype(bf16)
        second = jnp.concatenate([w_value[0, :, whole].astype(f32), w_out[0, :, whole].astype(f32)], 1).astype(bf16)
        for k in range(4):
            out = out_ref.at[2 * k + half]
            out[:, 0:768] = w_up[0, :, wide]
            out[:, 768:1536] = w_down[0, :, wide]
            out[:, 1536:1920] = first
            out[:, 1920:2304] = second
            out[:, 2304:2368] = small


def gather_start(params):
    tensor = lax.axis_index("tensor")
    rows = kernel_call(
        pack_kernel, "pack", list(params), [((8, 24, 2368), bf16)],
        scratch=[pltpu.VMEM((8, 128), f32), pltpu.VMEM((24, 64), f32)],
        blocks=[(param.shape, (0,) * param.ndim) for param in params], large=False,
    )[0]
    rows = lax.all_to_all(rows, ("pipe", "tensor", "core"), 0, 0, tiled=True)
    rows = rows.reshape(2, 2, 48, 2368)
    a = jnp.where(tensor == 0, rows[:, 0], rows[:, 1])
    b = jnp.where(tensor == 0, rows[:, 1], rows[:, 0])
    parts = [
        [a[..., 1536:1728], b[..., 1536:1728], a[..., :768]],
        [a[..., 1728:1920], b[..., 1728:1920], b[..., :768]],
        [a[..., 1920:2112], b[..., 1920:2112], a[..., 768:1536]],
        [a[..., 2112:2304], b[..., 2112:2304], a[..., 2304:], b[..., 2304:], b[..., 768:1536]],
    ]
    parts = [jnp.concatenate(part, -1)[:, None] for part in parts]
    for step in range(2):
        got = [exchange(part, ORDERS[i][step]) for i, part in enumerate(parts)]
        parts = [jnp.concatenate([x, y], 1) for x, y in zip(parts, got)]
    return parts, [exchange(part, ORDERS[i][2]) for i, part in enumerate(parts)]


def gather_layer(parts, got, layer):
    return [jnp.concatenate([x[layer], y[layer]], 0) for x, y in zip(parts, got)]


def gather_fourth(held):
    return [exchange(part, ORDERS[i][3]) for i, part in enumerate(held)]


def fold_kernel(fixed, outputs, *refs):
    terms, outs = refs[: len(fixed)], refs[len(fixed) :]
    for out, places in zip(outs, outputs):
        for sources, layer, start in places:
            total = None
            for term, index, first, width in sources:
                value = terms[term][(*index, *(0,) * fixed[term], slice(None), slice(None), slice(first, first + width))]
                total = value.astype(f32) if total is None else total + value.astype(f32)
            cols = slice(start, start + total.shape[-1])
            if layer is None:
                out[:, :, cols] = total.astype(bf16)
            else:
                out[layer, :, :, cols] = total.astype(bf16)


def fold(terms, outputs, layers, grid, name):
    arrays, specs, shapes, out_specs = [], [], [], []
    for array, bits in terms:
        lead, (n, rows, cols) = array.shape[:-3], array.shape[-3:]
        n >>= len(bits)
        arrays.append(array.reshape(*lead, *(2,) * len(bits), n, rows, cols))
        block = (*lead, *(1,) * len(bits), n // grid, rows, cols)
        specs.append(pl.BlockSpec(block, lambda b, at=(0,) * len(lead) + tuple(bits): (*at, b, 0, 0)))
    for places in outputs:
        width = max(start + sources[0][3] for sources, _, start in places)
        lead = () if layers is None else (layers,)
        shapes.append(jax.ShapeDtypeStruct((*lead, n, 48, width), bf16))
        out_specs.append(pl.BlockSpec((*lead, n // grid, 48, width), lambda b, at=(0,) * len(lead): (*at, b, 0, 0)))
    return pl.pallas_call(
        functools.partial(fold_kernel, [len(bits) for _, bits in terms], outputs),
        name=name,
        grid=(grid,),
        out_shape=shapes,
        in_specs=specs,
        out_specs=out_specs,
        cost_estimate=pl.CostEstimate(flops=1, bytes_accessed=1, transcendentals=0),
        compiler_params=pltpu.CompilerParams(vmem_limit_bytes=52 * 2**20),
    )(*arrays)


def send_parts(parts, step):
    return [exchange(part, ORDERS[i][step]) for i, part in enumerate(parts)]


def fold_attention(own, got):
    outputs = [[([(k, (), 384 * i, ATTN_COLS[i]) for k in range(2)], None, 0)] for i in range(4)]
    return fold([(own, (1,)), (got, (1,))], outputs, None, 2, "fold_attention")


def fold_units(own, got):
    outputs = [[([(k, (i,), 0, 768) for k in range(2)], None, 0)] for i in range(4)]
    return fold([(own, (1,)), (got, (1,))], outputs, None, 2, "fold_units")


def fold_both(groups, side):
    terms = []
    outputs = [[] for _ in range(4)]
    for number, (own, got, received) in enumerate(groups):
        base, units = len(terms), number == 1
        terms += [(own, (0, side)), (got, (0, side))] + [(part, (side,)) for part in received]
        for i in range(4):
            width = 768 if units else ATTN_COLS[i]
            index, first = ((i,), 0) if units else ((), 384 * i)
            sources = [(base, index, first, width), (base + 1, index, first, width), (base + 2 + i, (), 0, width)]
            outputs[i].append((sources, None, (0, ATTN_COLS[i], ATTN_COLS[i] + 768)[number]))
    return fold(terms, outputs, None, 2, ("fold_both_kept", "fold_both_sent")[side])


def fold_on(kept, got, side, name):
    terms = [(part, (side,)) for pair in zip(kept, got) for part in pair]
    outputs = []
    for i in range(4):
        width = kept[i].shape[-1]
        outputs.append([([(2 * i + k, (), 0, width) for k in range(2)], None, 0)])
    return fold(terms, outputs, None, 1, name + ("_kept", "_sent")[side])


def collect_kernel(tensor_ref, *refs):
    kept, got, units, out_ref = refs[:4], refs[4:8], refs[8], refs[9]
    p = [x[0].astype(f32) + y[0].astype(f32) for x, y in zip(kept, got)]
    layers = [
        (
            [part[:, : ATTN_COLS[i]] for i, part in enumerate(p)],
            [part[:, ATTN_COLS[i] : ATTN_COLS[i] + 768] for i, part in enumerate(p)],
        ),
        (
            [part[:, ATTN_COLS[i] + 768 :] for i, part in enumerate(p)],
            [units[0, :, 768 * i : 768 * i + 768].astype(f32) for i in range(4)],
        ),
    ]
    for layer, (first, wide) in enumerate(layers):
        for t in range(2):
            at = slice(192 * t, 192 * t + 192)
            values = [
                (0, wide[t]),
                (768, wide[2 + t]),
                (1536, jnp.concatenate([first[0][:, at], first[1][:, at]], 1)),
                (1920, jnp.concatenate([first[2][:, at], first[3][:, at]], 1)),
                (2304, first[3][:, 384 + 64 * t : 448 + 64 * t]),
            ]
            place = 4 * layer + 2 * (t ^ tensor_ref[0])
            for core in range(2):
                out = out_ref.at[place + core]
                for start, value in values:
                    out[:, start : start + value.shape[1]] = value[24 * core : 24 * core + 24].astype(bf16)


def finish_kernel(rows_ref, *refs):
    g_query, g_key, g_value, g_out, g_up, g_down, gb_query, gb_value = refs[:8]
    gb_up = refs[9]
    vectors = [refs[8], *refs[10:15]]
    small_ref = refs[15]
    halves = []
    for core in range(2):
        total = rows_ref[core].astype(f32)
        for k in range(1, 4):
            total = total + rows_ref[2 * k + core].astype(f32)
        halves.append(total)
        g_up[0, :, 768 * core : 768 * core + 768] = total[:, 0:768]
        g_down[0, :, 768 * core : 768 * core + 768] = total[:, 768:1536]
    for i, out in enumerate((g_query, g_key, g_value, g_out)):
        start = 1536 + 192 * i
        out[0] = jnp.concatenate([half[:, start : start + 192] for half in halves], 1)
    for out, lo, hi in ((gb_query, 8, 11), (gb_value, 11, 14), (gb_up, 14, 26)):
        out[0] = jnp.concatenate([half[0:2, 2304 + lo : 2304 + hi] for half in halves], 1)
    small_ref[...] = jnp.zeros_like(small_ref)
    small_ref[0:24, 0:64] = halves[0][:, 2304:2368]
    cols = small_ref[...].T
    for i, out in enumerate(vectors):
        out[...] = cols[i : i + 1, 0:24]


def scatter_end(kept, got, units):
    tensor = lax.axis_index("tensor").astype(jnp.int32).reshape(1)
    rows = kernel_call(collect_kernel, "collect", [tensor, *kept, *got, units], [((8, 24, 2368), bf16)], scalar=True)[0]
    rows = lax.all_to_all(rows, ("pipe", "tensor", "core"), 0, 0, tiled=True)
    shapes = [(1, 24, 384)] * 4 + [(1, 24, 1536)] * 2 + [(1, 2, 6)] * 2 + [(1, 24), (1, 2, 24)] + [(1, 24)] * 5
    return kernel_call(
        finish_kernel, "finish", [rows], [(shape, f32) for shape in shapes], scratch=[pltpu.VMEM((128, 128), f32)]
    )


def share_outputs(first_rows, second_rows):
    pipe, tensor = lax.axis_index("pipe"), lax.axis_index("tensor")
    keep = jnp.where(pipe == 0, first_rows, second_rows)
    send = jnp.where(pipe == 0, second_rows, first_rows)
    return keep, exchange_tensor(keep), exchange_pipe(send), exchange_both(send)


def order_outputs(rows):
    pipe, tensor = lax.axis_index("pipe"), lax.axis_index("tensor")
    a, b, c, d = rows
    a, b = jnp.where(tensor == 0, a, b), jnp.where(tensor == 0, b, a)
    c, d = jnp.where(tensor == 0, c, d), jnp.where(tensor == 0, d, c)
    a, c = jnp.where(pipe == 0, a, c), jnp.where(pipe == 0, c, a)
    b, d = jnp.where(pipe == 0, b, d), jnp.where(pipe == 0, d, b)
    return jnp.stack([a, b, c, d])[None]


def local(clip_frames, out_cotangent, clip_lengths, *params):
    micro = lax.axis_index("pipe") * 2 + lax.axis_index("tensor")
    chip = lax.axis_index("z") * 4 + lax.axis_index("x")

    where = jnp.stack([chip, lax.axis_index("core")]).astype(jnp.int32)

    parts, third = gather_start(params)
    held = [gather_layer(parts, third, layer) for layer in range(2)]
    got = [gather_fourth(held[0])]
    got[0], held[1] = pin(got[0], held[1])
    got.append(gather_fourth(held[1]))

    blocks = (chip ^ jnp.asarray(MASKS))[:, None]
    rows_at = (blocks * 48 + jnp.arange(48)[None]).reshape(-1)
    place_rows = (jnp.arange(768)[:, None] == rows_at[None]).astype(bf16)
    within = np.arange(48)
    units_at = np.where(within % 24 < 2, within // 24 * 2 + within % 24, 1000)
    units_at = (blocks * 4 + jnp.asarray(units_at)[None]).reshape(-1)
    place_units = (jnp.arange(64)[:, None] == units_at[None]).astype(bf16)
    place_back = (units_at[:, None] == jnp.arange(64)[None]).astype(bf16)

    frames = lax.dynamic_index_in_dim(clip_frames, micro, 0, keepdims=False)
    cotangent = lax.dynamic_index_in_dim(out_cotangent, micro, 0, keepdims=False)
    length = lax.dynamic_index_in_dim(clip_lengths, micro, 0, keepdims=False)
    x_first = dot(frames, place_rows).astype(bf16)
    grad_out = dot(cotangent, place_rows).astype(bf16)

    def placed_back(rows):
        return dot_cols(rows, place_rows).astype(bf16)

    attn_own = assemble(held[0], got[0], False)
    attn_own, got[0] = pin(attn_own, got[0])
    attn_peer = exchange(attn_own, "c")
    units_own = assemble(held[0], got[0], True)
    attn_peer, units_own = pin(attn_peer, units_own)
    attn_first = attn_own, attn_peer
    units_first = units_own, exchange(units_own, "c")
    middle_first, heads_first, soft_first, mixed_first, vec_first, up_bias_first = attention_forward(
        length, x_first, attn_first, place_units
    )
    x_second, active_first, slope_first = units_forward(middle_first, units_first, vec_first, up_bias_first)
    x_second, got[1] = pin(x_second, got[1])
    attn_own = assemble(held[1], got[1], False)
    attn_own, got[1] = pin(attn_own, got[1])
    attn_peer = exchange(attn_own, "c")
    units_own = assemble(held[1], got[1], True)
    attn_peer, units_own = pin(attn_peer, units_own)
    attn_second = attn_own, attn_peer
    units_second = units_own, exchange(units_own, "c")
    middle_second, heads_second, soft_second, mixed_second, vec_second, up_bias_second = attention_forward(
        length, x_second, attn_second, place_units
    )
    out_second, active_second, slope_second = units_forward(middle_second, units_second, vec_second, up_bias_second)
    shared = share_outputs(placed_back(x_second), placed_back(out_second))

    grad_middle, units_vec, up_bias_grad, units_placed = units_backward(
        grad_out, middle_second, active_second, slope_second, units_second, vec_second, where
    )
    units_total = lax.psum_scatter(units_placed, ("z", "x", "core"), scatter_dimension=0, tiled=True)
    attn = attention_backward(
        grad_middle, x_second, heads_second, soft_second, mixed_second, attn_second, vec_second, units_vec,
        up_bias_grad, place_back,
    )
    attn, shared = pin(attn, shared)
    section_output = order_outputs(shared)
    second_grad, attn_own_second, attn_peer = attn
    attn_got_second = exchange(attn_peer, "c")

    units = units_backward(second_grad, middle_first, active_first, slope_first, units_first, vec_first)
    units, attn_got_second = pin(units, attn_got_second)
    grad_middle, units_vec, up_bias_grad, units_own, units_peer = units
    attn_fourth_second = send_parts(fold_attention(attn_own_second, attn_got_second), 3)
    units_got = exchange(units_peer, "c")
    attn = attention_backward(
        grad_middle, x_first, heads_first, soft_first, mixed_first, attn_first, vec_first, units_vec,
        up_bias_grad, place_back,
    )
    attn, units_got, attn_fourth_second = pin(attn, units_got, attn_fourth_second)
    first_grad, attn_own, attn_peer = attn
    units_fourth = send_parts(fold_units(units_own, units_got), 3)
    attn_got = exchange(attn_peer, "c")
    attn_fourth = send_parts(fold_attention(attn_own, attn_got), 3)
    input_grad = order_outputs(share_outputs(placed_back(first_grad), placed_back(second_grad)))

    groups = (
        (attn_own, attn_got, attn_fourth), (units_own, units_got, units_fourth),
        (attn_own_second, attn_got_second, attn_fourth_second),
    )
    kept, got = fold_both(groups, 0), send_parts(fold_both(groups, 1), 2)
    kept, got = fold_on(kept, got, 0, "fold_four"), send_parts(fold_on(kept, got, 1, "fold_four"), 1)
    kept, got = fold_on(kept, got, 0, "fold_two"), send_parts(fold_on(kept, got, 1, "fold_two"), 0)
    return (section_output, input_grad, *scatter_end(kept, got, units_total))


def solution(mesh):
    fine = Mesh(mesh.devices.reshape(2, 4, 4, 2, 2), ("pipe", "z", "x", "core", "tensor"))
    shard = ("z", "x", "core")
    rows = P(None, shard, None)
    matrix = P("pipe", shard, "tensor")
    vector = P("pipe", shard)
    params = (matrix,) * 8 + (vector, matrix) + (vector,) * 5
    return jax.shard_map(
        local,
        mesh=fine,
        in_specs=(rows, rows, P(None, shard)) + params,
        out_specs=(P("pipe", None, shard, None),) * 2 + params,
        check_vma=False,
    )
```

```python
import functools

import jax
import jax.numpy as jnp
import numpy as np
from jax import lax
from jax.experimental import pallas as pl
from jax.experimental.pallas import tpu as pltpu
from jax.sharding import Mesh
from jax.sharding import PartitionSpec as P

HEAD = 64
bf16 = jnp.bfloat16
f32 = jnp.float32

half_root = 0.7071067811865476
gauss_factor = 0.3989422804014327


EXCHANGES = {"xu": ("x", 4, 1), "xv": ("x", 4, 3), "zu": ("z", 4, 1), "zv": ("z", 4, 3), "c": ("core", 2, 1)}
BLOCK_BITS = ("zv", "zu", "xv", "xu")
BIT_MASK = {"xu": 1, "xv": 3, "zu": 4, "zv": 12}
ORDERS = (
    ("xu", "xv", "zu", "zv"),
    ("xv", "xu", "zv", "zu"),
    ("zu", "zv", "xu", "xv"),
    ("zv", "zu", "xv", "xu"),
)
MASKS = np.zeros(16, np.int32)
for _index in range(16):
    for _place, _bit in enumerate(BLOCK_BITS):
        if (_index >> (3 - _place)) & 1:
            MASKS[_index] ^= BIT_MASK[_bit]
ATTN_COLS = (384, 384, 384, 512)


def block_place(part, index):
    place = 0
    for step in range(4):
        if (index >> step) & 1:
            place += 8 >> BLOCK_BITS.index(ORDERS[part][step])
    return place


def dot(left_side, right_side):
    return lax.dot_general(left_side, right_side, (((1,), (0,)), ((), ())), preferred_element_type=f32)


def dot_rows(left_side, right_side):
    return lax.dot_general(left_side, right_side, (((0,), (0,)), ((), ())), preferred_element_type=f32)


def dot_cols(left_side, right_side):
    return lax.dot_general(left_side, right_side, (((1,), (1,)), ((), ())), preferred_element_type=f32)


def norm_parts(values):
    center = values - jnp.mean(values, -1, keepdims=True)
    rescale = lax.rsqrt(jnp.mean(center * center, -1, keepdims=True) + 1e-05)
    return center * rescale, rescale


def norm_backward(grad_rows, normed, rescale, norm_gain):
    scaled = grad_rows * norm_gain
    inner = (
        scaled
        - jnp.mean(scaled, -1, keepdims=True)
        - normed * jnp.mean(scaled * normed, -1, keepdims=True)
    )
    return rescale * inner


def put_blocks(out_ref, part, slot, value):
    value = value.astype(bf16)
    for index in range(16):
        place = 48 * block_place(part, index)
        out_ref[slot, index] = value[place : place + 48]


def put_columns(out_ref, part, start, value):
    value = value.astype(bf16)
    for index in range(16):
        place = 48 * block_place(part, index)
        out_ref[index, :, start : start + value.shape[1]] = value[place : place + 48]


def attention_forward_kernel(
    length_ref, x_ref, own_ref, peer_ref, place_ref,
    middle_ref, heads_ref, soft_ref, mixed_ref, vec_ref, up_bias_ref,
):
    length = length_ref[0]
    vec_ref[0:6] = own_ref[:, 1536:].astype(f32).T[0:6]
    units = []
    for weight_ref in (own_ref, peer_ref):
        rows = dot(place_ref[...], weight_ref[:, 1536:]).T
        units += [rows[:64], rows[64:]]
    for row, first in ((6, 8), (7, 11)):
        pieces = [rows[first + i : first + i + 1] for rows in units for i in range(3)]
        vec_ref[row : row + 1] = jnp.concatenate(pieces, 1)
    pieces = [rows[14 + i : 15 + i] for rows in units for i in range(12)]
    for i in range(24):
        up_bias_ref[0:1, 128 * i : 128 * i + 128] = jnp.concatenate(pieces[2 * i : 2 * i + 2], 1)
    normed, _ = norm_parts(x_ref[...].astype(f32))
    normed_b = (normed * vec_ref[2:3] + vec_ref[3:4]).astype(bf16)
    for j in range(3):
        for half, weight_ref in enumerate((own_ref, peer_ref)):
            cols = slice(384 * half, 384 * half + 384)
            rows = dot(normed_b, weight_ref[:, 384 * j : 384 * j + 384])
            if j != 1:
                rows = rows + vec_ref[6 + j // 2 : 7 + j // 2, cols]
            heads_ref[j, :, cols] = rows.astype(bf16)
    count = x_ref.shape[0]
    live_keys = lax.broadcasted_iota(jnp.int32, (count, count), 1) < length
    for pair in range(6):
        both = []
        for head in (2 * pair, 2 * pair + 1):
            cols = slice(HEAD * head, HEAD * head + HEAD)
            scores = dot_cols(heads_ref[0, :, cols] * bf16(HEAD ** (-0.5)), heads_ref[1, :, cols])
            scores = jnp.where(live_keys, scores, -1e30)
            powers = jnp.exp(scores - jnp.max(scores, -1, keepdims=True))
            soft = powers * (1.0 / jnp.sum(powers, -1, keepdims=True))
            soft_ref[head] = soft
            both.append(dot(soft.astype(bf16), heads_ref[2, :, cols]))
        mixed_ref[:, 128 * pair : 128 * pair + 128] = jnp.concatenate(both, 1).astype(bf16)
    total = dot_cols(mixed_ref[:, :384], own_ref[:, 1152:1536])
    total = total + dot_cols(mixed_ref[:, 384:], peer_ref[:, 1152:1536])
    middle_ref[...] = x_ref[...].astype(f32) + total + vec_ref[0:1]


def units_forward_kernel(middle_ref, own_ref, peer_ref, vec_ref, up_bias_ref, result_ref, active_ref, slope_ref):
    middle = middle_ref[...]
    normed, _ = norm_parts(middle)
    normed_b = (normed * vec_ref[4:5] + vec_ref[5:6]).astype(bf16)
    total = middle + vec_ref[1:2]
    for half, weight_ref in enumerate((own_ref, peer_ref)):
        for j in range(2):
            cols = slice(768 * (2 * half + j), 768 * (2 * half + j) + 768)
            pre_active = dot(normed_b, weight_ref[j]) + up_bias_ref[0:1, cols]
            below = 0.5 * (1.0 + lax.erf(pre_active * half_root))
            active_b = (pre_active * below).astype(bf16)
            active_ref[:, cols] = active_b
            slope_ref[:, cols] = below + pre_active * jnp.exp(-0.5 * pre_active * pre_active) * gauss_factor
            total = total + dot_cols(active_b, weight_ref[2 + j])
    result_ref[...] = total.astype(bf16)


def units_backward_kernel(
    grad_ref, middle_ref, active_ref, slope_ref, own_ref, peer_ref, vec_ref,
    grad_middle_ref, grad_own_ref, grad_peer_ref, vec_grad_ref, up_bias_grad_ref,
):
    grad_b = grad_ref[...]
    grad_rows = grad_b.astype(f32)
    normed, rescale = norm_parts(middle_ref[...])
    normed_b = (normed * vec_ref[4:5] + vec_ref[5:6]).astype(bf16)
    normed_t = normed_b.T
    grad_t = grad_b.T
    grad_normed = None
    for half, weight_ref, out_ref in ((1, peer_ref, grad_peer_ref), (0, own_ref, grad_own_ref)):
        for j in range(2):
            cols = slice(768 * (2 * half + j), 768 * (2 * half + j) + 768)
            put_blocks(out_ref, 2 + j, 2 + j, dot(grad_t, active_ref[:, cols]))
            grad_upper = (dot(grad_b, weight_ref[2 + j]) * slope_ref[:, cols]).astype(bf16)
            up_bias_grad_ref[0:1, cols] = jnp.sum(grad_upper.astype(f32), 0, keepdims=True)
            put_blocks(out_ref, j, j, dot(normed_t, grad_upper))
            term = dot_cols(grad_upper, weight_ref[j])
            grad_normed = term if grad_normed is None else grad_normed + term
    grad_middle = grad_rows + norm_backward(grad_normed, normed, rescale, vec_ref[4:5])
    grad_middle_ref[...] = grad_middle
    vec_grad_ref[...] = jnp.zeros_like(vec_grad_ref)
    vec_grad_ref[0:1] = jnp.sum(grad_middle, 0, keepdims=True)
    vec_grad_ref[1:2] = jnp.sum(grad_rows, 0, keepdims=True)
    vec_grad_ref[4:5] = jnp.sum(grad_normed * normed, 0, keepdims=True)
    vec_grad_ref[5:6] = jnp.sum(grad_normed, 0, keepdims=True)


def attention_backward_kernel(
    grad_ref, x_ref, heads_ref, soft_ref, mixed_ref, own_ref, peer_ref, vec_ref,
    units_vec_ref, up_bias_grad_ref, place_ref,
    grad_in_ref, grad_own_ref, grad_peer_ref,
    grad_mixed_ref, grad_heads_ref, cols_ref, small_ref,
):
    grad_b = grad_ref[...].astype(bf16)
    grad_t = grad_b.T
    grad_mixed_ref[:, :384] = dot(grad_b, own_ref[:, 1152:1536]).astype(bf16)
    grad_mixed_ref[:, 384:] = dot(grad_b, peer_ref[:, 1152:1536]).astype(bf16)
    factor = HEAD ** (-0.5)
    for pair in range(6):
        found = ([], [], [])
        for head in (2 * pair, 2 * pair + 1):
            cols = slice(HEAD * head, HEAD * head + HEAD)
            soft = soft_ref[head]
            grad_head = grad_mixed_ref[:, cols]
            grad_soft = dot_cols(grad_head, heads_ref[2, :, cols])
            inner = jnp.sum(grad_soft * soft, -1, keepdims=True)
            grad_scores = (soft * (grad_soft - inner)).astype(bf16)
            found[0].append(dot(grad_scores, heads_ref[1, :, cols]) * factor)
            found[1].append(dot_rows(grad_scores, heads_ref[0, :, cols]) * factor)
            found[2].append(dot_rows(soft.astype(bf16), grad_head))
        for j in range(3):
            grad_heads_ref[j, :, 128 * pair : 128 * pair + 128] = jnp.concatenate(found[j], 1).astype(bf16)
    normed, rescale = norm_parts(x_ref[...].astype(f32))
    normed_b = (normed * vec_ref[2:3] + vec_ref[3:4]).astype(bf16)
    normed_t = normed_b.T
    grad_normed = None
    for half, weight_ref, out_ref in ((1, peer_ref, grad_peer_ref), (0, own_ref, grad_own_ref)):
        for j in range(3):
            rows = grad_heads_ref[j, :, 384 * half : 384 * half + 384]
            put_columns(out_ref, j, 384 * j, dot(normed_t, rows))
            term = dot_cols(rows, weight_ref[:, 384 * j : 384 * j + 384])
            grad_normed = term if grad_normed is None else grad_normed + term
    grad_in = grad_ref[...] + norm_backward(grad_normed, normed, rescale, vec_ref[2:3])
    grad_in_ref[...] = grad_in.astype(bf16)
    cols_ref[...] = jnp.zeros_like(cols_ref)
    cols_ref[0:2] = units_vec_ref[0:2]
    cols_ref[2:3] = jnp.sum(grad_normed * normed, 0, keepdims=True)
    cols_ref[3:4] = jnp.sum(grad_normed, 0, keepdims=True)
    cols_ref[4:6] = units_vec_ref[4:6]
    cols_ref[64:70] = cols_ref[0:6]
    cols = cols_ref[...].T
    query_bias = jnp.sum(grad_heads_ref[0].astype(f32), 0, keepdims=True)
    value_bias = jnp.sum(grad_heads_ref[2].astype(f32), 0, keepdims=True)
    for half, out_ref in ((1, grad_peer_ref), (0, grad_own_ref)):
        small_ref[...] = jnp.zeros_like(small_ref)
        for t in range(2):
            base = 64 * t
            for i in range(3):
                at = HEAD * (6 * half + 3 * t + i)
                small_ref[base + 8 + i : base + 9 + i] = query_bias[:, at : at + HEAD]
                small_ref[base + 11 + i : base + 12 + i] = value_bias[:, at : at + HEAD]
            for i in range(12):
                at = HEAD * (24 * half + 12 * t + i)
                small_ref[base + 14 + i : base + 15 + i] = up_bias_grad_ref[0:1, at : at + HEAD]
        small = dot_cols(place_ref[...], small_ref[...].astype(bf16)) + cols
        weight = dot(grad_t, mixed_ref[:, 384 * half : 384 * half + 384])
        put_columns(out_ref, 3, 1152, jnp.concatenate([weight, small], 1))


def kernel_call(kernel, name, inputs, outputs, scratch=(), scalar=False, blocks=None, large=True):
    whole = pl.BlockSpec(memory_space=pltpu.VMEM)
    specs = [whole] * len(inputs)
    out_specs = [whole] * len(outputs)
    if blocks is not None:
        specs = [pl.BlockSpec(shape, lambda i, at=at: at) for shape, at in blocks]
        out_specs = [pl.BlockSpec(shape, lambda i, n=len(shape): (0,) * n) for shape, _ in outputs]
    if scalar:
        specs[0] = pl.BlockSpec(memory_space=pltpu.SMEM)
    shapes = [jax.ShapeDtypeStruct(shape, dtype) for shape, dtype in outputs]
    return pl.pallas_call(
        kernel,
        name=name,
        out_shape=shapes,
        in_specs=specs,
        out_specs=out_specs,
        grid=() if blocks is None else (1,),
        scratch_shapes=list(scratch),
        cost_estimate=pl.CostEstimate(flops=1, bytes_accessed=1, transcendentals=0),
        compiler_params=pltpu.CompilerParams(vmem_limit_bytes=52 * 2**20 if large else None),
    )(*inputs)


ROWS = (192, 768)
HEADS_SHAPE = (3, 192, 768)
UNITS_SHAPE = (4, 16, 48, 768)
ATTN_SHAPE = (16, 48, 1664)


def attention_forward(length, x, attn, place_units):
    own, peer = attn
    return kernel_call(
        attention_forward_kernel, "attention_forward",
        [length, x, own, peer, place_units],
        [(ROWS, f32), (HEADS_SHAPE, bf16), ((12, 192, 192), f32), (ROWS, bf16), ((8, 768), f32), ((1, 3072), f32)],
        scalar=True,
    )


def units_forward(middle, units, vec, up_bias):
    own, peer = units
    return kernel_call(
        units_forward_kernel, "units_forward", [middle, own, peer, vec, up_bias],
        [(ROWS, bf16), ((192, 3072), bf16), ((192, 3072), f32)],
    )


def units_backward(grad_b, middle, active, slope, units, vec):
    own, peer = units
    return kernel_call(
        units_backward_kernel, "units_backward", [grad_b, middle, active, slope, own, peer, vec],
        [(ROWS, f32), (UNITS_SHAPE, bf16), (UNITS_SHAPE, bf16), ((8, 768), f32), ((1, 3072), f32)],
    )


def attention_backward(grad_middle, x, heads, soft, mixed, attn, vec, units_vec, up_bias_grad, place_units):
    own, peer = attn
    return kernel_call(
        attention_backward_kernel, "attention_backward",
        [grad_middle, x, heads, soft, mixed, own, peer, vec, units_vec, up_bias_grad, place_units],
        [(ROWS, bf16), (ATTN_SHAPE, bf16), (ATTN_SHAPE, bf16)],
        scratch=[pltpu.VMEM(ROWS, bf16), pltpu.VMEM(HEADS_SHAPE, bf16), pltpu.VMEM((128, 768), f32), pltpu.VMEM((128, 64), f32)],
    )


def exchange(value, bit):
    axis, size, flip = EXCHANGES[bit]
    return lax.ppermute(value, axis, [(i, i ^ flip) for i in range(size)])


def exchange_pipe(value):
    return lax.ppermute(value, "pipe", [(0, 1), (1, 0)])


def exchange_both(value):
    return lax.ppermute(value, ("pipe", "tensor"), [(i, i ^ 3) for i in range(4)])


def exchange_tensor(value):
    return lax.ppermute(value, "tensor", [(0, 1), (1, 0)])


def pin(*values):
    return lax.optimization_barrier(values)


def assemble_kernel(slots, *refs):
    count = len(slots)
    out = refs[-1]
    for number, (part, slot, start) in enumerate(slots):
        for index in range(16):
            rows = refs[number + (0 if index < 8 else count)][index % 8]
            place = slice(48 * block_place(part, index), 48 * block_place(part, index) + 48)
            cols = slice(start, start + rows.shape[1])
            if slot is None:
                out[place, cols] = rows
            else:
                out[slot, place, cols] = rows


def assemble(held, got, units):
    inputs, blocks, slots = [], [], []
    for part in range(4):
        width = (384, 256)[part // 3] if units else ATTN_COLS[part]
        first = ATTN_COLS[part] // width if units else 0
        for k in range(768 // width if units else 1):
            inputs.append(part)
            blocks.append(((8, 48, width), (0, 0, first + k)))
            slots.append((part, part, width * k) if units else (part, None, 384 * part))
    arrays = [held[part] for part in inputs] + [got[part] for part in inputs]
    shape = (4, 768, 768) if units else (768, 1664)
    kernel = functools.partial(assemble_kernel, slots)
    name = "assemble_units" if units else "assemble_attention"
    return kernel_call(kernel, name, arrays, [(shape, bf16)], blocks=blocks * 2)[0]


def pack_kernel(*refs):
    w_query, w_key, w_value, w_out, w_up, w_down, b_query, b_value = refs[:8]
    b_up = refs[9]
    vectors = [refs[8], *refs[10:15]]
    out_ref, vec_ref, small_ref = refs[15:]
    vec_ref[...] = jnp.zeros_like(vec_ref)
    for i, vector in enumerate(vectors):
        vec_ref[i : i + 1, 0:24] = vector[...].astype(f32)
    cols = vec_ref[...].T[0:24, 0:8]
    for half in range(2):
        small_ref[...] = jnp.zeros_like(small_ref)
        small_ref[:, 0:8] = cols
        small_ref[0:2, 8:11] = b_query[0, :, 3 * half : 3 * half + 3].astype(f32)
        small_ref[0:2, 11:14] = b_value[0, :, 3 * half : 3 * half + 3].astype(f32)
        small_ref[0:2, 14:26] = b_up[0, :, 12 * half : 12 * half + 12].astype(f32)
        small = small_ref[...].astype(bf16)
        wide, whole = slice(768 * half, 768 * half + 768), slice(192 * half, 192 * half + 192)
        first = jnp.concatenate([w_query[0, :, whole].astype(f32), w_key[0, :, whole].astype(f32)], 1).astype(bf16)
        second = jnp.concatenate([w_value[0, :, whole].astype(f32), w_out[0, :, whole].astype(f32)], 1).astype(bf16)
        for k in range(4):
            out = out_ref.at[2 * k + half]
            out[:, 0:768] = w_up[0, :, wide]
            out[:, 768:1536] = w_down[0, :, wide]
            out[:, 1536:1920] = first
            out[:, 1920:2304] = second
            out[:, 2304:2368] = small


def gather_start(params):
    tensor = lax.axis_index("tensor")
    rows = kernel_call(
        pack_kernel, "pack", list(params), [((8, 24, 2368), bf16)],
        scratch=[pltpu.VMEM((8, 128), f32), pltpu.VMEM((24, 64), f32)],
        blocks=[(param.shape, (0,) * param.ndim) for param in params], large=False,
    )[0]
    rows = lax.all_to_all(rows, ("pipe", "tensor", "core"), 0, 0, tiled=True)
    rows = rows.reshape(2, 2, 48, 2368)
    a = jnp.where(tensor == 0, rows[:, 0], rows[:, 1])
    b = jnp.where(tensor == 0, rows[:, 1], rows[:, 0])
    parts = [
        [a[..., 1536:1728], b[..., 1536:1728], a[..., :768]],
        [a[..., 1728:1920], b[..., 1728:1920], b[..., :768]],
        [a[..., 1920:2112], b[..., 1920:2112], a[..., 768:1536]],
        [a[..., 2112:2304], b[..., 2112:2304], a[..., 2304:], b[..., 2304:], b[..., 768:1536]],
    ]
    parts = [jnp.concatenate(part, -1)[:, None] for part in parts]
    for step in range(2):
        got = [exchange(part, ORDERS[i][step]) for i, part in enumerate(parts)]
        parts = [jnp.concatenate([x, y], 1) for x, y in zip(parts, got)]
    return parts, [exchange(part, ORDERS[i][2]) for i, part in enumerate(parts)]


def gather_layer(parts, got, layer):
    return [jnp.concatenate([x[layer], y[layer]], 0) for x, y in zip(parts, got)]


def gather_fourth(held):
    return [exchange(part, ORDERS[i][3]) for i, part in enumerate(held)]


def fold_kernel(fixed, outputs, *refs):
    terms, outs = refs[: len(fixed)], refs[len(fixed) :]
    for out, places in zip(outs, outputs):
        for sources, layer, start in places:
            total = None
            for term, index, first, width in sources:
                value = terms[term][(*index, *(0,) * fixed[term], slice(None), slice(None), slice(first, first + width))]
                total = value.astype(f32) if total is None else total + value.astype(f32)
            cols = slice(start, start + total.shape[-1])
            if layer is None:
                out[:, :, cols] = total.astype(bf16)
            else:
                out[layer, :, :, cols] = total.astype(bf16)


def fold(terms, outputs, layers, grid, name):
    arrays, specs, shapes, out_specs = [], [], [], []
    for array, bits in terms:
        lead, (n, rows, cols) = array.shape[:-3], array.shape[-3:]
        n >>= len(bits)
        arrays.append(array.reshape(*lead, *(2,) * len(bits), n, rows, cols))
        block = (*lead, *(1,) * len(bits), n // grid, rows, cols)
        specs.append(pl.BlockSpec(block, lambda b, at=(0,) * len(lead) + tuple(bits): (*at, b, 0, 0)))
    for places in outputs:
        width = max(start + sources[0][3] for sources, _, start in places)
        lead = () if layers is None else (layers,)
        shapes.append(jax.ShapeDtypeStruct((*lead, n, 48, width), bf16))
        out_specs.append(pl.BlockSpec((*lead, n // grid, 48, width), lambda b, at=(0,) * len(lead): (*at, b, 0, 0)))
    return pl.pallas_call(
        functools.partial(fold_kernel, [len(bits) for _, bits in terms], outputs),
        name=name,
        grid=(grid,),
        out_shape=shapes,
        in_specs=specs,
        out_specs=out_specs,
        cost_estimate=pl.CostEstimate(flops=1, bytes_accessed=1, transcendentals=0),
        compiler_params=pltpu.CompilerParams(vmem_limit_bytes=52 * 2**20),
    )(*arrays)


def send_parts(parts, step):
    return [exchange(part, ORDERS[i][step]) for i, part in enumerate(parts)]


def fold_attention(own, got):
    outputs = [[([(k, (), 384 * i, ATTN_COLS[i]) for k in range(2)], None, 0)] for i in range(4)]
    return fold([(own, (1,)), (got, (1,))], outputs, None, 2, "fold_attention")


def fold_units(own, got):
    outputs = [[([(k, (i,), 0, 768) for k in range(2)], None, 0)] for i in range(4)]
    return fold([(own, (1,)), (got, (1,))], outputs, None, 2, "fold_units")


def fold_both(groups, side):
    terms = []
    outputs = [[] for _ in range(4)]
    for number, (own, got, received) in enumerate(groups):
        base, units = len(terms), number % 2
        terms += [(own, (0, side)), (got, (0, side))] + [(part, (side,)) for part in received]
        for i in range(4):
            width = 768 if units else ATTN_COLS[i]
            index, first = ((i,), 0) if units else ((), 384 * i)
            sources = [(base, index, first, width), (base + 1, index, first, width), (base + 2 + i, (), 0, width)]
            outputs[i].append((sources, number // 2, ATTN_COLS[i] * units))
    return fold(terms, outputs, 2, 2, ("fold_both_kept", "fold_both_sent")[side])


def fold_on(kept, got, side, name):
    terms = [(part, (side,)) for pair in zip(kept, got) for part in pair]
    outputs = []
    for i in range(4):
        width = kept[i].shape[-1]
        outputs.append([([(2 * i + k, (layer,), 0, width) for k in range(2)], layer, 0) for layer in range(2)])
    return fold(terms, outputs, 2, 1, name + ("_kept", "_sent")[side])


def collect_kernel(tensor_ref, *refs):
    kept, got, out_ref = refs[:4], refs[4:8], refs[8]
    for layer in range(2):
        p = [x[layer, 0].astype(f32) + y[layer, 0].astype(f32) for x, y in zip(kept, got)]
        for t in range(2):
            at = slice(192 * t, 192 * t + 192)
            values = [
                (0, p[t][:, 384:]),
                (768, p[2][:, 384:] if t == 0 else p[3][:, 512:]),
                (1536, jnp.concatenate([p[0][:, at], p[1][:, at]], 1)),
                (1920, jnp.concatenate([p[2][:, at], p[3][:, at]], 1)),
                (2304, p[3][:, 384 + 64 * t : 448 + 64 * t]),
            ]
            place = 4 * layer + 2 * (t ^ tensor_ref[0])
            for core in range(2):
                out = out_ref.at[place + core]
                for start, value in values:
                    out[:, start : start + value.shape[1]] = value[24 * core : 24 * core + 24].astype(bf16)


def finish_kernel(rows_ref, *refs):
    g_query, g_key, g_value, g_out, g_up, g_down, gb_query, gb_value = refs[:8]
    gb_up = refs[9]
    vectors = [refs[8], *refs[10:15]]
    small_ref = refs[15]
    halves = []
    for core in range(2):
        total = rows_ref[core].astype(f32)
        for k in range(1, 4):
            total = total + rows_ref[2 * k + core].astype(f32)
        halves.append(total)
        g_up[0, :, 768 * core : 768 * core + 768] = total[:, 0:768]
        g_down[0, :, 768 * core : 768 * core + 768] = total[:, 768:1536]
    for i, out in enumerate((g_query, g_key, g_value, g_out)):
        start = 1536 + 192 * i
        out[0] = jnp.concatenate([half[:, start : start + 192] for half in halves], 1)
    for out, lo, hi in ((gb_query, 8, 11), (gb_value, 11, 14), (gb_up, 14, 26)):
        out[0] = jnp.concatenate([half[0:2, 2304 + lo : 2304 + hi] for half in halves], 1)
    small_ref[...] = jnp.zeros_like(small_ref)
    small_ref[0:24, 0:64] = halves[0][:, 2304:2368]
    cols = small_ref[...].T
    for i, out in enumerate(vectors):
        out[...] = cols[i : i + 1, 0:24]


def scatter_end(kept, got):
    tensor = lax.axis_index("tensor").astype(jnp.int32).reshape(1)
    rows = kernel_call(collect_kernel, "collect", [tensor, *kept, *got], [((8, 24, 2368), bf16)], scalar=True)[0]
    rows = lax.all_to_all(rows, ("pipe", "tensor", "core"), 0, 0, tiled=True)
    shapes = [(1, 24, 384)] * 4 + [(1, 24, 1536)] * 2 + [(1, 2, 6)] * 2 + [(1, 24), (1, 2, 24)] + [(1, 24)] * 5
    return kernel_call(
        finish_kernel, "finish", [rows], [(shape, f32) for shape in shapes], scratch=[pltpu.VMEM((128, 128), f32)]
    )


def share_outputs(first_rows, second_rows):
    pipe, tensor = lax.axis_index("pipe"), lax.axis_index("tensor")
    keep = jnp.where(pipe == 0, first_rows, second_rows)
    send = jnp.where(pipe == 0, second_rows, first_rows)
    return keep, exchange_tensor(keep), exchange_pipe(send), exchange_both(send)


def rows_apart(first_rows, second_rows):
    pipe = lax.axis_index("pipe")
    return jnp.where(pipe == 0, first_rows, second_rows), jnp.where(pipe == 0, second_rows, first_rows)


def order_outputs(rows):
    pipe, tensor = lax.axis_index("pipe"), lax.axis_index("tensor")
    a, b, c, d = rows
    a, b = jnp.where(tensor == 0, a, b), jnp.where(tensor == 0, b, a)
    c, d = jnp.where(tensor == 0, c, d), jnp.where(tensor == 0, d, c)
    a, c = jnp.where(pipe == 0, a, c), jnp.where(pipe == 0, c, a)
    b, d = jnp.where(pipe == 0, b, d), jnp.where(pipe == 0, d, b)
    return jnp.stack([a, b, c, d])[None]


def local(clip_frames, out_cotangent, clip_lengths, *params):
    micro = lax.axis_index("pipe") * 2 + lax.axis_index("tensor")
    chip = lax.axis_index("z") * 4 + lax.axis_index("x")

    parts, third = gather_start(params)
    held = [gather_layer(parts, third, layer) for layer in range(2)]
    got = [gather_fourth(held[0])]
    got[0], held[1] = pin(got[0], held[1])
    got.append(gather_fourth(held[1]))

    blocks = (chip ^ jnp.asarray(MASKS))[:, None]
    rows_at = (blocks * 48 + jnp.arange(48)[None]).reshape(-1)
    place_rows = (jnp.arange(768)[:, None] == rows_at[None]).astype(bf16)
    within = np.arange(48)
    units_at = np.where(within % 24 < 2, within // 24 * 2 + within % 24, 1000)
    units_at = (blocks * 4 + jnp.asarray(units_at)[None]).reshape(-1)
    place_units = (jnp.arange(64)[:, None] == units_at[None]).astype(bf16)
    place_back = (units_at[:, None] == jnp.arange(64)[None]).astype(bf16)

    frames = lax.dynamic_index_in_dim(clip_frames, micro, 0, keepdims=False)
    cotangent = lax.dynamic_index_in_dim(out_cotangent, micro, 0, keepdims=False)
    length = lax.dynamic_index_in_dim(clip_lengths, micro, 0, keepdims=False)
    x_first = dot(frames, place_rows).astype(bf16)
    grad_out = dot(cotangent, place_rows).astype(bf16)

    def placed_back(rows):
        return dot_cols(rows, place_rows).astype(bf16)

    attn_own = assemble(held[0], got[0], False)
    attn_own, got[0] = pin(attn_own, got[0])
    attn_peer = exchange(attn_own, "c")
    units_own = assemble(held[0], got[0], True)
    attn_peer, units_own = pin(attn_peer, units_own)
    attn_first = attn_own, attn_peer
    units_first = units_own, exchange(units_own, "c")
    middle_first, heads_first, soft_first, mixed_first, vec_first, up_bias_first = attention_forward(
        length, x_first, attn_first, place_units
    )
    x_second, active_first, slope_first = units_forward(middle_first, units_first, vec_first, up_bias_first)
    x_second, got[1] = pin(x_second, got[1])
    attn_own = assemble(held[1], got[1], False)
    attn_own, got[1] = pin(attn_own, got[1])
    attn_peer = exchange(attn_own, "c")
    units_own = assemble(held[1], got[1], True)
    attn_peer, units_own = pin(attn_peer, units_own)
    attn_second = attn_own, attn_peer
    units_second = units_own, exchange(units_own, "c")
    middle_second, heads_second, soft_second, mixed_second, vec_second, up_bias_second = attention_forward(
        length, x_second, attn_second, place_units
    )
    out_second, active_second, slope_second = units_forward(middle_second, units_second, vec_second, up_bias_second)
    shared = share_outputs(placed_back(x_second), placed_back(out_second))

    grad_middle, units_own_second, units_peer, units_vec, up_bias_grad = units_backward(
        grad_out, middle_second, active_second, slope_second, units_second, vec_second
    )
    units_got_second = exchange(units_peer, "c")
    attn = attention_backward(
        grad_middle, x_second, heads_second, soft_second, mixed_second, attn_second, vec_second, units_vec,
        up_bias_grad, place_back,
    )
    attn, units_got_second, shared = pin(attn, units_got_second, shared)
    section_output = order_outputs(shared)
    second_grad, attn_own_second, attn_peer = attn
    units_fourth_second = send_parts(fold_units(units_own_second, units_got_second), 3)
    attn_got_second = exchange(attn_peer, "c")

    units = units_backward(second_grad, middle_first, active_first, slope_first, units_first, vec_first)
    units, attn_got_second, units_fourth_second = pin(units, attn_got_second, units_fourth_second)
    grad_middle, units_own, units_peer, units_vec, up_bias_grad = units
    attn_fourth_second = send_parts(fold_attention(attn_own_second, attn_got_second), 3)
    units_got = exchange(units_peer, "c")

    attn = attention_backward(
        grad_middle, x_first, heads_first, soft_first, mixed_first, attn_first, vec_first, units_vec,
        up_bias_grad, place_back,
    )
    attn, units_got, attn_fourth_second = pin(attn, units_got, attn_fourth_second)
    first_grad, attn_own, attn_peer = attn
    attn_got = exchange(attn_peer, "c")
    attn_own, sent = pin(attn_own, fold_units(units_own, units_got))
    units_fourth = send_parts(sent, 3)
    sent, units_fourth = pin(fold_attention(attn_own, attn_got), units_fourth)
    attn_fourth = send_parts(sent, 3)
    keep, send = rows_apart(placed_back(first_grad), placed_back(second_grad))
    other_pipe = exchange_pipe(send)
    attn_fourth, other_pipe = pin(attn_fourth, other_pipe)
    across = exchange_tensor(jnp.stack([keep, other_pipe]))

    groups = (
        (attn_own, attn_got, attn_fourth), (units_own, units_got, units_fourth),
        (attn_own_second, attn_got_second, attn_fourth_second),
        (units_own_second, units_got_second, units_fourth_second),
    )
    kept, got = fold_both(groups, 0), send_parts(fold_both(groups, 1), 2)
    got, across = pin(got, across)
    input_grad = order_outputs((keep, across[0], other_pipe, across[1]))
    kept, got = fold_on(kept, got, 0, "fold_four"), send_parts(fold_on(kept, got, 1, "fold_four"), 1)
    kept, got = fold_on(kept, got, 0, "fold_two"), send_parts(fold_on(kept, got, 1, "fold_two"), 0)
    return (section_output, input_grad, *scatter_end(kept, got))


def solution(mesh):
    fine = Mesh(mesh.devices.reshape(2, 4, 4, 2, 2), ("pipe", "z", "x", "core", "tensor"))
    shard = ("z", "x", "core")
    rows = P(None, shard, None)
    matrix = P("pipe", shard, "tensor")
    vector = P("pipe", shard)
    params = (matrix,) * 8 + (vector, matrix) + (vector,) * 5
    return jax.shard_map(
        local,
        mesh=fine,
        in_specs=(rows, rows, P(None, shard)) + params,
        out_specs=(P("pipe", None, shard, None),) * 2 + params,
        check_vma=False,
    )
```
